256 devices in a mesh: ctx: 32 (over x_hi, z, core), head: 8 (over x_lo, y).
Axes of the slice: x: 4 (x_hi: 2, x_lo: 2; x = x_hi * 2 + x_lo), y: 4, z: 8, core: 2. Of those that a mesh axis runs over, the one named last changes fastest.
Arguments:
- queries_one: bfloat16 [4096, 4096], P('ctx', 'head'), may hold values from -6 to 6
- grads_one: bfloat16 [4096, 4096], P('ctx', 'head'), may hold values from -6 to 6
- queries_two: bfloat16 [4096, 4096], P('ctx', 'head'), may hold values from -6 to 6
- grads_two: bfloat16 [4096, 4096], P('ctx', 'head'), may hold values from -6 to 6
- key_rows: bfloat16 [4096, 1024], P('ctx', 'head'), may hold values from -6 to 6
- value_rows: bfloat16 [4096, 1024], P('ctx', 'head'), may hold values from -6 to 6
- shared_input: bfloat16 [4096, 8192], P('ctx'), may hold values from -6 to 6
- key_weight: bfloat16 [8192, 1024], P(None, 'head'), may hold values from -0.09375 to 0.09375
- value_weight: bfloat16 [8192, 1024], P(None, 'head'), may hold values from -0.0625 to 0.0625
- block_order: int32 [64], replicated, may hold values from 0 to 63, as said below
Outputs:
- query_grad_one: bfloat16 [4096, 4096], P('ctx', 'head')
- query_grad_two: bfloat16 [4096, 4096], P('ctx', 'head')
- input_grad: bfloat16 [4096, 8192], P('ctx', 'head')
- key_weight_grad: float32 [8192, 1024], P('ctx', 'head')
- value_weight_grad: float32 [8192, 1024], P('ctx', 'head')
The draws below stay inside these ranges and needn't reach their ends.
Inputs may be any that keep to these rules, and one draw needn't show every extreme that they name: `block_order`: each block 0 to 63 once; slots 2c and 2c + 1 hold blocks i and 63 - i for some i.
All inputs are finite; a program needn't handle non-finite values.
Results may differ from the reference program's by a relative error of at most 0.013.
Values may be sent and summed in bfloat16 or wider, within the bound.
No kernel may reach another device: no remote copies, remote signals or barrier semaphores. Data moves between devices by JAX's collectives and lax.ppermute only.
A program may use at most 128 MiB of HBM per device.

```python
import math
import jax
import jax.numpy as jnp
from jax import lax

D = 8192
H = 32
KV = 8
DH = 128
TOK_DEV = 128
SEQ = 4096
N_CTX = 32


def draw_key_rows(key, part):
    inner = jax.random.fold_in(key, 21)
    field = jnp.clip(jax.random.normal(inner, (SEQ, KV * DH), jnp.float32), -4.0, 4.0)
    return field.astype(jnp.bfloat16)


def place_queries(key, salt):
    inner = jax.random.fold_in(key, salt)
    field = jnp.clip(jax.random.normal(inner, (SEQ, H * DH), jnp.float32), -4.0, 4.0)
    return field


def draw_queries_one(key, part):
    return place_queries(key, 31).astype(jnp.bfloat16)


def draw_queries_two(key, part):
    return place_queries(key, 41).astype(jnp.bfloat16)


def draw_block_order(key, part):
    owner_key, flip_key = jax.random.split(jax.random.fold_in(key, 51))
    owners = jax.random.permutation(owner_key, N_CTX).astype(jnp.int32)
    flips = jax.random.randint(flip_key, (N_CTX,), 0, 2).astype(jnp.int32)
    lower = jnp.arange(N_CTX, dtype=jnp.int32)
    order = jnp.zeros((2 * N_CTX,), jnp.int32)
    order = order.at[2 * owners + flips].set(lower)
    order = order.at[2 * owners + 1 - flips].set(2 * N_CTX - 1 - lower)
    return order


def spiked(drawn, key, source, target, parts, factor):
    def block_of(axis_at):
        return (jnp.arange(drawn.shape[axis_at]) // (drawn.shape[axis_at] // parts)).reshape((-1,) + (1,) * (drawn.ndim - 1 - axis_at))

    near = jax.random.permutation(key, parts)[block_of(target)]
    far = (block_of(target) + parts // 2) % parts
    return jnp.where((block_of(source) == near) | (block_of(source) == far), factor * drawn, drawn)


def steps_of(rng, shape, cuts, low, largest):
    def one(position, blocks):
        draws = jax.random.uniform(jax.random.fold_in(jax.random.fold_in(rng, 6), position), (blocks,), jnp.float32, low / len(cuts), largest / len(cuts))
        return jnp.repeat(jnp.exp(draws), shape[position] // blocks).reshape((-1,) + (1,) * (len(shape) - position - 1))

    loudness = one(*cuts[0])
    for cut in cuts[1:]:
        loudness = loudness * one(*cut)
    return loudness


def centred(rng, shape, deviation, most, cuts=(), kind=jnp.bfloat16):
    result = deviation * jax.random.normal(rng, shape, jnp.float32)
    if cuts:
        result = result * steps_of(rng, shape, cuts, -0.22, 0.18)
    return jnp.clip(result, -most, most).astype(kind)


def gaussian_with(key, shape, scale, limit, shards, heavy, kind=jnp.bfloat16):
    entries = scale * jax.random.normal(key, shape, jnp.float32)
    if shards:
        entries = entries * steps_of(key, shape, shards, -0.22, 0.18)
    return jnp.clip(spiked(entries, jax.random.fold_in(key, 3), *heavy), -limit, limit).astype(kind)


def setup_inputs(seed: int = 0) -> dict:
    keys = jax.random.split(jax.random.key(seed), 11)
    return {
        "queries_one": draw_queries_one(jax.random.fold_in(keys[10], 71), 0),
        "grads_one": centred(keys[1], (SEQ, H * DH), 1.0, 6.0, ((0, 32), (1, 8))),
        "queries_two": draw_queries_two(jax.random.fold_in(keys[10], 71), 0),
        "grads_two": centred(keys[3], (SEQ, H * DH), 1.0, 6.0, ((0, 32), (1, 8))),
        "key_rows": draw_key_rows(jax.random.fold_in(keys[10], 71), 0),
        "value_rows": centred(keys[5], (SEQ, KV * DH), 1.0, 6.0, ((0, 32), (1, 8))),
        "shared_input": gaussian_with(keys[6], (SEQ, D), 1.0, 6.0, ((0, 32),), (0, 1, 32, 2.75)),
        "key_weight": gaussian_with(keys[7], (D, KV * DH), D ** -0.5, 0.09375, ((1, 8),), (1, 0, 8, 2.0)),
        "value_weight": centred(keys[8], (D, KV * DH), D ** -0.5, 0.0625, ((1, 8),)),
        "block_order": draw_block_order(jax.random.fold_in(keys[10], 71), 0),
    }


def head_backward(query, grad_out, key_head, value_head, positions):
    scale = 1.0 / math.sqrt(DH)
    scores = jnp.dot(query, key_head.T, preferred_element_type=jnp.float32) * scale
    allowed = positions[None, :] <= positions[:, None]
    scores = jnp.where(allowed, scores, -jnp.inf)
    peak = lax.optimization_barrier(jnp.max(scores, axis=1, keepdims=True))
    weights = jnp.exp(scores - peak)
    probabilities = weights / lax.optimization_barrier(jnp.sum(weights, axis=1, keepdims=True))
    prob_low = probabilities.astype(jnp.bfloat16)
    dprob = jnp.dot(grad_out, value_head.T, preferred_element_type=jnp.float32)
    row_delta = lax.optimization_barrier(jnp.sum(probabilities * dprob, axis=1, keepdims=True))
    dscore = (probabilities * (dprob - row_delta) * scale).astype(jnp.bfloat16)
    dquery = jnp.dot(dscore, key_head, preferred_element_type=jnp.float32).astype(jnp.bfloat16)
    dkey = jnp.dot(dscore.T, query, preferred_element_type=jnp.float32)
    dvalue = jnp.dot(prob_low.T, grad_out, preferred_element_type=jnp.float32)
    return (dquery, dkey, dvalue)

def layer_backward(queries, grads, key_heads, value_heads, positions):
    group = H // KV
    query_heads = queries.reshape(SEQ, H, DH).transpose(1, 0, 2)
    grad_heads = grads.reshape(SEQ, H, DH).transpose(1, 0, 2)

    def one_head(items):
        query, grad_out, head_index = items
        kv_index = head_index // group
        key_head = lax.dynamic_index_in_dim(key_heads, kv_index, 0, keepdims=False)
        value_head = lax.dynamic_index_in_dim(value_heads, kv_index, 0, keepdims=False)
        return head_backward(query, grad_out, key_head, value_head, positions)
    dquery, dkey, dvalue = lax.map(one_head, (query_heads, grad_heads, jnp.arange(H, dtype=jnp.int32)))
    dquery = dquery.transpose(1, 0, 2).reshape(SEQ, H * DH)
    dkey = dkey.reshape(KV, group, SEQ, DH).sum(axis=1).transpose(1, 0, 2).reshape(SEQ, KV * DH)
    dvalue = dvalue.reshape(KV, group, SEQ, DH).sum(axis=1).transpose(1, 0, 2).reshape(SEQ, KV * DH)
    return (dquery, dkey, dvalue)

def reference(queries_one, grads_one, queries_two, grads_two, key_rows, value_rows, shared_input, key_weight, value_weight, block_order):
    half_rows = TOK_DEV // 2
    positions = (block_order.astype(jnp.int32)[:, None] * half_rows + jnp.arange(half_rows, dtype=jnp.int32)[None, :]).reshape(SEQ)
    key_heads = key_rows.reshape(SEQ, KV, DH).transpose(1, 0, 2)
    value_heads = value_rows.reshape(SEQ, KV, DH).transpose(1, 0, 2)
    dq_one, dk_one, dv_one = layer_backward(queries_one, grads_one, key_heads, value_heads, positions)
    dq_two, dk_two, dv_two = layer_backward(queries_two, grads_two, key_heads, value_heads, positions)
    key_grad = (dk_one + dk_two).astype(jnp.bfloat16)
    value_grad = (dv_one + dv_two).astype(jnp.bfloat16)
    input_grad = jnp.dot(key_grad, key_weight.T, preferred_element_type=jnp.float32) + jnp.dot(value_grad, value_weight.T, preferred_element_type=jnp.float32)
    key_weight_grad = jnp.dot(shared_input.T, key_grad, preferred_element_type=jnp.float32)
    value_weight_grad = jnp.dot(shared_input.T, value_grad, preferred_element_type=jnp.float32)
    return (dq_one, dq_two, input_grad.astype(jnp.bfloat16), key_weight_grad, value_weight_grad)
```

```python
import functools
import math

import jax
import jax.numpy as jnp
from jax import lax
from jax.experimental import pallas as pl
from jax.experimental.pallas import tpu as pltpu
from jax.sharding import Mesh
from jax.sharding import PartitionSpec as P

H = 32
KV = 8
DH = 128
GROUP = H // KV
CTX = ("xh", "z", "core")
CHIPS = ("xh", "z")
HEAD = ("xl", "y")
NT = (((1,), (1,)), ((), ()))
TN = (((0,), (0,)), ((), ()))
f32 = jnp.float32
bf16 = jnp.bfloat16


def attention_kernel(
    order, where, q1, g1, q2, g2, own, other, dq1, dq2, keep, send,
    kpos, vpos, weight, dprob, dk, dv, q_all, g_all, *, tile_rows,
):
    half = q1.shape[0] // 2
    chips = own.shape[0]
    n_blocks = order.shape[0]
    rows = 2 * GROUP * half
    per = tile_rows // half
    scale = 1.0 / math.sqrt(DH)
    to_log2 = scale * math.log2(math.e)
    core = where[1]

    def block(j):
        return pl.ds(pl.multiple_of(j * half, half), half)

    def tile(t):
        return pl.ds(pl.multiple_of(t * tile_rows, tile_rows), tile_rows)

    def sort(m, _):
        for ref, at in ((own, core), (other, 1 - core)):
            for i in range(2):
                to = block(order[4 * m + 2 * at + i])
                kpos[to, :] = ref[m, i * half:(i + 1) * half, :DH]
                vpos[to, :] = ref[m, i * half:(i + 1) * half, DH:]
        return 0

    lax.fori_loop(0, chips, sort, 0, unroll=2)
    first = where[0]
    upper = jnp.where(order[first] > order[first + 1], 0, 1)

    def part(at, fresh):
        p = order[first + at]
        mine = block(at)
        for i, (q_ref, g_ref) in enumerate(((q1, g1), (q2, g2))):
            for h in range(GROUP):
                r = (i * GROUP + h) * half
                q_all[r:r + half, :] = q_ref[mine, h * DH:(h + 1) * DH]
                g_all[r:r + half, :] = g_ref[mine, h * DH:(h + 1) * DH]
        last = lax.div(p, per)
        q = q_all[...]
        g = g_all[...]

        def fold(x, op):
            return op(x.reshape(tile_rows // 8, 8, rows), axis=0)

        def score(t, peak, masked):
            s = lax.dot_general(kpos[tile(t), :], q, NT, preferred_element_type=f32)
            if masked:
                key = t * tile_rows + lax.broadcasted_iota(jnp.int32, s.shape, 0)
                row = p * half + lax.rem(lax.broadcasted_iota(jnp.int32, s.shape, 1), half)
                s = jnp.where(key <= row, s, -jnp.inf)
            weight[tile(t), :] = s
            return jnp.maximum(peak, fold(s, jnp.max))

        peak = jnp.full((8, rows), -jnp.inf, f32)
        peak = lax.fori_loop(0, last, lambda t, m: score(t, m, False), peak)
        peak = score(last, peak, True)
        peak = jnp.max(peak, axis=0, keepdims=True) * to_log2

        def weigh(t, carry):
            total, delta = carry
            e = jnp.exp2(weight[tile(t), :] * to_log2 - peak)
            d = lax.dot_general(vpos[tile(t), :], g, NT, preferred_element_type=f32)
            weight[tile(t), :] = e
            dprob[tile(t), :] = d
            return total + fold(e, jnp.sum), delta + fold(e * d, jnp.sum)

        zero = jnp.zeros((8, rows), f32)
        total, delta = lax.fori_loop(0, last + 1, weigh, (zero, zero))
        share = 1.0 / jnp.sum(total, axis=0, keepdims=True)
        delta = jnp.sum(delta, axis=0, keepdims=True) * share

        def grads(t, dq):
            prob = weight[tile(t), :] * share
            ds = (prob * (dprob[tile(t), :] - delta) * scale).astype(bf16)
            dv_tile = jnp.dot(prob.astype(bf16), g, preferred_element_type=f32)
            dk_tile = jnp.dot(ds, q, preferred_element_type=f32)
            if fresh:
                dv[tile(t), :] = dv_tile
                dk[tile(t), :] = dk_tile
            else:
                dv[tile(t), :] += dv_tile
                dk[tile(t), :] += dk_tile
            return dq + lax.dot_general(kpos[tile(t), :], ds, TN, preferred_element_type=f32)

        dq = lax.fori_loop(0, last + 1, grads, jnp.zeros((DH, rows), f32))
        if fresh:

            def clear(t, _):
                dv[tile(t), :] = jnp.zeros((tile_rows, DH), f32)
                dk[tile(t), :] = jnp.zeros((tile_rows, DH), f32)
                return 0

            lax.fori_loop(last + 1, n_blocks // per, clear, 0)
        dq = dq.T.astype(bf16)
        for i, out in enumerate((dq1, dq2)):
            for h in range(GROUP):
                r = (i * GROUP + h) * half
                out[mine, h * DH:(h + 1) * DH] = dq[r:r + half, :]

    part(upper, True)
    part(1 - upper, False)

    def unsort(m, _):
        for ref, at in ((keep, core), (send, 1 - core)):
            for i in range(2):
                of = block(order[4 * m + 2 * at + i])
                ref[m, i * half:(i + 1) * half, :DH] = dk[of, :].astype(bf16)
                ref[m, i * half:(i + 1) * half, DH:] = dv[of, :].astype(bf16)
        return 0

    lax.fori_loop(0, chips, unsort, 0, unroll=2)


def attention(order, where, q1, g1, q2, g2, own, other):
    chips, rows, width = own.shape
    seq = 2 * chips * rows
    every = GROUP * rows
    vmem = pl.BlockSpec(memory_space=pltpu.VMEM)
    smem = pl.BlockSpec(memory_space=pltpu.SMEM)
    return pl.pallas_call(
        functools.partial(attention_kernel, tile_rows=512),
        out_shape=(
            jax.ShapeDtypeStruct(q1.shape, bf16),
            jax.ShapeDtypeStruct(q2.shape, bf16),
            jax.ShapeDtypeStruct(own.shape, bf16),
            jax.ShapeDtypeStruct(own.shape, bf16),
        ),
        in_specs=[smem] * 2 + [vmem] * 6,
        out_specs=(vmem,) * 4,
        scratch_shapes=[
            pltpu.VMEM((seq, DH), bf16),
            pltpu.VMEM((seq, DH), bf16),
            pltpu.VMEM((seq, every), f32),
            pltpu.VMEM((seq, every), f32),
            pltpu.VMEM((seq, DH), f32),
            pltpu.VMEM((seq, DH), f32),
            pltpu.VMEM((every, DH), bf16),
            pltpu.VMEM((every, DH), bf16),
        ],
        compiler_params=pltpu.CompilerParams(vmem_limit_bytes=48 * 2**20),
        cost_estimate=pl.CostEstimate(
            flops=10 * seq * every * DH // 2, bytes_accessed=6 * 2**20, transcendentals=seq * every // 2
        ),
    )(order, where, q1, g1, q2, g2, own, other)


def input_terms_kernel(grad, key_weight, value_weight, out):
    terms = lax.dot_general(grad[:, :DH], key_weight[...], NT, preferred_element_type=f32)
    terms += lax.dot_general(grad[:, DH:], value_weight[...], NT, preferred_element_type=f32)
    out[0] = terms.astype(bf16)


def input_terms(grad, key_weight, value_weight, parts):
    rows = grad.shape[0]
    columns = key_weight.shape[0] // parts
    return pl.pallas_call(
        input_terms_kernel,
        grid=(parts,),
        out_shape=jax.ShapeDtypeStruct((parts, rows, columns), bf16),
        in_specs=[
            pl.BlockSpec(grad.shape, lambda j: (0, 0)),
            pl.BlockSpec((columns, DH), lambda j: (j, 0)),
            pl.BlockSpec((columns, DH), lambda j: (j, 0)),
        ],
        out_specs=pl.BlockSpec((1, rows, columns), lambda j: (j, 0, 0)),
        cost_estimate=pl.CostEstimate(
            flops=4 * rows * DH * key_weight.shape[0], bytes_accessed=6 * 2**20, transcendentals=0
        ),
    )(grad, key_weight, value_weight)


def swap(x, axis):
    return lax.ppermute(x, axis, [(0, 1), (1, 0)])


def to_all(x, axes, count):
    return lax.all_to_all(jnp.broadcast_to(x[None], (count,) + x.shape), axes, 0, 0)


def on_device(
    queries_one, grads_one, queries_two, grads_two, key_rows, value_rows,
    shared_input, key_weight, value_weight, block_order,
):
    rows, width = shared_input.shape
    n_xh, n_z, n_core, n_xl, n_y = (lax.axis_size(a) for a in CTX + HEAD)
    chips, heads = n_xh * n_z, n_xl * n_y
    core, xh = lax.axis_index("core"), lax.axis_index("xh")
    head = lax.axis_index(HEAD)
    where = jnp.stack([2 * lax.axis_index(CTX), core]).astype(jnp.int32)

    with jax.named_scope("gather_keys"):
        own = to_all(jnp.concatenate([key_rows, value_rows], axis=1), CHIPS, chips)
        other = swap(own, "core")

    with jax.named_scope("spread_input"):
        piece = width // (n_xh * n_z * 4)
        cut = shared_input.reshape(rows, n_xh, n_z, 4, piece)
        cut = lax.dynamic_slice(cut, (0, head // 4, 0, head % 4, 0), (rows, 1, n_z, 1, piece))
        cut = cut.reshape(rows, n_z, piece).transpose(1, 0, 2)
        cut = lax.all_to_all(cut, "z", 0, 0)
        cut = to_all(cut.reshape(n_z * rows, piece), HEAD, heads)

    with jax.named_scope("attention"):
        dq_one, dq_two, keep, send = attention(
            block_order, where, queries_one, grads_one, queries_two, grads_two, own, other
        )
    with jax.named_scope("scatter_grads"):
        both = (keep.astype(f32) + swap(send, "core").astype(f32)).astype(bf16)
        both = lax.all_to_all(both, CHIPS, 0, 0)
        grad = jnp.sum(both.astype(f32), axis=0).astype(bf16)

    with jax.named_scope("input_grad"):
        terms = lax.all_to_all(input_terms(grad, key_weight, value_weight, heads), HEAD, 0, 0)
        input_grad = jnp.sum(terms.astype(f32), axis=0).astype(bf16)

    with jax.named_scope("weight_grad"):
        ring = to_all(grad, "z", n_z).reshape(n_z * rows, 2 * DH)
        terms = jnp.einsum("hrc,rn->hcn", cut, ring, preferred_element_type=f32)
        terms = terms.reshape(n_xh, n_core, 2 * piece, 2 * DH)
        kept = lax.dynamic_index_in_dim(terms, core, 1, keepdims=False)
        sent = lax.dynamic_index_in_dim(terms, 1 - core, 1, keepdims=False).astype(bf16)
        terms = kept + swap(sent, "core").astype(f32)
        kept = lax.dynamic_index_in_dim(terms, xh, 0, keepdims=False)
        sent = lax.dynamic_index_in_dim(terms, 1 - xh, 0, keepdims=False).astype(bf16)
        weight_grad = kept + swap(sent, "xh").astype(f32)
    return (dq_one, dq_two, input_grad, weight_grad[:, :DH], weight_grad[:, DH:])


def solution(mesh):
    fine = Mesh(mesh.devices.reshape(2, 8, 2, 2, 4), CTX + HEAD)
    both = P(CTX, HEAD)
    return jax.shard_map(
        on_device,
        mesh=fine,
        in_specs=(both,) * 6 + (P(CTX, None), P(None, HEAD), P(None, HEAD), P()),
        out_specs=(both,) * 5,
        check_vma=False,
    )
```

```python
import functools
import math

import jax
import jax.numpy as jnp
from jax import lax
from jax.experimental import pallas as pl
from jax.experimental.pallas import tpu as pltpu
from jax.sharding import Mesh
from jax.sharding import PartitionSpec as P

H = 32
KV = 8
DH = 128
GROUP = H // KV
CTX = ("xh", "z", "core")
HEAD = ("xl", "y")
NT = (((1,), (1,)), ((), ()))
TN = (((0,), (0,)), ((), ()))
f32 = jnp.float32
bf16 = jnp.bfloat16
SCALE = 1.0 / math.sqrt(DH)
TO_LOG2 = SCALE * math.log2(math.e)
LOWEST = -1e30
VMEM = pl.BlockSpec(memory_space=pltpu.VMEM)
SMEM = pl.BlockSpec(memory_space=pltpu.SMEM)


class Plan:
    def __init__(self, order, where, n_keys, half):
        self.half = half
        self.n_keys = n_keys
        self.order, self.where = order, where
        self.near = []
        for b in range(n_keys):
            slot = where[4 + b]
            self.near.append(jnp.minimum(order[slot], order[slot + 1]))
        self.rank = []
        for b in range(n_keys):
            r = jnp.int32(0)
            for o in range(n_keys):
                r += jnp.where(self.near[o] < self.near[b], 1, 0)
            self.rank.append(r)

    def key_rows(self, b, i):
        pos = self.order[self.where[4 + b] + i]
        r = self.rank[b]
        at = jnp.where(pos == self.near[b], r, 2 * self.n_keys - 1 - r)
        return pl.ds(pl.multiple_of(at * self.half, self.half), self.half)

    def limits(self, a, width):
        slot = self.where[a]
        first, second = self.order[slot], self.order[slot + 1]
        mine = jnp.minimum(first, second)
        below, upto = jnp.int32(0), jnp.int32(0)
        for near in self.near:
            below += jnp.where(near < mine, 1, 0)
            upto += jnp.where(near <= mine, 1, 0)
        early, late = upto, 2 * self.n_keys - below
        inside = lax.rem(lax.broadcasted_iota(jnp.int32, (1, width), 1), self.half)
        same = upto > below

        def last(blocks):
            return jnp.where(same, (blocks - 1) * self.half + inside, blocks * self.half - 1)

        return early, late, last(early), last(late)


def load_heads(refs, q_all, g_all, order, where, half):
    for a, (ref, lead) in enumerate(refs):
        slot = where[a]
        late_at = jnp.where(order[slot] > order[slot + 1], 0, 1)
        for part, at in ((0, late_at), (1, 1 - late_at)):
            rows = pl.ds(pl.multiple_of(at * half, half), half)
            for layer in range(2):
                for h in range(GROUP):
                    r = (layer * GROUP + h) * half
                    c = (layer * 2 * GROUP + h) * DH
                    q_all[a, part, r:r + half, :] = ref[lead + (rows, slice(c, c + DH))]
                    c += GROUP * DH
                    g_all[a, part, r:r + half, :] = ref[lead + (rows, slice(c, c + DH))]


def sort_keys(plan, kv, k_sorted, v_sorted):
    for b in range(plan.n_keys):
        for i in range(2):
            to = plan.key_rows(b, i)
            rows = slice(i * plan.half, (i + 1) * plan.half)
            k_sorted[to, :] = kv[b, rows, :DH]
            v_sorted[to, :] = kv[b, rows, DH:]


def fold(x, op):
    return op(x.reshape(x.shape[0] // 8, 8, x.shape[1]), axis=0)


def tiles(seen, n_keys, half, part):
    step = n_keys * half // 2
    if part == 0:
        return (
            (0, 2 * step, None, False),
            (2 * step, step, seen > n_keys, True),
            (3 * step, step, seen > n_keys + n_keys // 2, True),
        )
    return ((0, step, seen > 0, True), (step, step, seen > n_keys // 2, True))


def under(condition, body):
    if condition is None:
        body()
    else:
        pl.when(condition)(body)


def masked_scores(k, q, start, last, masked):
    s = lax.dot_general(k, q, NT, preferred_element_type=f32)
    if masked:
        key = start + lax.broadcasted_iota(jnp.int32, s.shape, 0)
        s = jnp.where(key <= last, s, -jnp.inf)
    return s


def stats_kernel(
    order, where, own, far, side, kv, stats, k_sorted, v_sorted, q_all, g_all, scores, peak, total, delta
):
    half = own.shape[0] // 2
    n_keys = kv.shape[0]
    width = q_all.shape[2]
    plan = Plan(order, where, n_keys, half)
    sort_keys(plan, kv, k_sorted, v_sorted)
    load_heads(
        ((own, ()), (far, ()), (side, (0,)), (side, (1,))), q_all, g_all, order, where, half
    )
    for a in range(4):
        early, late, last_early, last_late = plan.limits(a, width)
        for part, seen, last in ((0, late, last_late), (1, early, last_early)):
            q, g = q_all[a, part], g_all[a, part]
            peak[...] = jnp.full(peak.shape, LOWEST, f32)
            for start, size, condition, masked in tiles(seen, n_keys, half, part):

                def score():
                    s = masked_scores(k_sorted[start:start + size, :], q, start, last, masked)
                    scores[start:start + size, :] = s
                    peak[...] = jnp.maximum(peak[...], fold(s, jnp.max))

                under(condition, score)
            top = jnp.max(peak[...], axis=0, keepdims=True) * TO_LOG2
            total[...] = jnp.zeros(total.shape, f32)
            delta[...] = jnp.zeros(delta.shape, f32)
            for start, size, condition, masked in tiles(seen, n_keys, half, part):

                def weigh():
                    e = jnp.exp2(scores[start:start + size, :] * TO_LOG2 - top)
                    d = lax.dot_general(
                        v_sorted[start:start + size, :], g, NT, preferred_element_type=f32
                    )
                    total[...] += fold(e, jnp.sum)
                    delta[...] += fold(e * d, jnp.sum)

                under(condition, weigh)
            row = 2 * a + part
            stats[0, row:row + 1, :] = top
            stats[1, row:row + 1, :] = jnp.sum(total[...], axis=0, keepdims=True)
            stats[2, row:row + 1, :] = jnp.sum(delta[...], axis=0, keepdims=True)


def grads_kernel(
    order, where, own, far, side, kv, s_own, s_far, s_side, s_both, dq_own, dq_far, dq_side, dq_both, dkv,
    k_sorted, v_sorted, q_all, g_all, dk, dv, dq,
):
    half = own.shape[0] // 2
    n_keys = kv.shape[0]
    width = q_all.shape[2]
    plan = Plan(order, where, n_keys, half)
    sort_keys(plan, kv, k_sorted, v_sorted)
    load_heads(
        ((own, ()), (far, ()), (side, (0,)), (side, (1,))), q_all, g_all, order, where, half
    )
    dk[...] = jnp.zeros(dk.shape, f32)
    dv[...] = jnp.zeros(dv.shape, f32)
    for a, dq_out in enumerate((dq_own, dq_far, dq_side, dq_both)):
        early, late, last_early, last_late = plan.limits(a, width)
        slot = where[a]
        late_at = jnp.where(order[slot] > order[slot + 1], 0, 1)
        for part, seen, last, at in ((0, late, last_late, late_at), (1, early, last_early, 1 - late_at)):
            q, g = q_all[a, part], g_all[a, part]
            held = []
            for flip, ref in ((0, s_own), (1, s_far), (2, s_side), (3, s_both)):
                r = 2 * (a ^ flip) + part
                held.append(tuple(ref[j, r:r + 1, :] for j in range(3)))
            top = functools.reduce(jnp.maximum, (t for t, _, _ in held))
            total = sum(n * jnp.exp2(t - top) for t, n, _ in held)
            delta = sum(d * jnp.exp2(t - top) for t, _, d in held) / total
            base = top + jnp.log2(total)
            dq[...] = jnp.zeros(dq.shape, f32)
            for start, size, condition, masked in tiles(seen, n_keys, half, part):

                def grads():
                    span = slice(start, start + size)
                    k = k_sorted[span, :]
                    s = masked_scores(k, q, start, last, masked)
                    p = jnp.exp2(s * TO_LOG2 - base)
                    d = lax.dot_general(v_sorted[span, :], g, NT, preferred_element_type=f32)
                    ds = (p * (d - delta)).astype(bf16)
                    dv[span, :] += jnp.dot(p.astype(bf16), g, preferred_element_type=f32)
                    dk[span, :] += jnp.dot(ds, q, preferred_element_type=f32)
                    dq[...] += lax.dot_general(k, ds, TN, preferred_element_type=f32)

                under(condition, grads)
            turned = (dq[...] * SCALE).T.astype(dq_out.dtype)
            rows = pl.ds(pl.multiple_of(at * half, half), half)
            for j in range(2 * GROUP):
                dq_out[rows, j * DH:(j + 1) * DH] = turned[j * half:(j + 1) * half, :]
    for b in range(n_keys):
        for i in range(2):
            of = plan.key_rows(b, i)
            rows = slice(i * half, (i + 1) * half)
            dkv[b, rows, :DH] = (dk[of, :] * SCALE).astype(bf16)
            dkv[b, rows, DH:] = dv[of, :].astype(bf16)


def scratch(n_keys, rows):
    width = GROUP * rows
    return [
        pltpu.VMEM((n_keys * rows, DH), bf16),
        pltpu.VMEM((n_keys * rows, DH), bf16),
        pltpu.VMEM((4, 2, width, DH), bf16),
        pltpu.VMEM((4, 2, width, DH), bf16),
    ]


def cost(n_keys, rows, products):
    pairs = 4 * GROUP * rows * n_keys * rows
    return pl.CostEstimate(
        flops=2 * products * pairs * DH, bytes_accessed=8 * 2**20, transcendentals=pairs
    )


def attention_stats(order, where, own, far, side, kv):
    n_keys, rows, _ = kv.shape
    width = GROUP * rows
    return pl.pallas_call(
        stats_kernel,
        out_shape=jax.ShapeDtypeStruct((3, 8, width), f32),
        in_specs=[SMEM] * 2 + [VMEM] * 4,
        out_specs=VMEM,
        scratch_shapes=scratch(n_keys, rows)
        + [pltpu.VMEM((n_keys * rows, width), f32)]
        + [pltpu.VMEM((8, width), f32)] * 3,
        compiler_params=pltpu.CompilerParams(vmem_limit_bytes=24 * 2**20),
        cost_estimate=cost(n_keys, rows, 2),
    )(order, where, own, far, side, kv)


def attention_grads(order, where, own, far, side, kv, stats):
    n_keys, rows, _ = kv.shape
    width = GROUP * rows
    shape = (rows, 2 * GROUP * DH)
    return pl.pallas_call(
        grads_kernel,
        out_shape=(
            jax.ShapeDtypeStruct(shape, f32),
            jax.ShapeDtypeStruct(shape, bf16),
            jax.ShapeDtypeStruct(shape, bf16),
            jax.ShapeDtypeStruct(shape, bf16),
            jax.ShapeDtypeStruct(kv.shape, bf16),
        ),
        in_specs=[SMEM] * 2 + [VMEM] * 8,
        out_specs=(VMEM,) * 5,
        scratch_shapes=scratch(n_keys, rows)
        + [pltpu.VMEM((n_keys * rows, DH), f32)] * 2
        + [pltpu.VMEM((DH, width), f32)],
        compiler_params=pltpu.CompilerParams(vmem_limit_bytes=24 * 2**20),
        cost_estimate=cost(n_keys, rows, 5),
    )(order, where, own, far, side, kv, *stats)


def cut_kernel(at, x, out):
    out[0] = x[...]


def cut_input(x, at, count, stride, width):
    rows = x.shape[0]
    return pl.pallas_call(
        cut_kernel,
        grid_spec=pltpu.PrefetchScalarGridSpec(
            num_scalar_prefetch=1,
            grid=(count,),
            in_specs=[pl.BlockSpec((rows, width), lambda j, at: (0, at[0] + j * stride))],
            out_specs=pl.BlockSpec((1, rows, width), lambda j, at: (j, 0, 0)),
        ),
        out_shape=jax.ShapeDtypeStruct((count, rows, width), x.dtype),
    )(at, x)


def input_terms_kernel(grad, key_weight, value_weight, out):
    terms = lax.dot_general(grad[:, :DH], key_weight[...], NT, preferred_element_type=f32)
    terms += lax.dot_general(grad[:, DH:], value_weight[...], NT, preferred_element_type=f32)
    out[0] = terms.astype(bf16)


def input_terms(grad, key_weight, value_weight, parts):
    rows = grad.shape[0]
    columns = key_weight.shape[0] // parts
    return pl.pallas_call(
        input_terms_kernel,
        grid=(parts,),
        out_shape=jax.ShapeDtypeStruct((parts, rows, columns), bf16),
        in_specs=[
            pl.BlockSpec(grad.shape, lambda j: (0, 0)),
            pl.BlockSpec((columns, DH), lambda j: (j, 0)),
            pl.BlockSpec((columns, DH), lambda j: (j, 0)),
        ],
        out_specs=pl.BlockSpec((1, rows, columns), lambda j: (j, 0, 0)),
        cost_estimate=pl.CostEstimate(
            flops=4 * rows * DH * key_weight.shape[0], bytes_accessed=6 * 2**20, transcendentals=0
        ),
    )(grad, key_weight, value_weight)


def swap(x, axis):
    return lax.ppermute(x, axis, [(0, 1), (1, 0)])


def cross(x):
    return lax.ppermute(x, ("xh", "core"), [(0, 3), (1, 2), (2, 1), (3, 0)])


def to_all(x, axes, count):
    return lax.all_to_all(jnp.broadcast_to(x[None], (count,) + x.shape), axes, 0, 0)


def on_device(
    queries_one, grads_one, queries_two, grads_two, key_rows, value_rows,
    shared_input, key_weight, value_weight, block_order,
):
    rows, width = shared_input.shape
    n_xh, n_z, n_core, n_xl, n_y = (lax.axis_size(a) for a in CTX + HEAD)
    heads = n_xl * n_y
    core, xh, z = lax.axis_index("core"), lax.axis_index("xh"), lax.axis_index("z")
    head = lax.axis_index(HEAD)

    def slot(h, at, c):
        return 2 * ((h * n_z + at) * n_core + c)

    where = jnp.stack(
        [slot(xh, z, core), slot(1 - xh, z, core), slot(xh, z, 1 - core), slot(1 - xh, z, 1 - core)]
        + [slot(xh, b, core) for b in range(n_z)]
    ).astype(jnp.int32)

    with jax.named_scope("gather_keys"):
        kv = to_all(jnp.concatenate([key_rows, value_rows], axis=1), "z", n_z)
    with jax.named_scope("gather_queries"):
        own = jnp.concatenate([queries_one, grads_one, queries_two, grads_two], axis=1)
        far = swap(own, "xh")
        side = swap(jnp.stack([own, far]), "core")

    with jax.named_scope("cut_input"):
        piece = DH
        per = width // (n_xh * n_z * piece)
        at = (lax.div(head, per) * (n_z * per) + lax.rem(head, per)).astype(jnp.int32)
        cut = cut_input(shared_input, at.reshape(1), n_z, per, piece)

    with jax.named_scope("attention_stats"):
        stats = attention_stats(block_order, where, own, far, side, kv)
    with jax.named_scope("share_stats"):
        stats = (stats, swap(stats, "xh"), swap(stats, "core"), cross(stats))
    with jax.named_scope("spread_input"):
        cut = lax.all_to_all(cut, "z", 0, 0)
    with jax.named_scope("attention_grads"):
        stats, cut = lax.optimization_barrier((stats, cut))
        dq_own, dq_far, dq_side, dq_both, dkv = attention_grads(
            block_order, where, own, far, side, kv, stats
        )
    with jax.named_scope("spread_input"):
        cut = lax.all_gather(cut.reshape(n_z * rows, piece), HEAD)

    with jax.named_scope("scatter_grads"):
        dkv = lax.all_to_all(dkv, "z", 0, 0)
        grad = jnp.sum(dkv.astype(f32), axis=0).astype(bf16)
    with jax.named_scope("query_grads"):
        dq = dq_own + swap(dq_far, "xh").astype(f32)
        dq = (dq + swap(dq_side, "core").astype(f32) + cross(dq_both).astype(f32)).astype(bf16)
        dq_one, dq_two = dq[:, :GROUP * DH], dq[:, GROUP * DH:]

    with jax.named_scope("input_grad"):
        terms = lax.all_to_all(input_terms(grad, key_weight, value_weight, heads), HEAD, 0, 0)
        input_grad = jnp.sum(terms.astype(f32), axis=0).astype(bf16)

    with jax.named_scope("weight_grad"):
        ring = to_all(grad, "z", n_z).reshape(n_z * rows, 2 * DH)
        terms = jnp.einsum("hrc,rn->hcn", cut, ring, preferred_element_type=f32)
        terms = terms.reshape(n_xh, n_core, 2 * piece, 2 * DH)
        kept = lax.dynamic_index_in_dim(terms, core, 1, keepdims=False)
        sent = lax.dynamic_index_in_dim(terms, 1 - core, 1, keepdims=False).astype(bf16)
        terms = kept + swap(sent, "core").astype(f32)
        kept = lax.dynamic_index_in_dim(terms, xh, 0, keepdims=False)
        sent = lax.dynamic_index_in_dim(terms, 1 - xh, 0, keepdims=False).astype(bf16)
        weight_grad = kept + swap(sent, "xh").astype(f32)
    return (dq_one, dq_two, input_grad, weight_grad[:, :DH], weight_grad[:, DH:])


def solution(mesh):
    fine = Mesh(mesh.devices.reshape(2, 8, 2, 2, 4), CTX + HEAD)
    both = P(CTX, HEAD)
    return jax.shard_map(
        on_device,
        mesh=fine,
        in_specs=(both,) * 6 + (P(CTX, None), P(None, HEAD), P(None, HEAD), P()),
        out_specs=(both,) * 5,
        check_vma=False,
    )
```

```python
import functools
import math

import jax
import jax.numpy as jnp
from jax import lax
from jax.experimental import pallas as pl
from jax.experimental.pallas import tpu as pltpu
from jax.sharding import Mesh
from jax.sharding import PartitionSpec as P

H = 32
KV = 8
DH = 128
GROUP = H // KV
CTX = ("xh", "z", "core")
HEAD = ("xl", "y")
NT = (((1,), (1,)), ((), ()))
TN = (((0,), (0,)), ((), ()))
f32 = jnp.float32
bf16 = jnp.bfloat16
SCALE = 1.0 / math.sqrt(DH)
TO_LOG2 = SCALE * math.log2(math.e)
LOWEST = -1e30
BIG = 59 * 2**20
SMALL = 8 * 2**20
VMEM = pl.BlockSpec(memory_space=pltpu.VMEM)
SMEM = pl.BlockSpec(memory_space=pltpu.SMEM)
ANY = pl.BlockSpec(memory_space=pl.ANY)


class Plan:
    def __init__(self, order, where, n_keys, half):
        self.half = half
        self.n_keys = n_keys
        self.order, self.where = order, where
        self.near = []
        for b in range(n_keys):
            slot = where[4 + b]
            self.near.append(jnp.minimum(order[slot], order[slot + 1]))
        self.rank = []
        for b in range(n_keys):
            r = jnp.int32(0)
            for o in range(n_keys):
                r += jnp.where(self.near[o] < self.near[b], 1, 0)
            self.rank.append(r)

    def key_rows(self, b, i):
        pos = self.order[self.where[4 + b] + i]
        r = self.rank[b]
        at = jnp.where(pos == self.near[b], r, 2 * self.n_keys - 1 - r)
        return pl.ds(pl.multiple_of(at * self.half, self.half), self.half)

    def limits(self, a, width):
        slot = self.where[a]
        first, second = self.order[slot], self.order[slot + 1]
        mine = jnp.minimum(first, second)
        below, upto = jnp.int32(0), jnp.int32(0)
        for near in self.near:
            below += jnp.where(near < mine, 1, 0)
            upto += jnp.where(near <= mine, 1, 0)
        early, late = upto, 2 * self.n_keys - below
        inside = lax.rem(lax.broadcasted_iota(jnp.int32, (1, width), 1), self.half)
        same = upto > below

        def last(blocks):
            return jnp.where(same, (blocks - 1) * self.half + inside, blocks * self.half - 1)

        return early, late, last(early), last(late)


def load_heads(a, ref, q_all, g_all, order, where, half):
    slot = where[a]
    late_at = jnp.where(order[slot] > order[slot + 1], 0, 1)
    for part, at in ((0, late_at), (1, 1 - late_at)):
        rows = pl.ds(pl.multiple_of(at * half, half), half)
        for layer in range(2):
            for h in range(GROUP):
                r = (layer * GROUP + h) * half
                c = (layer * 2 * GROUP + h) * DH
                q_all[part, r:r + half, :] = ref[rows, c:c + DH]
                c += GROUP * DH
                g_all[part, r:r + half, :] = ref[rows, c:c + DH]


def fetch(pairs, sems):
    copies = [pltpu.make_async_copy(src, dst, sems.at[i]) for i, (src, dst) in enumerate(pairs)]
    for copy in copies:
        copy.start()
    return copies


def sort_keys(plan, kv, k_sorted, v_sorted):
    for b in range(plan.n_keys):
        for i in range(2):
            to = plan.key_rows(b, i)
            rows = slice(i * plan.half, (i + 1) * plan.half)
            k_sorted[to, :] = kv[b, rows, :DH]
            v_sorted[to, :] = kv[b, rows, DH:]


def fold(x, op):
    return op(x.reshape(x.shape[0] // 8, 8, x.shape[1]), axis=0)


def tiles(seen, n_keys, half, part):
    step = n_keys * half // 2
    if part == 0:
        return (
            (0, 2 * step, None, False),
            (2 * step, step, seen > n_keys, True),
            (3 * step, step, seen > n_keys + n_keys // 2, True),
        )
    return ((0, step, seen > 0, True), (step, step, seen > n_keys // 2, True))


def under(condition, body):
    if condition is None:
        body()
    else:
        pl.when(condition)(body)


def masked_scores(k, q, start, last, masked):
    s = lax.dot_general(k, q, NT, preferred_element_type=f32)
    if masked:
        key = start + lax.broadcasted_iota(jnp.int32, s.shape, 0)
        s = jnp.where(key <= last, s, -jnp.inf)
    return s


def stats_kernel(
    order, where, own, far, side, both, kv, stats, held, kv_held, k_sorted, v_sorted, q_all, g_all, sems,
    scores, peak, total, delta,
):
    half = own.shape[0] // 2
    n_keys = kv.shape[0]
    width = q_all.shape[1]
    copies = fetch(
        [(kv, kv_held)] + [(ref, held.at[a]) for a, ref in enumerate((own, far, side, both))], sems
    )
    plan = Plan(order, where, n_keys, half)
    copies[0].wait()
    sort_keys(plan, kv_held, k_sorted, v_sorted)
    for a in range(4):
        copies[1 + a].wait()
        load_heads(a, held.at[a], q_all, g_all, order, where, half)
        early, late, last_early, last_late = plan.limits(a, width)
        for part, seen, last in ((0, late, last_late), (1, early, last_early)):
            q, g = q_all[part], g_all[part]
            peak[...] = jnp.full(peak.shape, LOWEST, f32)
            for start, size, condition, masked in tiles(seen, n_keys, half, part):

                def score():
                    s = masked_scores(k_sorted[start:start + size, :], q, start, last, masked)
                    scores[start:start + size, :] = s
                    peak[...] = jnp.maximum(peak[...], fold(s, jnp.max))

                under(condition, score)
            top = jnp.max(peak[...], axis=0, keepdims=True) * TO_LOG2
            total[...] = jnp.zeros(total.shape, f32)
            delta[...] = jnp.zeros(delta.shape, f32)
            for start, size, condition, masked in tiles(seen, n_keys, half, part):

                def weigh():
                    e = jnp.exp2(scores[start:start + size, :] * TO_LOG2 - top)
                    d = lax.dot_general(
                        v_sorted[start:start + size, :], g, NT, preferred_element_type=f32
                    )
                    total[...] += fold(e, jnp.sum)
                    delta[...] += fold(e * d, jnp.sum)

                under(condition, weigh)
            row = 2 * a + part
            stats[0, row:row + 1, :] = top
            stats[1, row:row + 1, :] = jnp.sum(total[...], axis=0, keepdims=True)
            stats[2, row:row + 1, :] = jnp.sum(delta[...], axis=0, keepdims=True)


def grads_kernel(
    order, where, own, far, side, both, kv, s_own, s_far, s_side, s_both, dq_own, dq_far, dq_side, dq_both, dkv,
    held, kv_held, k_sorted, v_sorted, q_all, g_all, sems, s_held, out_own, out_rest, out_kv, out_sems, dk, dv, dq,
):
    half = own.shape[0] // 2
    n_keys = kv.shape[0]
    width = q_all.shape[1]
    copies = fetch(
        [(kv, kv_held)]
        + [(ref, held.at[a]) for a, ref in enumerate((own, far, side, both))]
        + [(ref, s_held.at[a]) for a, ref in enumerate((s_own, s_far, s_side, s_both))],
        sems,
    )
    plan = Plan(order, where, n_keys, half)
    copies[0].wait()
    sort_keys(plan, kv_held, k_sorted, v_sorted)
    dk[...] = jnp.zeros(dk.shape, f32)
    dv[...] = jnp.zeros(dv.shape, f32)
    for copy in copies[5:]:
        copy.wait()
    sent = []
    for a, out in enumerate((dq_own, dq_far, dq_side, dq_both)):
        dq_out = out_rest.at[a - 1] if a else out_own
        copies[1 + a].wait()
        load_heads(a, held.at[a], q_all, g_all, order, where, half)
        early, late, last_early, last_late = plan.limits(a, width)
        slot = where[a]
        late_at = jnp.where(order[slot] > order[slot + 1], 0, 1)
        for part, seen, last, at in ((0, late, last_late, late_at), (1, early, last_early, 1 - late_at)):
            q, g = q_all[part], g_all[part]
            shares = []
            for flip in range(4):
                r = 2 * (a ^ flip) + part
                shares.append(tuple(s_held[flip, j, r:r + 1, :] for j in range(3)))
            top = functools.reduce(jnp.maximum, (t for t, _, _ in shares))
            total = sum(n * jnp.exp2(t - top) for t, n, _ in shares)
            delta = sum(d * jnp.exp2(t - top) for t, _, d in shares) / total
            base = top + jnp.log2(total)
            dq[...] = jnp.zeros(dq.shape, f32)
            for start, size, condition, masked in tiles(seen, n_keys, half, part):

                def grads():
                    span = slice(start, start + size)
                    k = k_sorted[span, :]
                    s = masked_scores(k, q, start, last, masked)
                    p = jnp.exp2(s * TO_LOG2 - base)
                    d = lax.dot_general(v_sorted[span, :], g, NT, preferred_element_type=f32)
                    ds = (p * (d - delta)).astype(bf16)
                    dv[span, :] += jnp.dot(p.astype(bf16), g, preferred_element_type=f32)
                    dk[span, :] += jnp.dot(ds, q, preferred_element_type=f32)
                    dq[...] += lax.dot_general(k, ds, TN, preferred_element_type=f32)

                under(condition, grads)
            turned = (dq[...] * SCALE).T.astype(dq_out.dtype)
            rows = pl.ds(pl.multiple_of(at * half, half), half)
            for j in range(2 * GROUP):
                dq_out[rows, j * DH:(j + 1) * DH] = turned[j * half:(j + 1) * half, :]
        copy = pltpu.make_async_copy(dq_out, out, out_sems.at[a])
        copy.start()
        sent.append(copy)
    for b in range(n_keys):
        for i in range(2):
            of = plan.key_rows(b, i)
            rows = slice(i * half, (i + 1) * half)
            out_kv[b, rows, :DH] = (dk[of, :] * SCALE).astype(bf16)
            out_kv[b, rows, DH:] = dv[of, :].astype(bf16)
    copy = pltpu.make_async_copy(out_kv, dkv, out_sems.at[4])
    copy.start()
    for copy in sent + [copy]:
        copy.wait()


def scratch(n_keys, rows, copies):
    width = GROUP * rows
    return [
        pltpu.VMEM((4, rows, 4 * GROUP * DH), bf16),
        pltpu.VMEM((n_keys, rows, 2 * DH), bf16),
        pltpu.VMEM((n_keys * rows, DH), bf16),
        pltpu.VMEM((n_keys * rows, DH), bf16),
        pltpu.VMEM((2, width, DH), bf16),
        pltpu.VMEM((2, width, DH), bf16),
        pltpu.SemaphoreType.DMA((copies,)),
    ]


def cost(n_keys, rows, products):
    pairs = 4 * GROUP * rows * n_keys * rows
    return pl.CostEstimate(
        flops=2 * products * pairs * DH, bytes_accessed=8 * 2**20, transcendentals=pairs
    )


def attention_stats(order, where, own, far, side, both, kv):
    n_keys, rows, _ = kv.shape
    width = GROUP * rows
    return pl.pallas_call(
        stats_kernel,
        out_shape=jax.ShapeDtypeStruct((3, 8, width), f32),
        in_specs=[SMEM] * 2 + [ANY] * 5,
        out_specs=VMEM,
        scratch_shapes=scratch(n_keys, rows, 5)
        + [pltpu.VMEM((n_keys * rows, width), f32)]
        + [pltpu.VMEM((8, width), f32)] * 3,
        compiler_params=pltpu.CompilerParams(vmem_limit_bytes=BIG),
        cost_estimate=cost(n_keys, rows, 2),
    )(order, where, own, far, side, both, kv)


def attention_grads(order, where, own, far, side, both, kv, stats):
    n_keys, rows, _ = kv.shape
    width = GROUP * rows
    shape = (rows, 2 * GROUP * DH)
    return pl.pallas_call(
        grads_kernel,
        out_shape=(
            jax.ShapeDtypeStruct(shape, f32),
            jax.ShapeDtypeStruct(shape, bf16),
            jax.ShapeDtypeStruct(shape, bf16),
            jax.ShapeDtypeStruct(shape, bf16),
            jax.ShapeDtypeStruct(kv.shape, bf16),
        ),
        in_specs=[SMEM] * 2 + [ANY] * 9,
        out_specs=(ANY,) * 5,
        scratch_shapes=scratch(n_keys, rows, 9)
        + [
            pltpu.VMEM((4, 3, 8, width), f32),
            pltpu.VMEM(shape, f32),
            pltpu.VMEM((3,) + shape, bf16),
            pltpu.VMEM(kv.shape, bf16),
            pltpu.SemaphoreType.DMA((5,)),
        ]
        + [pltpu.VMEM((n_keys * rows, DH), f32)] * 2
        + [pltpu.VMEM((DH, width), f32)],
        compiler_params=pltpu.CompilerParams(vmem_limit_bytes=BIG),
        cost_estimate=cost(n_keys, rows, 5),
    )(order, where, own, far, side, both, kv, *stats)


def cut_kernel(at, x, out):
    out[0] = x[...]


def cut_input(x, at, count, stride, width):
    rows = x.shape[0]
    return pl.pallas_call(
        cut_kernel,
        grid_spec=pltpu.PrefetchScalarGridSpec(
            num_scalar_prefetch=1,
            grid=(count,),
            in_specs=[pl.BlockSpec((rows, width), lambda j, at: (0, at[0] + j * stride))],
            out_specs=pl.BlockSpec((1, rows, width), lambda j, at: (j, 0, 0)),
        ),
        out_shape=jax.ShapeDtypeStruct((count, rows, width), x.dtype),
    )(at, x)


def input_terms_kernel(grad, key_weight, value_weight, out):
    parts, _, columns = out.shape
    dk, dv = grad[:, :DH], grad[:, DH:]
    for j in range(parts):
        span = slice(j * columns, (j + 1) * columns)
        terms = lax.dot_general(dk, key_weight[span, :], NT, preferred_element_type=f32)
        terms += lax.dot_general(dv, value_weight[span, :], NT, preferred_element_type=f32)
        out[j] = terms.astype(bf16)


def input_terms(grad, key_weight, value_weight, parts):
    rows = grad.shape[0]
    columns = key_weight.shape[0] // parts
    return pl.pallas_call(
        input_terms_kernel,
        out_shape=jax.ShapeDtypeStruct((parts, rows, columns), bf16),
        in_specs=[VMEM] * 3,
        out_specs=VMEM,
        compiler_params=pltpu.CompilerParams(vmem_limit_bytes=12 * 2**20),
        cost_estimate=pl.CostEstimate(
            flops=4 * rows * DH * key_weight.shape[0], bytes_accessed=6 * 2**20, transcendentals=0
        ),
    )(grad, key_weight, value_weight)


def weight_terms_kernel(at, *refs):
    *blocks, cut, kept, sent, ring = refs
    core, z = at[0], at[1]
    n_z = len(blocks)
    rows = blocks[0].shape[0]
    for k, block in enumerate(blocks):
        source = lax.rem(z + n_z - k, n_z)
        ring[pl.ds(pl.multiple_of(source * rows, rows), rows), :] = block[...]
    n_xh = kept.shape[0]
    per = cut.shape[0] // (2 * n_xh)
    width = cut.shape[2]
    for out, c in ((sent, 1 - core), (kept, core)):
        for h in range(n_xh):
            for i in range(per):
                x = cut[(2 * h + c) * per + i]
                terms = lax.dot_general(ring[...], x, TN, preferred_element_type=f32)
                out[h, :, i * width:(i + 1) * width] = terms.astype(out.dtype)


def weight_terms(at, blocks, cut, n_xh):
    rows, columns = blocks[0].shape
    shape = (n_xh, columns, cut.shape[0] * cut.shape[2] // (2 * n_xh))
    return pl.pallas_call(
        weight_terms_kernel,
        out_shape=(jax.ShapeDtypeStruct(shape, f32), jax.ShapeDtypeStruct(shape, bf16)),
        in_specs=[SMEM] + [VMEM] * (len(blocks) + 1),
        out_specs=(VMEM, VMEM),
        scratch_shapes=[pltpu.VMEM((len(blocks) * rows, columns), bf16)],
        compiler_params=pltpu.CompilerParams(vmem_limit_bytes=12 * 2**20),
        cost_estimate=pl.CostEstimate(
            flops=4 * rows * len(blocks) * columns * shape[0] * shape[2], bytes_accessed=4 * 2**20, transcendentals=0
        ),
    )(at, *blocks, cut)


def half_sum_kernel(at, kept, came, mine, sent):
    xh = at[0]
    mine[...] = kept[xh] + came[xh].astype(f32)
    sent[...] = (kept[1 - xh] + came[1 - xh].astype(f32)).astype(bf16)


def half_sum(at, kept, came):
    shape = kept.shape[1:]
    return pl.pallas_call(
        half_sum_kernel,
        out_shape=(jax.ShapeDtypeStruct(shape, f32), jax.ShapeDtypeStruct(shape, bf16)),
        in_specs=[SMEM, VMEM, VMEM],
        out_specs=(VMEM, VMEM),
        compiler_params=pltpu.CompilerParams(vmem_limit_bytes=SMALL),
    )(at, kept, came)


def last_sum_kernel(mine, came, key_out, value_out):
    total = mine[...] + came[...].astype(f32)
    key_out[...] = total[:DH, :].T
    value_out[...] = total[DH:, :].T


def last_sum(mine, came):
    shape = jax.ShapeDtypeStruct((mine.shape[1], DH), f32)
    return pl.pallas_call(
        last_sum_kernel,
        out_shape=(shape, shape),
        in_specs=[VMEM, VMEM],
        out_specs=(VMEM, VMEM),
        compiler_params=pltpu.CompilerParams(vmem_limit_bytes=SMALL),
    )(mine, came)


def swap(x, axis):
    return lax.ppermute(x, axis, [(0, 1), (1, 0)])


def cross(x):
    return lax.ppermute(x, ("xh", "core"), [(0, 3), (1, 2), (2, 1), (3, 0)])


def to_all(x, axes, count):
    return lax.all_to_all(jnp.broadcast_to(x[None], (count,) + x.shape), axes, 0, 0)


def on_device(
    queries_one, grads_one, queries_two, grads_two, key_rows, value_rows,
    shared_input, key_weight, value_weight, block_order,
):
    rows, width = shared_input.shape
    n_xh, n_z, n_core, n_xl, n_y = (lax.axis_size(a) for a in CTX + HEAD)
    heads = n_xl * n_y
    core, xh, z = lax.axis_index("core"), lax.axis_index("xh"), lax.axis_index("z")
    head = lax.axis_index(HEAD)

    def slot(h, at, c):
        return 2 * ((h * n_z + at) * n_core + c)

    where = jnp.stack(
        [slot(xh, z, core), slot(1 - xh, z, core), slot(xh, z, 1 - core), slot(1 - xh, z, 1 - core)]
        + [slot(xh, b, core) for b in range(n_z)]
    ).astype(jnp.int32)

    with jax.named_scope("gather_keys"):
        kv = jnp.concatenate([key_rows, value_rows], axis=1)
        kv = jnp.broadcast_to(kv[None], (n_z,) + kv.shape)
        kv, queries_one, shared_input = lax.optimization_barrier((kv, queries_one, shared_input))
        kv = lax.all_to_all(kv, "z", 0, 0)
    with jax.named_scope("gather_queries"):
        own = jnp.concatenate([queries_one, grads_one, queries_two, grads_two], axis=1)
        far = swap(own, "xh")
        side = swap(own, "core")
        both = swap(far, "core")

    with jax.named_scope("cut_input"):
        piece = DH
        per = width // (n_xh * n_z * piece)
        at = (lax.div(head, per) * (n_z * per) + lax.rem(head, per)).astype(jnp.int32)
        cut = cut_input(shared_input, at.reshape(1), n_z, per, piece)

    with jax.named_scope("attention_stats"):
        stats = attention_stats(block_order, where, own, far, side, both, kv)
    with jax.named_scope("share_stats"):
        stats = (stats, swap(stats, "xh"), swap(stats, "core"), cross(stats))
    with jax.named_scope("spread_input"):
        cut = lax.all_to_all(cut, "z", 0, 0)
    with jax.named_scope("attention_grads"):
        stats, cut = lax.optimization_barrier((stats, cut))
        dq_own, dq_far, dq_side, dq_both, dkv = attention_grads(
            block_order, where, own, far, side, both, kv, stats
        )
    with jax.named_scope("spread_input"):
        cut = lax.all_gather(cut.reshape(n_z * rows, piece), HEAD)

    with jax.named_scope("scatter_grads"):
        dkv = lax.all_to_all(dkv, "z", 0, 0)
        came = (swap(dq_far, "xh"), swap(dq_side, "core"), cross(dq_both))
        dkv, came = lax.optimization_barrier((dkv, came))
        grad = jnp.sum(dkv.astype(f32), axis=0).astype(bf16)
    with jax.named_scope("query_grads"):
        dq = (dq_own + sum(x.astype(f32) for x in came)).astype(bf16)
        dq_one, dq_two = dq[:, :GROUP * DH], dq[:, GROUP * DH:]

    with jax.named_scope("input_grad"):
        terms = lax.all_to_all(input_terms(grad, key_weight, value_weight, heads), HEAD, 0, 0)
        input_grad = jnp.sum(terms.astype(f32), axis=0).astype(bf16)

    with jax.named_scope("weight_grad"):
        blocks = [grad] + [
            lax.ppermute(grad, "z", [(i, (i + k) % n_z) for i in range(n_z)]) for k in range(1, n_z)
        ]
        at = jnp.stack([core, z]).astype(jnp.int32)
        kept, sent = weight_terms(at, blocks, cut, n_xh)
        kept, sent = half_sum(xh.astype(jnp.int32).reshape(1), kept, swap(sent, "core"))
        key_weight_grad, value_weight_grad = last_sum(kept, swap(sent, "xh"))
    return (dq_one, dq_two, input_grad, key_weight_grad, value_weight_grad)


def solution(mesh):
    fine = Mesh(mesh.devices.reshape(2, 8, 2, 2, 4), CTX + HEAD)
    both = P(CTX, HEAD)
    return jax.shard_map(
        on_device,
        mesh=fine,
        in_specs=(both,) * 6 + (P(CTX, None), P(None, HEAD), P(None, HEAD), P()),
        out_specs=(both,) * 5,
        check_vma=False,
    )
```

```python
import functools
import math

import jax
import jax.numpy as jnp
from jax import lax
from jax.experimental import pallas as pl
from jax.experimental.pallas import tpu as pltpu
from jax.sharding import Mesh
from jax.sharding import PartitionSpec as P

H = 32
KV = 8
DH = 128
GROUP = H // KV
CTX = ("xh", "z", "core")
HEAD = ("xl", "y")
NT = (((1,), (1,)), ((), ()))
TN = (((0,), (0,)), ((), ()))
f32 = jnp.float32
bf16 = jnp.bfloat16
SCALE = 1.0 / math.sqrt(DH)
TO_LOG2 = SCALE * math.log2(math.e)
LOWEST = -1e30
BIG = 59 * 2**20
SMALL = 8 * 2**20
VMEM = pl.BlockSpec(memory_space=pltpu.VMEM)
SMEM = pl.BlockSpec(memory_space=pltpu.SMEM)
ANY = pl.BlockSpec(memory_space=pl.ANY)


class Plan:
    def __init__(self, order, where, n_keys, half):
        self.half = half
        self.n_keys = n_keys
        self.order, self.where = order, where
        self.near = []
        for b in range(n_keys):
            slot = where[4 + b]
            self.near.append(jnp.minimum(order[slot], order[slot + 1]))
        self.rank = []
        for b in range(n_keys):
            r = jnp.int32(0)
            for o in range(n_keys):
                r += jnp.where(self.near[o] < self.near[b], 1, 0)
            self.rank.append(r)

    def key_rows(self, b, i):
        pos = self.order[self.where[4 + b] + i]
        r = self.rank[b]
        at = jnp.where(pos == self.near[b], r, 2 * self.n_keys - 1 - r)
        return pl.ds(pl.multiple_of(at * self.half, self.half), self.half)

    def limits(self, a, width):
        slot = self.where[a]
        first, second = self.order[slot], self.order[slot + 1]
        mine = jnp.minimum(first, second)
        below, upto = jnp.int32(0), jnp.int32(0)
        for near in self.near:
            below += jnp.where(near < mine, 1, 0)
            upto += jnp.where(near <= mine, 1, 0)
        early, late = upto, 2 * self.n_keys - below
        inside = lax.rem(lax.broadcasted_iota(jnp.int32, (1, width), 1), self.half)
        same = upto > below

        def last(blocks):
            return jnp.where(same, (blocks - 1) * self.half + inside, blocks * self.half - 1)

        return early, late, last(early), last(late)


def load_heads(a, ref, q_all, g_all, order, where, half):
    slot = where[a]
    late_at = jnp.where(order[slot] > order[slot + 1], 0, 1)
    for part, at in ((0, late_at), (1, 1 - late_at)):
        rows = pl.ds(pl.multiple_of(at * half, half), half)
        for layer in range(2):
            for h in range(GROUP):
                r = (layer * GROUP + h) * half
                c = (layer * 2 * GROUP + h) * DH
                q_all[part, r:r + half, :] = ref[rows, c:c + DH]
                c += GROUP * DH
                g_all[part, r:r + half, :] = ref[rows, c:c + DH]


def fetch(pairs, sems):
    copies = [pltpu.make_async_copy(src, dst, sems.at[i]) for i, (src, dst) in enumerate(pairs)]
    for copy in copies:
        copy.start()
    return copies


def sort_keys(plan, kv, k_sorted, v_sorted):
    for b in range(plan.n_keys):
        for i in range(2):
            to = plan.key_rows(b, i)
            rows = slice(i * plan.half, (i + 1) * plan.half)
            k_sorted[to, :] = kv[b, rows, :DH]
            v_sorted[to, :] = kv[b, rows, DH:]


def fold(x, op):
    return op(x.reshape(x.shape[0] // 8, 8, x.shape[1]), axis=0)


def tiles(seen, n_keys, half, part):
    step = n_keys * half // 2
    if part == 0:
        return (
            (0, 2 * step, None, False),
            (2 * step, step, seen > n_keys, True),
            (3 * step, step, seen > n_keys + n_keys // 2, True),
        )
    return ((0, step, seen > 0, True), (step, step, seen > n_keys // 2, True))


def under(condition, body):
    if condition is None:
        body()
    else:
        pl.when(condition)(body)


def masked_scores(k, q, start, last, masked):
    s = lax.dot_general(k, q, NT, preferred_element_type=f32)
    if masked:
        key = start + lax.broadcasted_iota(jnp.int32, s.shape, 0)
        s = jnp.where(key <= last, s, -jnp.inf)
    return s


def stats_kernel(
    order, where, own, far, side, both, packed, stats, piece, held, kv_held, k_sorted, v_sorted, q_all, g_all, sems,
    scores, peak, total, delta,
):
    half = own.shape[0] // 2
    n_keys = packed.shape[0]
    width = q_all.shape[1]
    copies = fetch(
        [(packed.at[:, :, :2 * DH], kv_held)]
        + [(ref, held.at[a]) for a, ref in enumerate((own, far, side, both))]
        + [(packed.at[:, :, 2 * DH:], piece)],
        sems,
    )
    plan = Plan(order, where, n_keys, half)
    copies[0].wait()
    sort_keys(plan, kv_held, k_sorted, v_sorted)
    for a in range(4):
        copies[1 + a].wait()
        load_heads(a, held.at[a], q_all, g_all, order, where, half)
        early, late, last_early, last_late = plan.limits(a, width)
        for part, seen, last in ((0, late, last_late), (1, early, last_early)):
            q, g = q_all[part], g_all[part]
            peak[...] = jnp.full(peak.shape, LOWEST, f32)
            for start, size, condition, masked in tiles(seen, n_keys, half, part):

                def score():
                    s = masked_scores(k_sorted[start:start + size, :], q, start, last, masked)
                    scores[start:start + size, :] = s
                    peak[...] = jnp.maximum(peak[...], fold(s, jnp.max))

                under(condition, score)
            top = jnp.max(peak[...], axis=0, keepdims=True) * TO_LOG2
            total[...] = jnp.zeros(total.shape, f32)
            delta[...] = jnp.zeros(delta.shape, f32)
            for start, size, condition, masked in tiles(seen, n_keys, half, part):

                def weigh():
                    e = jnp.exp2(scores[start:start + size, :] * TO_LOG2 - top)
                    d = lax.dot_general(
                        v_sorted[start:start + size, :], g, NT, preferred_element_type=f32
                    )
                    total[...] += fold(e, jnp.sum)
                    delta[...] += fold(e * d, jnp.sum)

                under(condition, weigh)
            row = 2 * a + part
            stats[0, row:row + 1, :] = top
            stats[1, row:row + 1, :] = jnp.sum(total[...], axis=0, keepdims=True)
            stats[2, row:row + 1, :] = jnp.sum(delta[...], axis=0, keepdims=True)
    copies[5].wait()


def grads_kernel(
    order, where, own, far, side, both, packed, s_own, s_far, s_side, s_both, piece, near, dq_own, dq_far, dq_pair, dkv,
    pieces,
    held, kv_held, k_sorted, v_sorted, q_all, g_all, sems, s_held, out_mine, out_pair, out_kv, out_sems, dk, dv, dq,
):
    half = own.shape[0] // 2
    n_keys = packed.shape[0]
    width = q_all.shape[1]
    copies = fetch(
        [(packed.at[:, :, :2 * DH], kv_held)]
        + [(ref, held.at[a]) for a, ref in enumerate((own, far, side, both))]
        + [(ref, s_held.at[a]) for a, ref in enumerate((s_own, s_far, s_side, s_both))]
        + [(piece, pieces.at[0]), (near, pieces.at[1])],
        sems,
    )
    plan = Plan(order, where, n_keys, half)
    copies[0].wait()
    sort_keys(plan, kv_held, k_sorted, v_sorted)
    dk[...] = jnp.zeros(dk.shape, f32)
    dv[...] = jnp.zeros(dv.shape, f32)
    for copy in copies[5:9]:
        copy.wait()
    sent = []
    for a, out in enumerate((dq_own, dq_far, dq_pair.at[0], dq_pair.at[1])):
        dq_out = out_pair.at[a - 2] if a > 1 else out_mine.at[a]
        copies[1 + a].wait()
        load_heads(a, held.at[a], q_all, g_all, order, where, half)
        early, late, last_early, last_late = plan.limits(a, width)
        slot = where[a]
        late_at = jnp.where(order[slot] > order[slot + 1], 0, 1)
        for part, seen, last, at in ((0, late, last_late, late_at), (1, early, last_early, 1 - late_at)):
            q, g = q_all[part], g_all[part]
            shares = []
            for flip in range(4):
                r = 2 * (a ^ flip) + part
                shares.append(tuple(s_held[flip, j, r:r + 1, :] for j in range(3)))
            top = functools.reduce(jnp.maximum, (t for t, _, _ in shares))
            total = sum(n * jnp.exp2(t - top) for t, n, _ in shares)
            delta = sum(d * jnp.exp2(t - top) for t, _, d in shares) / total
            base = top + jnp.log2(total)
            dq[...] = jnp.zeros(dq.shape, f32)
            for start, size, condition, masked in tiles(seen, n_keys, half, part):

                def grads():
                    span = slice(start, start + size)
                    k = k_sorted[span, :]
                    s = masked_scores(k, q, start, last, masked)
                    p = jnp.exp2(s * TO_LOG2 - base)
                    d = lax.dot_general(v_sorted[span, :], g, NT, preferred_element_type=f32)
                    ds = (p * (d - delta)).astype(bf16)
                    dv[span, :] += jnp.dot(p.astype(bf16), g, preferred_element_type=f32)
                    dk[span, :] += jnp.dot(ds, q, preferred_element_type=f32)
                    dq[...] += lax.dot_general(k, ds, TN, preferred_element_type=f32)

                under(condition, grads)
            turned = (dq[...] * SCALE).T.astype(dq_out.dtype)
            rows = pl.ds(pl.multiple_of(at * half, half), half)
            for j in range(2 * GROUP):
                dq_out[rows, j * DH:(j + 1) * DH] = turned[j * half:(j + 1) * half, :]
        copy = pltpu.make_async_copy(dq_out, out, out_sems.at[a])
        copy.start()
        sent.append(copy)
    for b in range(n_keys):
        for i in range(2):
            of = plan.key_rows(b, i)
            rows = slice(i * half, (i + 1) * half)
            out_kv[b, rows, :DH] = (dk[of, :] * SCALE).astype(bf16)
            out_kv[b, rows, DH:] = dv[of, :].astype(bf16)
    copy = pltpu.make_async_copy(out_kv, dkv, out_sems.at[4])
    copy.start()
    for copy in sent + [copy] + copies[9:]:
        copy.wait()


def scratch(n_keys, rows, copies):
    width = GROUP * rows
    return [
        pltpu.VMEM((4, rows, 4 * GROUP * DH), bf16),
        pltpu.VMEM((n_keys, rows, 2 * DH), bf16),
        pltpu.VMEM((n_keys * rows, DH), bf16),
        pltpu.VMEM((n_keys * rows, DH), bf16),
        pltpu.VMEM((2, width, DH), bf16),
        pltpu.VMEM((2, width, DH), bf16),
        pltpu.SemaphoreType.DMA((copies,)),
    ]


def cost(n_keys, rows, products):
    pairs = 4 * GROUP * rows * n_keys * rows
    return pl.CostEstimate(
        flops=2 * products * pairs * DH, bytes_accessed=8 * 2**20, transcendentals=pairs
    )


def attention_stats(order, where, own, far, side, both, packed):
    n_keys, rows, _ = packed.shape
    width = GROUP * rows
    return pl.pallas_call(
        stats_kernel,
        out_shape=(
            jax.ShapeDtypeStruct((3, 8, width), f32),
            jax.ShapeDtypeStruct((n_keys, rows, DH), bf16),
        ),
        in_specs=[SMEM] * 2 + [ANY] * 5,
        out_specs=(VMEM, ANY),
        scratch_shapes=scratch(n_keys, rows, 6)
        + [pltpu.VMEM((n_keys * rows, width), f32)]
        + [pltpu.VMEM((8, width), f32)] * 3,
        compiler_params=pltpu.CompilerParams(vmem_limit_bytes=BIG),
        cost_estimate=cost(n_keys, rows, 2),
    )(order, where, own, far, side, both, packed)


def attention_grads(order, where, own, far, side, both, packed, stats, piece, near):
    n_keys, rows, _ = packed.shape
    width = GROUP * rows
    shape = (rows, 2 * GROUP * DH)
    return pl.pallas_call(
        grads_kernel,
        out_shape=(
            jax.ShapeDtypeStruct(shape, f32),
            jax.ShapeDtypeStruct(shape, f32),
            jax.ShapeDtypeStruct((2,) + shape, bf16),
            jax.ShapeDtypeStruct((n_keys, rows, 2 * DH), bf16),
            jax.ShapeDtypeStruct((2,) + piece.shape, bf16),
        ),
        in_specs=[SMEM] * 2 + [ANY] * 11,
        out_specs=(ANY,) * 5,
        scratch_shapes=scratch(n_keys, rows, 11)
        + [
            pltpu.VMEM((4, 3, 8, width), f32),
            pltpu.VMEM((2,) + shape, f32),
            pltpu.VMEM((2,) + shape, bf16),
            pltpu.VMEM((n_keys, rows, 2 * DH), bf16),
            pltpu.SemaphoreType.DMA((5,)),
        ]
        + [pltpu.VMEM((n_keys * rows, DH), f32)] * 2
        + [pltpu.VMEM((DH, width), f32)],
        compiler_params=pltpu.CompilerParams(vmem_limit_bytes=BIG),
        cost_estimate=cost(n_keys, rows, 5),
    )(order, where, own, far, side, both, packed, *stats, piece, near)


def pack_kernel(at, *refs):
    *heads, key_rows, value_rows, x, own, packed, sems = refs
    count = packed.shape[0]
    stride = x.shape[1] // (2 * count)
    wide = heads[0].shape[1]
    pairs = []
    for j in range(count):
        columns = pl.ds(pl.multiple_of(at[0] * DH + j * stride, DH), DH)
        for i, ref in enumerate((key_rows, value_rows, x.at[:, columns])):
            pairs.append((ref, packed.at[j, :, i * DH:(i + 1) * DH]))
    for i, ref in enumerate(heads):
        pairs.append((ref, own.at[:, i * wide:(i + 1) * wide]))
    for copy in fetch(pairs, sems):
        copy.wait()


def pack(at, heads, key_rows, value_rows, x, count):
    rows = x.shape[0]
    return pl.pallas_call(
        pack_kernel,
        in_specs=[SMEM] + [ANY] * (len(heads) + 3),
        out_specs=(ANY, ANY),
        out_shape=(
            jax.ShapeDtypeStruct((rows, len(heads) * heads[0].shape[1]), bf16),
            jax.ShapeDtypeStruct((count, rows, 3 * DH), bf16),
        ),
        scratch_shapes=[pltpu.SemaphoreType.DMA((3 * count + len(heads),))],
        compiler_params=pltpu.CompilerParams(vmem_limit_bytes=BIG),
    )(at, *heads, key_rows, value_rows, x)


def input_terms_kernel(parts, key_weight, value_weight, grad, out, held, total, k_held, v_held, terms, sems, out_sems):
    columns = out.shape[2]
    n = out.shape[0]
    spans = [pl.ds(j * columns, columns) for j in range(n)]
    [parts_in] = fetch([(parts, held)], sems.at[2])
    k_in = fetch([(key_weight.at[p], k_held.at[p]) for p in spans], sems.at[0])
    v_in = fetch([(value_weight.at[p], v_held.at[p]) for p in spans], sems.at[1])
    parts_in.wait()
    whole = held[0].astype(f32)
    for i in range(1, held.shape[0]):
        whole += held[i].astype(f32)
    total[...] = whole.astype(bf16)
    grad[...] = total[...]
    outs = []
    for j in range(n):
        k_in[j].wait()
        v_in[j].wait()
        t = lax.dot_general(total[:, :DH], k_held[spans[j], :], NT, preferred_element_type=f32)
        t += lax.dot_general(total[:, DH:], v_held[spans[j], :], NT, preferred_element_type=f32)
        terms[j] = t.astype(bf16)
        copy = pltpu.make_async_copy(terms.at[j], out.at[j], out_sems.at[j])
        copy.start()
        outs.append(copy)
    for copy in outs:
        copy.wait()


def input_terms(parts, key_weight, value_weight, heads):
    rows = parts.shape[1]
    columns = key_weight.shape[0] // heads
    shape = (heads, rows, columns)
    return pl.pallas_call(
        input_terms_kernel,
        out_shape=(
            jax.ShapeDtypeStruct(parts.shape[1:], bf16),
            jax.ShapeDtypeStruct(shape, bf16),
        ),
        in_specs=[ANY] * 3,
        out_specs=(VMEM, ANY),
        scratch_shapes=[
            pltpu.VMEM(parts.shape, bf16),
            pltpu.VMEM(parts.shape[1:], bf16),
            pltpu.VMEM(key_weight.shape, bf16),
            pltpu.VMEM(key_weight.shape, bf16),
            pltpu.VMEM(shape, bf16),
            pltpu.SemaphoreType.DMA((3, heads)),
            pltpu.SemaphoreType.DMA((heads,)),
        ],
        compiler_params=pltpu.CompilerParams(vmem_limit_bytes=BIG),
        cost_estimate=pl.CostEstimate(
            flops=4 * rows * DH * key_weight.shape[0], bytes_accessed=6 * 2**20, transcendentals=0
        ),
    )(parts, key_weight, value_weight)


def weight_terms_kernel(at, *refs):
    (*blocks, p0, p1, p2, p3), (kept, sent, held, ring, terms, sems) = refs[:-6], refs[-6:]
    core, z, xl, y = at[0], at[1], at[2], at[3]
    copies = fetch([(p, held.at[i]) for i, p in enumerate((p0, p1, p2, p3))], sems)
    n_z = len(blocks)
    rows = blocks[0].shape[0]
    for k, block in enumerate(blocks):
        ring[lax.rem(z + n_z - k, n_z)] = block[...]
    gathered = ring[...].reshape(n_z * rows, ring.shape[2])
    for i in range(4):
        copies[i].wait()
        other = y ^ i
        for j in range(2):
            x = held[i, j].reshape(n_z * rows, DH)
            terms[xl ^ j, lax.div(other, 2), lax.rem(other, 2)] = lax.dot_general(
                gathered, x, TN, preferred_element_type=f32
            )
    for h in range(2):
        kept[h] = terms[h, core]
        sent[h] = terms[h, 1 - core].astype(bf16)


def weight_terms(at, blocks, pieces):
    rows, columns = blocks[0].shape
    shape = (2, 2, columns, DH)
    return pl.pallas_call(
        weight_terms_kernel,
        out_shape=(jax.ShapeDtypeStruct(shape, f32), jax.ShapeDtypeStruct(shape, bf16)),
        in_specs=[SMEM] + [VMEM] * len(blocks) + [ANY] * 4,
        out_specs=(VMEM, VMEM),
        scratch_shapes=[
            pltpu.VMEM((4,) + pieces[0].shape, bf16),
            pltpu.VMEM((len(blocks), rows, columns), bf16),
            pltpu.VMEM((2,) + shape, f32),
            pltpu.SemaphoreType.DMA((4,)),
        ],
        compiler_params=pltpu.CompilerParams(vmem_limit_bytes=40 * 2**20),
        cost_estimate=pl.CostEstimate(
            flops=16 * rows * len(blocks) * columns * DH, bytes_accessed=4 * 2**20, transcendentals=0
        ),
    )(at, *blocks, *pieces)


def half_sum_kernel(at, kept, came, mine, sent):
    xh = at[0]
    mine[...] = kept[xh] + came[xh].astype(f32)
    sent[...] = (kept[1 - xh] + came[1 - xh].astype(f32)).astype(bf16)


def half_sum(at, kept, came):
    shape = kept.shape[1:]
    return pl.pallas_call(
        half_sum_kernel,
        out_shape=(jax.ShapeDtypeStruct(shape, f32), jax.ShapeDtypeStruct(shape, bf16)),
        in_specs=[SMEM, VMEM, VMEM],
        out_specs=(VMEM, VMEM),
        compiler_params=pltpu.CompilerParams(vmem_limit_bytes=SMALL),
    )(at, kept, came)


def last_sum_kernel(mine, came, key_out, value_out):
    for i in range(mine.shape[0]):
        total = mine[i] + came[i].astype(f32)
        key_out[i * DH:(i + 1) * DH, :] = total[:DH, :].T
        value_out[i * DH:(i + 1) * DH, :] = total[DH:, :].T


def last_sum(mine, came):
    shape = jax.ShapeDtypeStruct((mine.shape[0] * DH, DH), f32)
    return pl.pallas_call(
        last_sum_kernel,
        out_shape=(shape, shape),
        in_specs=[VMEM, VMEM],
        out_specs=(VMEM, VMEM),
        compiler_params=pltpu.CompilerParams(vmem_limit_bytes=SMALL),
    )(mine, came)


def swap(x, axis):
    return lax.ppermute(x, axis, [(0, 1), (1, 0)])


def cross(x):
    return lax.ppermute(x, ("xh", "core"), [(0, 3), (1, 2), (2, 1), (3, 0)])


def on_device(
    queries_one, grads_one, queries_two, grads_two, key_rows, value_rows,
    shared_input, key_weight, value_weight, block_order,
):
    rows, width = shared_input.shape
    n_xh, n_z, n_core, n_xl, n_y = (lax.axis_size(a) for a in CTX + HEAD)
    heads = n_xl * n_y
    core, xh, z = lax.axis_index("core"), lax.axis_index("xh"), lax.axis_index("z")
    head = lax.axis_index(HEAD)

    def slot(h, at, c):
        return 2 * ((h * n_z + at) * n_core + c)

    where = jnp.stack(
        [slot(xh, z, core), slot(1 - xh, z, core), slot(xh, z, 1 - core), slot(1 - xh, z, 1 - core)]
        + [slot(xh, b, core) for b in range(n_z)]
    ).astype(jnp.int32)

    per = width // (n_xh * n_z * DH)
    at = (lax.div(head, per) * (n_z * per) + lax.rem(head, per)).astype(jnp.int32).reshape(1)

    with jax.named_scope("gather"):
        own, packed = pack(
            at, (queries_one, grads_one, queries_two, grads_two), key_rows, value_rows, shared_input, n_z
        )
        packed = lax.all_to_all(packed, "z", 0, 0)
        far = swap(own, "xh")
        side = swap(own, "core")
        both = swap(far, "core")
        where, packed = lax.optimization_barrier((where, packed))

    with jax.named_scope("attention_stats"):
        stats, piece = attention_stats(block_order, where, own, far, side, both, packed)
    with jax.named_scope("share_stats"):
        stats = (stats, swap(stats, "xh"), swap(stats, "core"), cross(stats))
    with jax.named_scope("spread_input"):
        near = swap(piece, "xl")
    with jax.named_scope("attention_grads"):
        dq_own, dq_far, dq_pair, dkv, pieces = attention_grads(
            block_order, where, own, far, side, both, packed, stats, piece, near
        )
    with jax.named_scope("scatter_grads"):
        dkv = lax.all_to_all(dkv, "z", 0, 0)
    with jax.named_scope("query_grads"):
        dq_pair = swap(dq_pair, "core").astype(f32)
        dq_own = dq_own + dq_pair[0]
        dq_far = swap((dq_far + dq_pair[1]).astype(bf16), "xh")
    with jax.named_scope("spread_input"):
        pieces = [pieces] + [lax.ppermute(pieces, "y", [(i, i ^ j) for i in range(n_y)]) for j in (1, 2, 3)]
    with jax.named_scope("query_grads"):
        dkv, dq_own, dq_far, pieces = lax.optimization_barrier((dkv, dq_own, dq_far, pieces))
        dq = (dq_own + dq_far.astype(f32)).astype(bf16)
        dq_one, dq_two = dq[:, :GROUP * DH], dq[:, GROUP * DH:]

    with jax.named_scope("input_grad"):
        grad, terms = input_terms(dkv, key_weight, value_weight, heads)
        terms = lax.all_to_all(terms, HEAD, 0, 0)
        input_grad = jnp.sum(terms.astype(f32), axis=0).astype(bf16)

    with jax.named_scope("weight_grad"):
        blocks = [grad] + [
            lax.ppermute(grad, "z", [(i, (i + k) % n_z) for i in range(n_z)]) for k in range(1, n_z)
        ]
        place = jnp.stack([core, z, lax.axis_index("xl"), lax.axis_index("y")]).astype(jnp.int32)
        kept, sent = weight_terms(place, blocks, pieces)
        kept, sent = half_sum(xh.astype(jnp.int32).reshape(1), kept, swap(sent, "core"))
        key_weight_grad, value_weight_grad = last_sum(kept, swap(sent, "xh"))
    return (dq_one, dq_two, input_grad, key_weight_grad, value_weight_grad)


def solution(mesh):
    fine = Mesh(mesh.devices.reshape(2, 8, 2, 2, 4), CTX + HEAD)
    both = P(CTX, HEAD)
    return jax.shard_map(
        on_device,
        mesh=fine,
        in_specs=(both,) * 6 + (P(CTX, None), P(None, HEAD), P(None, HEAD), P()),
        out_specs=(both,) * 5,
        check_vma=False,
    )
```

```python
import functools
import math

import jax
import jax.numpy as jnp
from jax import lax
from jax.experimental import pallas as pl
from jax.experimental.pallas import tpu as pltpu
from jax.sharding import Mesh
from jax.sharding import PartitionSpec as P

H = 32
KV = 8
DH = 128
GROUP = H // KV
CTX = ("xh", "z", "core")
HEAD = ("xl", "y")
NT = (((1,), (1,)), ((), ()))
TN = (((0,), (0,)), ((), ()))
f32 = jnp.float32
bf16 = jnp.bfloat16
SCALE = 1.0 / math.sqrt(DH)
TO_LOG2 = SCALE * math.log2(math.e)
LOWEST = -1e30
BIG = 56 * 2**20
MIDDLE = 16 * 2**20
SMALL = 8 * 2**20
VMEM = pl.BlockSpec(memory_space=pltpu.VMEM)
SMEM = pl.BlockSpec(memory_space=pltpu.SMEM)
ANY = pl.BlockSpec(memory_space=pl.ANY)


class Plan:
    def __init__(self, order, where, n_keys, half):
        self.half = half
        self.n_keys = n_keys
        self.order, self.where = order, where
        self.near = []
        for b in range(n_keys):
            slot = where[4 + b]
            self.near.append(jnp.minimum(order[slot], order[slot + 1]))
        self.rank = []
        for b in range(n_keys):
            r = jnp.int32(0)
            for o in range(n_keys):
                r += jnp.where(self.near[o] < self.near[b], 1, 0)
            self.rank.append(r)

    def key_rows(self, b, i):
        pos = self.order[self.where[4 + b] + i]
        r = self.rank[b]
        at = jnp.where(pos == self.near[b], r, 2 * self.n_keys - 1 - r)
        return pl.ds(pl.multiple_of(at * self.half, self.half), self.half)

    def limits(self, a, width):
        slot = self.where[a]
        first, second = self.order[slot], self.order[slot + 1]
        mine = jnp.minimum(first, second)
        below, upto = jnp.int32(0), jnp.int32(0)
        for near in self.near:
            below += jnp.where(near < mine, 1, 0)
            upto += jnp.where(near <= mine, 1, 0)
        early, late = upto, 2 * self.n_keys - below
        inside = lax.rem(lax.broadcasted_iota(jnp.int32, (1, width), 1), self.half)
        same = upto > below

        def last(blocks):
            return jnp.where(same, (blocks - 1) * self.half + inside, blocks * self.half - 1)

        return early, late, last(early), last(late)


def load_heads(a, ref, q_all, g_all, order, where, half):
    slot = where[a]
    late_at = jnp.where(order[slot] > order[slot + 1], 0, 1)
    for part, at in ((0, late_at), (1, 1 - late_at)):
        rows = pl.ds(pl.multiple_of(at * half, half), half)
        for layer in range(2):
            for h in range(GROUP):
                r = (layer * GROUP + h) * half
                c = (layer * 2 * GROUP + h) * DH
                q_all[part, r:r + half, :] = ref[rows, c:c + DH]
                c += GROUP * DH
                g_all[part, r:r + half, :] = ref[rows, c:c + DH]


def fetch(pairs, sems):
    copies = [pltpu.make_async_copy(src, dst, sems.at[i]) for i, (src, dst) in enumerate(pairs)]
    for copy in copies:
        copy.start()
    return copies


def sort_keys(plan, kv, k_sorted, v_sorted):
    for b in range(plan.n_keys):
        for i in range(2):
            to = plan.key_rows(b, i)
            rows = slice(i * plan.half, (i + 1) * plan.half)
            k_sorted[to, :] = kv[b, rows, :DH]
            v_sorted[to, :] = kv[b, rows, DH:2 * DH]


def fold(x, op):
    return op(x.reshape(x.shape[0] // 8, 8, x.shape[1]), axis=0)


def tiles(seen, n_keys, half, part):
    step = n_keys * half // 2
    if part == 0:
        return (
            (0, 2 * step, None, False),
            (2 * step, step, seen > n_keys, True),
            (3 * step, step, seen > n_keys + n_keys // 2, True),
        )
    return ((0, step, seen > 0, True), (step, step, seen > n_keys // 2, True))


def under(condition, body):
    if condition is None:
        body()
    else:
        pl.when(condition)(body)


def masked_scores(k, q, start, last, masked):
    s = lax.dot_general(k, q, NT, preferred_element_type=f32)
    if masked:
        key = start + lax.broadcasted_iota(jnp.int32, s.shape, 0)
        s = jnp.where(key <= last, s, -jnp.inf)
    return s


def stats_kernel(
    order, where, own, far, side, both, packed, stats, held, kv_held, k_sorted, v_sorted, q_all, g_all, sems,
    scores, peak, total, delta,
):
    half = own.shape[0] // 2
    n_keys = packed.shape[0]
    width = q_all.shape[1]
    copies = fetch(
        [(packed, kv_held)] + [(ref, held.at[a]) for a, ref in enumerate((own, far, side, both))], sems
    )
    plan = Plan(order, where, n_keys, half)
    copies[0].wait()
    sort_keys(plan, kv_held, k_sorted, v_sorted)
    for a in range(4):
        copies[1 + a].wait()
        load_heads(a, held.at[a], q_all, g_all, order, where, half)
        early, late, last_early, last_late = plan.limits(a, width)
        for part, seen, last in ((0, late, last_late), (1, early, last_early)):
            q, g = q_all[part], g_all[part]
            peak[...] = jnp.full(peak.shape, LOWEST, f32)
            for start, size, condition, masked in tiles(seen, n_keys, half, part):

                def score():
                    s = masked_scores(k_sorted[start:start + size, :], q, start, last, masked)
                    scores[start:start + size, :] = s
                    peak[...] = jnp.maximum(peak[...], fold(s, jnp.max))

                under(condition, score)
            top = jnp.max(peak[...], axis=0, keepdims=True) * TO_LOG2
            total[...] = jnp.zeros(total.shape, f32)
            delta[...] = jnp.zeros(delta.shape, f32)
            for start, size, condition, masked in tiles(seen, n_keys, half, part):

                def weigh():
                    e = jnp.exp2(scores[start:start + size, :] * TO_LOG2 - top)
                    d = lax.dot_general(
                        v_sorted[start:start + size, :], g, NT, preferred_element_type=f32
                    )
                    total[...] += fold(e, jnp.sum)
                    delta[...] += fold(e * d, jnp.sum)

                under(condition, weigh)
            row = 2 * a + part
            stats[0, row:row + 1, :] = top
            stats[1, row:row + 1, :] = jnp.sum(total[...], axis=0, keepdims=True)
            stats[2, row:row + 1, :] = jnp.sum(delta[...], axis=0, keepdims=True)


def grads_kernel(
    order, where, own, far, side, both, packed, s_own, s_far, s_side, s_both, dq_own, dq_far, dq_pair, dkv,
    held, kv_held, k_sorted, v_sorted, q_all, g_all, sems, s_held, out_mine, out_pair, out_kv, out_sems, dk, dv, dq,
):
    half = own.shape[0] // 2
    n_keys = packed.shape[0]
    width = q_all.shape[1]
    copies = fetch(
        [(packed, kv_held)]
        + [(ref, held.at[a]) for a, ref in enumerate((own, far, side, both))]
        + [(ref, s_held.at[a]) for a, ref in enumerate((s_own, s_far, s_side, s_both))],
        sems,
    )
    plan = Plan(order, where, n_keys, half)
    copies[0].wait()
    sort_keys(plan, kv_held, k_sorted, v_sorted)
    dk[...] = jnp.zeros(dk.shape, f32)
    dv[...] = jnp.zeros(dv.shape, f32)
    for copy in copies[5:9]:
        copy.wait()
    sent = []
    for a, out in enumerate((dq_own, dq_far, dq_pair.at[0], dq_pair.at[1])):
        dq_out = out_pair.at[a - 2] if a > 1 else out_mine.at[a]
        copies[1 + a].wait()
        load_heads(a, held.at[a], q_all, g_all, order, where, half)
        early, late, last_early, last_late = plan.limits(a, width)
        slot = where[a]
        late_at = jnp.where(order[slot] > order[slot + 1], 0, 1)
        for part, seen, last, at in ((0, late, last_late, late_at), (1, early, last_early, 1 - late_at)):
            q, g = q_all[part], g_all[part]
            shares = []
            for flip in range(4):
                r = 2 * (a ^ flip) + part
                shares.append(tuple(s_held[flip, j, r:r + 1, :] for j in range(3)))
            top = functools.reduce(jnp.maximum, (t for t, _, _ in shares))
            total = sum(n * jnp.exp2(t - top) for t, n, _ in shares)
            delta = sum(d * jnp.exp2(t - top) for t, _, d in shares) / total
            base = top + jnp.log2(total)
            dq[...] = jnp.zeros(dq.shape, f32)
            for start, size, condition, masked in tiles(seen, n_keys, half, part):

                def grads():
                    span = slice(start, start + size)
                    k = k_sorted[span, :]
                    s = masked_scores(k, q, start, last, masked)
                    p = jnp.exp2(s * TO_LOG2 - base)
                    d = lax.dot_general(v_sorted[span, :], g, NT, preferred_element_type=f32)
                    ds = (p * (d - delta)).astype(bf16)
                    dv[span, :] += jnp.dot(p.astype(bf16), g, preferred_element_type=f32)
                    dk[span, :] += jnp.dot(ds, q, preferred_element_type=f32)
                    dq[...] += lax.dot_general(k, ds, TN, preferred_element_type=f32)

                under(condition, grads)
            turned = (dq[...] * SCALE).T.astype(dq_out.dtype)
            rows = pl.ds(pl.multiple_of(at * half, half), half)
            for j in range(2 * GROUP):
                dq_out[rows, j * DH:(j + 1) * DH] = turned[j * half:(j + 1) * half, :]
        copy = pltpu.make_async_copy(dq_out, out, out_sems.at[a])
        copy.start()
        sent.append(copy)
    for b in range(n_keys):
        for i in range(2):
            of = plan.key_rows(b, i)
            rows = slice(i * half, (i + 1) * half)
            out_kv[b, rows, :DH] = (dk[of, :] * SCALE).astype(bf16)
            out_kv[b, rows, DH:] = dv[of, :].astype(bf16)
    copy = pltpu.make_async_copy(out_kv, dkv, out_sems.at[4])
    copy.start()
    for copy in sent + [copy]:
        copy.wait()


def scratch(n_keys, rows, copies):
    width = GROUP * rows
    return [
        pltpu.VMEM((4, rows, 4 * GROUP * DH), bf16),
        pltpu.VMEM((n_keys, rows, 2 * DH), bf16),
        pltpu.VMEM((n_keys * rows, DH), bf16),
        pltpu.VMEM((n_keys * rows, DH), bf16),
        pltpu.VMEM((2, width, DH), bf16),
        pltpu.VMEM((2, width, DH), bf16),
        pltpu.SemaphoreType.DMA((copies,)),
    ]


def cost(n_keys, rows, products):
    pairs = 4 * GROUP * rows * n_keys * rows
    return pl.CostEstimate(
        flops=2 * products * pairs * DH, bytes_accessed=8 * 2**20, transcendentals=pairs
    )


def attention_stats(order, where, own, far, side, both, packed):
    n_keys, rows, _ = packed.shape
    width = GROUP * rows
    return pl.pallas_call(
        stats_kernel,
        out_shape=jax.ShapeDtypeStruct((3, 8, width), f32),
        in_specs=[SMEM] * 2 + [ANY] * 5,
        out_specs=VMEM,
        scratch_shapes=scratch(n_keys, rows, 5)
        + [pltpu.VMEM((n_keys * rows, width), f32)]
        + [pltpu.VMEM((8, width), f32)] * 3,
        compiler_params=pltpu.CompilerParams(vmem_limit_bytes=BIG),
        cost_estimate=cost(n_keys, rows, 2),
    )(order, where, own, far, side, both, packed)


def attention_grads(order, where, own, far, side, both, packed, stats):
    n_keys, rows, _ = packed.shape
    width = GROUP * rows
    shape = (rows, 2 * GROUP * DH)
    return pl.pallas_call(
        grads_kernel,
        out_shape=(
            jax.ShapeDtypeStruct(shape, f32),
            jax.ShapeDtypeStruct(shape, f32),
            jax.ShapeDtypeStruct((2,) + shape, bf16),
            jax.ShapeDtypeStruct((n_keys, rows, 2 * DH), bf16),
        ),
        in_specs=[SMEM] * 2 + [ANY] * 9,
        out_specs=(ANY,) * 4,
        scratch_shapes=scratch(n_keys, rows, 9)
        + [
            pltpu.VMEM((4, 3, 8, width), f32),
            pltpu.VMEM((2,) + shape, f32),
            pltpu.VMEM((2,) + shape, bf16),
            pltpu.VMEM((n_keys, rows, 2 * DH), bf16),
            pltpu.SemaphoreType.DMA((5,)),
        ]
        + [pltpu.VMEM((n_keys * rows, DH), f32)] * 2
        + [pltpu.VMEM((DH, width), f32)],
        compiler_params=pltpu.CompilerParams(vmem_limit_bytes=BIG),
        cost_estimate=cost(n_keys, rows, 5),
    )(order, where, own, far, side, both, packed, *stats)


def pack_kernel(at, *refs):
    *heads, key_rows, value_rows, x, own, packed = refs[:-5]
    *cuts, sems = refs[-5:]
    count, _, wide = cuts[0].shape
    xh, core = at[0], at[1]
    pairs = []
    for j in range(count):
        for i, ref in enumerate((key_rows, value_rows)):
            pairs.append((ref, packed.at[j, :, i * DH:(i + 1) * DH]))
    side = heads[0].shape[1]
    for i, ref in enumerate(heads):
        pairs.append((ref, own.at[:, i * side:(i + 1) * side]))
    for i, cut in enumerate(cuts):
        lead = (xh ^ (i & 1)) * (2 * count) + (core ^ (i >> 1))
        for j in range(count):
            columns = pl.ds(pl.multiple_of((lead + 2 * j) * wide, wide), wide)
            pairs.append((x.at[:, columns], cut.at[j]))
    for copy in fetch(pairs, sems):
        copy.wait()


def pack(at, heads, key_rows, value_rows, x, count):
    rows = x.shape[0]
    cut = jax.ShapeDtypeStruct((count, rows, x.shape[1] // (4 * count)), bf16)
    return pl.pallas_call(
        pack_kernel,
        in_specs=[SMEM] + [ANY] * (len(heads) + 3),
        out_specs=(VMEM,) * 6,
        out_shape=(
            jax.ShapeDtypeStruct((rows, len(heads) * heads[0].shape[1]), bf16),
            jax.ShapeDtypeStruct((count, rows, 2 * DH), bf16),
            cut, cut, cut, cut,
        ),
        scratch_shapes=[pltpu.SemaphoreType.DMA((6 * count + len(heads),))],
        compiler_params=pltpu.CompilerParams(vmem_limit_bytes=BIG),
    )(at, *heads, key_rows, value_rows, x)


def key_sum_kernel(parts, grad):
    total = parts[0].astype(f32)
    for i in range(1, parts.shape[0]):
        total += parts[i].astype(f32)
    grad[...] = total.astype(bf16)


def key_sum(parts):
    return pl.pallas_call(
        key_sum_kernel,
        out_shape=jax.ShapeDtypeStruct(parts.shape[1:], bf16),
        in_specs=[VMEM],
        out_specs=VMEM,
        compiler_params=pltpu.CompilerParams(vmem_limit_bytes=SMALL),
    )(parts)


def input_terms_kernel(grad, key_weight, value_weight, out, k_held, v_held, terms, sems, out_sems):
    columns = out.shape[2]
    n = out.shape[0]
    spans = [pl.ds(j * columns, columns) for j in range(n)]
    k_in = fetch([(key_weight.at[p], k_held.at[p]) for p in spans], sems.at[0])
    v_in = fetch([(value_weight.at[p], v_held.at[p]) for p in spans], sems.at[1])
    outs = []
    for j in range(n):
        k_in[j].wait()
        v_in[j].wait()
        t = lax.dot_general(grad[:, :DH], k_held[spans[j], :], NT, preferred_element_type=f32)
        t += lax.dot_general(grad[:, DH:], v_held[spans[j], :], NT, preferred_element_type=f32)
        terms[j] = t.astype(bf16)
        copy = pltpu.make_async_copy(terms.at[j], out.at[j], out_sems.at[j])
        copy.start()
        outs.append(copy)
    for copy in outs:
        copy.wait()


def input_terms(grad, key_weight, value_weight, heads):
    rows = grad.shape[0]
    shape = (heads, rows, key_weight.shape[0] // heads)
    return pl.pallas_call(
        input_terms_kernel,
        out_shape=jax.ShapeDtypeStruct(shape, bf16),
        in_specs=[VMEM, ANY, ANY],
        out_specs=ANY,
        scratch_shapes=[
            pltpu.VMEM(key_weight.shape, bf16),
            pltpu.VMEM(key_weight.shape, bf16),
            pltpu.VMEM(shape, bf16),
            pltpu.SemaphoreType.DMA((2, heads)),
            pltpu.SemaphoreType.DMA((heads,)),
        ],
        compiler_params=pltpu.CompilerParams(vmem_limit_bytes=BIG),
        cost_estimate=pl.CostEstimate(
            flops=4 * rows * DH * key_weight.shape[0], bytes_accessed=6 * 2**20, transcendentals=0
        ),
    )(grad, key_weight, value_weight)


def weight_terms_kernel(at, g0, g1, g2, g3, x0, x1, x2, x3, *refs):
    *outs, held, turned, sems = refs
    z = at[0]
    copies = fetch([(x, held.at[i]) for i, x in enumerate((x0, x1, x2, x3))], sems)
    rows = g0.shape[0]
    for i, g in enumerate((g0, g1, g2, g3)):
        turned[:, i * rows:(i + 1) * rows] = g[...].T
    for copy in copies:
        copy.wait()
    n_z = len(outs)
    for k in reversed(range(n_z)):
        to = lax.rem(z + k, n_z)
        terms = jnp.dot(turned[:, :rows], held[0, to], preferred_element_type=f32)
        for i in range(1, 4):
            terms += jnp.dot(
                turned[:, i * rows:(i + 1) * rows], held[i, to], preferred_element_type=f32
            )
        outs[k][...] = terms.astype(outs[k].dtype)


def weight_terms(at, grads, cuts):
    rows, columns = grads[0].shape
    n_z = cuts[0].shape[0]
    shape = (columns, cuts[0].shape[2])
    return pl.pallas_call(
        weight_terms_kernel,
        out_shape=[jax.ShapeDtypeStruct(shape, bf16 if k else f32) for k in range(n_z)],
        in_specs=[SMEM] + [VMEM] * 4 + [ANY] * 4,
        out_specs=[VMEM] * n_z,
        scratch_shapes=[
            pltpu.VMEM((4,) + cuts[0].shape, bf16),
            pltpu.VMEM((columns, 4 * rows), bf16),
            pltpu.SemaphoreType.DMA((4,)),
        ],
        compiler_params=pltpu.CompilerParams(vmem_limit_bytes=MIDDLE),
        cost_estimate=pl.CostEstimate(
            flops=8 * rows * n_z * shape[0] * shape[1], bytes_accessed=4 * 2**20, transcendentals=0
        ),
    )(at, *grads, *cuts)


def weight_sum_kernel(*refs):
    *parts, key_out, value_out = refs
    total = parts[0][...]
    for part in parts[1:]:
        total += part[...].astype(f32)
    key_out[...] = total[:DH, :].T
    value_out[...] = total[DH:, :].T


def weight_sum(parts):
    shape = jax.ShapeDtypeStruct((parts[0].shape[1], DH), f32)
    return pl.pallas_call(
        weight_sum_kernel,
        out_shape=(shape, shape),
        in_specs=[VMEM] * len(parts),
        out_specs=(VMEM, VMEM),
        compiler_params=pltpu.CompilerParams(vmem_limit_bytes=SMALL),
    )(*parts)


def swap(x, axis):
    return lax.ppermute(x, axis, [(0, 1), (1, 0)])


def cross(x):
    return lax.ppermute(x, ("xh", "core"), [(0, 3), (1, 2), (2, 1), (3, 0)])


def on_device(
    queries_one, grads_one, queries_two, grads_two, key_rows, value_rows,
    shared_input, key_weight, value_weight, block_order,
):
    rows, width = shared_input.shape
    n_xh, n_z, n_core, n_xl, n_y = (lax.axis_size(a) for a in CTX + HEAD)
    heads = n_xl * n_y
    core, xh, z = lax.axis_index("core"), lax.axis_index("xh"), lax.axis_index("z")
    head = lax.axis_index(HEAD)

    def slot(h, at, c):
        return 2 * ((h * n_z + at) * n_core + c)

    where = jnp.stack(
        [slot(xh, z, core), slot(1 - xh, z, core), slot(xh, z, 1 - core), slot(1 - xh, z, 1 - core)]
        + [slot(xh, b, core) for b in range(n_z)]
    ).astype(jnp.int32)

    at = jnp.stack([xh, core]).astype(jnp.int32)

    with jax.named_scope("gather"):
        own, packed, *cuts = pack(
            at, (queries_one, grads_one, queries_two, grads_two), key_rows, value_rows, shared_input, n_z
        )
        packed = lax.all_to_all(packed, "z", 0, 0)
        far = swap(own, "xh")
        side = swap(own, "core")
        both = swap(far, "core")
        where, packed = lax.optimization_barrier((where, packed))
    with jax.named_scope("spread_input"):
        far, *cuts = lax.optimization_barrier((far, *cuts))
        cuts = [cuts[0], swap(cuts[1], "xh"), swap(cuts[2], "core"), cross(cuts[3])]

    with jax.named_scope("attention_stats"):
        stats = attention_stats(block_order, where, own, far, side, both, packed)
    with jax.named_scope("share_stats"):
        stats, *cuts = lax.optimization_barrier((stats, *cuts))
        stats = (stats, swap(stats, "xh"), swap(stats, "core"), cross(stats))
    with jax.named_scope("attention_grads"):
        dq_own, dq_far, dq_pair, dkv = attention_grads(
            block_order, where, own, far, side, both, packed, stats
        )
    with jax.named_scope("scatter_grads"):
        dkv = lax.all_to_all(dkv, "z", 0, 0)
    with jax.named_scope("query_grads"):
        dq_pair = swap(dq_pair, "core").astype(f32)
        dq_own = dq_own + dq_pair[0]
        dq_far = swap((dq_far + dq_pair[1]).astype(bf16), "xh")
        dkv, dq_own, dq_far = lax.optimization_barrier((dkv, dq_own, dq_far))
        dq = (dq_own + dq_far.astype(f32)).astype(bf16)
        dq_one, dq_two = dq[:, :GROUP * DH], dq[:, GROUP * DH:]
    with jax.named_scope("scatter_grads"):
        grad = key_sum(dkv)

        grads = [grad, swap(grad, "xh"), swap(grad, "core"), cross(grad)]

    with jax.named_scope("input_grad"):
        terms = input_terms(grad, key_weight, value_weight, heads)
        terms = lax.all_to_all(terms, HEAD, 0, 0)
        input_grad = jnp.sum(terms.astype(f32), axis=0).astype(bf16)

    with jax.named_scope("weight_grad"):
        own, *rest = weight_terms(z.astype(jnp.int32).reshape(1), grads, cuts)
        parts = [own] + [
            lax.ppermute(part, "z", [(i, (i + k) % n_z) for i in range(n_z)])
            for k, part in enumerate(rest, 1)
        ]
        key_weight_grad, value_weight_grad = weight_sum(parts)
    return (dq_one, dq_two, input_grad, key_weight_grad, value_weight_grad)


def solution(mesh):
    fine = Mesh(mesh.devices.reshape(2, 8, 2, 2, 4), CTX + HEAD)
    both = P(CTX, HEAD)
    return jax.shard_map(
        on_device,
        mesh=fine,
        in_specs=(both,) * 6 + (P(CTX, None), P(None, HEAD), P(None, HEAD), P()),
        out_specs=(both,) * 5,
        check_vma=False,
    )
```

```python
import functools
import math

import jax
import jax.numpy as jnp
from jax import lax
from jax.experimental import pallas as pl
from jax.experimental.pallas import tpu as pltpu
from jax.sharding import Mesh
from jax.sharding import PartitionSpec as P

H = 32
KV = 8
DH = 128
GROUP = H // KV
CTX = ("xh", "z", "core")
HEAD = ("xl", "y")
NT = (((1,), (1,)), ((), ()))
TN = (((0,), (0,)), ((), ()))
f32 = jnp.float32
bf16 = jnp.bfloat16
SCALE = 1.0 / math.sqrt(DH)
TO_LOG2 = SCALE * math.log2(math.e)
LOWEST = -1e30
BIG = 56 * 2**20
MIDDLE = 16 * 2**20
SMALL = 8 * 2**20
VMEM = pl.BlockSpec(memory_space=pltpu.VMEM)
SMEM = pl.BlockSpec(memory_space=pltpu.SMEM)
ANY = pl.BlockSpec(memory_space=pl.ANY)


class Plan:
    def __init__(self, order, where, n_keys, half):
        self.half = half
        self.n_keys = n_keys
        self.order, self.where = order, where
        self.near = []
        for b in range(n_keys):
            slot = where[4 + b]
            self.near.append(jnp.minimum(order[slot], order[slot + 1]))
        self.rank = []
        for b in range(n_keys):
            r = jnp.int32(0)
            for o in range(n_keys):
                r += jnp.where(self.near[o] < self.near[b], 1, 0)
            self.rank.append(r)

    def key_rows(self, b, i):
        pos = self.order[self.where[4 + b] + i]
        r = self.rank[b]
        at = jnp.where(pos == self.near[b], r, 2 * self.n_keys - 1 - r)
        return pl.ds(pl.multiple_of(at * self.half, self.half), self.half)

    def limits(self, a, width):
        slot = self.where[a]
        first, second = self.order[slot], self.order[slot + 1]
        mine = jnp.minimum(first, second)
        below, upto = jnp.int32(0), jnp.int32(0)
        for near in self.near:
            below += jnp.where(near < mine, 1, 0)
            upto += jnp.where(near <= mine, 1, 0)
        early, late = upto, 2 * self.n_keys - below
        inside = lax.rem(lax.broadcasted_iota(jnp.int32, (1, width), 1), self.half)
        same = upto > below

        def last(blocks):
            return jnp.where(same, (blocks - 1) * self.half + inside, blocks * self.half - 1)

        return early, late, last(early), last(late)


def load_heads(a, ref, q_all, g_all, order, where, half):
    slot = where[a]
    late_at = jnp.where(order[slot] > order[slot + 1], 0, 1)
    for part, at in ((0, late_at), (1, 1 - late_at)):
        rows = pl.ds(pl.multiple_of(at * half, half), half)
        for layer in range(2):
            for h in range(GROUP):
                r = (layer * GROUP + h) * half
                c = (layer * 2 * GROUP + h) * DH
                q_all[part, r:r + half, :] = ref[rows, c:c + DH]
                c += GROUP * DH
                g_all[part, r:r + half, :] = ref[rows, c:c + DH]


def fetch(pairs, sems):
    copies = [pltpu.make_async_copy(src, dst, sems.at[i]) for i, (src, dst) in enumerate(pairs)]
    for copy in copies:
        copy.start()
    return copies


def sort_keys(plan, kv, k_sorted, v_sorted):
    for b in range(plan.n_keys):
        for i in range(2):
            to = plan.key_rows(b, i)
            rows = slice(i * plan.half, (i + 1) * plan.half)
            k_sorted[to, :] = kv[b, rows, :DH]
            v_sorted[to, :] = kv[b, rows, DH:2 * DH]


def fold(x, op):
    return op(x.reshape(x.shape[0] // 8, 8, x.shape[1]), axis=0)


def tiles(seen, n_keys, half, part):
    step = n_keys * half // 2
    if part == 0:
        return (
            (0, 2 * step, None, False),
            (2 * step, step, seen > n_keys, True),
            (3 * step, step, seen > n_keys + n_keys // 2, True),
        )
    return ((0, step, seen > 0, True), (step, step, seen > n_keys // 2, True))


def under(condition, body):
    if condition is None:
        body()
    else:
        pl.when(condition)(body)


def masked_scores(k, q, start, last, masked):
    s = lax.dot_general(k, q, NT, preferred_element_type=f32)
    if masked:
        key = start + lax.broadcasted_iota(jnp.int32, s.shape, 0)
        s = jnp.where(key <= last, s, -jnp.inf)
    return s


def stats_kernel(
    order, where, own, far, side, both, packed, stats, held, kv_held, k_sorted, v_sorted, q_all, g_all, sems,
    scores, peak, total, delta,
):
    half = own.shape[0] // 2
    n_keys = packed.shape[0]
    width = q_all.shape[1]
    copies = fetch(
        [(packed, kv_held)] + [(ref, held.at[a]) for a, ref in enumerate((own, far, side, both))], sems
    )
    plan = Plan(order, where, n_keys, half)
    copies[0].wait()
    sort_keys(plan, kv_held, k_sorted, v_sorted)
    for a in range(4):
        copies[1 + a].wait()
        load_heads(a, held.at[a], q_all, g_all, order, where, half)
        early, late, last_early, last_late = plan.limits(a, width)
        for part, seen, last in ((0, late, last_late), (1, early, last_early)):
            q, g = q_all[part], g_all[part]
            peak[...] = jnp.full(peak.shape, LOWEST, f32)
            for start, size, condition, masked in tiles(seen, n_keys, half, part):

                def score():
                    s = masked_scores(k_sorted[start:start + size, :], q, start, last, masked)
                    scores[start:start + size, :] = s
                    peak[...] = jnp.maximum(peak[...], fold(s, jnp.max))

                under(condition, score)
            top = jnp.max(peak[...], axis=0, keepdims=True) * TO_LOG2
            total[...] = jnp.zeros(total.shape, f32)
            delta[...] = jnp.zeros(delta.shape, f32)
            for start, size, condition, masked in tiles(seen, n_keys, half, part):

                def weigh():
                    e = jnp.exp2(scores[start:start + size, :] * TO_LOG2 - top)
                    d = lax.dot_general(
                        v_sorted[start:start + size, :], g, NT, preferred_element_type=f32
                    )
                    total[...] += fold(e, jnp.sum)
                    delta[...] += fold(e * d, jnp.sum)

                under(condition, weigh)
            row = 2 * a + part
            stats[0, row:row + 1, :] = top
            stats[1, row:row + 1, :] = jnp.sum(total[...], axis=0, keepdims=True)
            stats[2, row:row + 1, :] = jnp.sum(delta[...], axis=0, keepdims=True)


def grads_kernel(
    order, where, own, far, side, both, packed, s_own, s_far, s_side, s_both, dq_own, dq_far, dq_pair, dkv,
    held, kv_held, k_sorted, v_sorted, q_all, g_all, sems, s_held, out_mine, out_pair, out_kv, out_sems, dk, dv, dq,
):
    half = own.shape[0] // 2
    n_keys = packed.shape[0]
    width = q_all.shape[1]
    copies = fetch(
        [(packed, kv_held)]
        + [(ref, held.at[a]) for a, ref in enumerate((own, far, side, both))]
        + [(ref, s_held.at[a]) for a, ref in enumerate((s_own, s_far, s_side, s_both))],
        sems,
    )
    plan = Plan(order, where, n_keys, half)
    copies[0].wait()
    sort_keys(plan, kv_held, k_sorted, v_sorted)
    dk[...] = jnp.zeros(dk.shape, f32)
    dv[...] = jnp.zeros(dv.shape, f32)
    for copy in copies[5:9]:
        copy.wait()
    sent = []
    for a, out in enumerate((dq_own, dq_far, dq_pair.at[0], dq_pair.at[1])):
        dq_out = out_pair.at[a - 2] if a > 1 else out_mine.at[a]
        copies[1 + a].wait()
        load_heads(a, held.at[a], q_all, g_all, order, where, half)
        early, late, last_early, last_late = plan.limits(a, width)
        slot = where[a]
        late_at = jnp.where(order[slot] > order[slot + 1], 0, 1)
        for part, seen, last, at in ((0, late, last_late, late_at), (1, early, last_early, 1 - late_at)):
            q, g = q_all[part], g_all[part]
            shares = []
            for flip in range(4):
                r = 2 * (a ^ flip) + part
                shares.append(tuple(s_held[flip, j, r:r + 1, :] for j in range(3)))
            top = functools.reduce(jnp.maximum, (t for t, _, _ in shares))
            total = sum(n * jnp.exp2(t - top) for t, n, _ in shares)
            delta = sum(d * jnp.exp2(t - top) for t, _, d in shares) / total
            base = top + jnp.log2(total)
            dq[...] = jnp.zeros(dq.shape, f32)
            for start, size, condition, masked in tiles(seen, n_keys, half, part):

                def grads():
                    span = slice(start, start + size)
                    k = k_sorted[span, :]
                    s = masked_scores(k, q, start, last, masked)
                    p = jnp.exp2(s * TO_LOG2 - base)
                    d = lax.dot_general(v_sorted[span, :], g, NT, preferred_element_type=f32)
                    ds = (p * (d - delta)).astype(bf16)
                    dv[span, :] += jnp.dot(p.astype(bf16), g, preferred_element_type=f32)
                    dk[span, :] += jnp.dot(ds, q, preferred_element_type=f32)
                    dq[...] += lax.dot_general(k, ds, TN, preferred_element_type=f32)

                under(condition, grads)
            turned = (dq[...] * SCALE).T.astype(dq_out.dtype)
            rows = pl.ds(pl.multiple_of(at * half, half), half)
            for j in range(2 * GROUP):
                dq_out[rows, j * DH:(j + 1) * DH] = turned[j * half:(j + 1) * half, :]
        copy = pltpu.make_async_copy(dq_out, out, out_sems.at[a])
        copy.start()
        sent.append(copy)
    for b in range(n_keys):
        for i in range(2):
            of = plan.key_rows(b, i)
            rows = slice(i * half, (i + 1) * half)
            out_kv[b, rows, :DH] = (dk[of, :] * SCALE).astype(bf16)
            out_kv[b, rows, DH:] = dv[of, :].astype(bf16)
    copy = pltpu.make_async_copy(out_kv, dkv, out_sems.at[4])
    copy.start()
    for copy in sent + [copy]:
        copy.wait()


def scratch(n_keys, rows, copies):
    width = GROUP * rows
    return [
        pltpu.VMEM((4, rows, 4 * GROUP * DH), bf16),
        pltpu.VMEM((n_keys, rows, 2 * DH), bf16),
        pltpu.VMEM((n_keys * rows, DH), bf16),
        pltpu.VMEM((n_keys * rows, DH), bf16),
        pltpu.VMEM((2, width, DH), bf16),
        pltpu.VMEM((2, width, DH), bf16),
        pltpu.SemaphoreType.DMA((copies,)),
    ]


def cost(n_keys, rows, products):
    pairs = 4 * GROUP * rows * n_keys * rows
    return pl.CostEstimate(
        flops=2 * products * pairs * DH, bytes_accessed=8 * 2**20, transcendentals=pairs
    )


def attention_stats(order, where, own, far, side, both, packed):
    n_keys, rows, _ = packed.shape
    width = GROUP * rows
    return pl.pallas_call(
        stats_kernel,
        out_shape=jax.ShapeDtypeStruct((3, 8, width), f32),
        in_specs=[SMEM] * 2 + [ANY] * 5,
        out_specs=VMEM,
        scratch_shapes=scratch(n_keys, rows, 5)
        + [pltpu.VMEM((n_keys * rows, width), f32)]
        + [pltpu.VMEM((8, width), f32)] * 3,
        compiler_params=pltpu.CompilerParams(vmem_limit_bytes=BIG),
        cost_estimate=cost(n_keys, rows, 2),
    )(order, where, own, far, side, both, packed)


def attention_grads(order, where, own, far, side, both, packed, stats):
    n_keys, rows, _ = packed.shape
    width = GROUP * rows
    shape = (rows, 2 * GROUP * DH)
    return pl.pallas_call(
        grads_kernel,
        out_shape=(
            jax.ShapeDtypeStruct(shape, f32),
            jax.ShapeDtypeStruct(shape, f32),
            jax.ShapeDtypeStruct((2,) + shape, bf16),
            jax.ShapeDtypeStruct((n_keys, rows, 2 * DH), bf16),
        ),
        in_specs=[SMEM] * 2 + [ANY] * 9,
        out_specs=(ANY,) * 4,
        scratch_shapes=scratch(n_keys, rows, 9)
        + [
            pltpu.VMEM((4, 3, 8, width), f32),
            pltpu.VMEM((2,) + shape, f32),
            pltpu.VMEM((2,) + shape, bf16),
            pltpu.VMEM((n_keys, rows, 2 * DH), bf16),
            pltpu.SemaphoreType.DMA((5,)),
        ]
        + [pltpu.VMEM((n_keys * rows, DH), f32)] * 2
        + [pltpu.VMEM((DH, width), f32)],
        compiler_params=pltpu.CompilerParams(vmem_limit_bytes=BIG),
        cost_estimate=cost(n_keys, rows, 5),
    )(order, where, own, far, side, both, packed, *stats)


def pack_kernel(*refs):
    *heads, key_rows, value_rows, own, packed, sems = refs
    pairs = []
    for j in range(packed.shape[0]):
        for i, ref in enumerate((key_rows, value_rows)):
            pairs.append((ref, packed.at[j, :, i * DH:(i + 1) * DH]))
    wide = heads[0].shape[1]
    for i, ref in enumerate(heads):
        pairs.append((ref, own.at[:, i * wide:(i + 1) * wide]))
    for copy in fetch(pairs, sems):
        copy.wait()


def pack(heads, key_rows, value_rows, count):
    rows = key_rows.shape[0]
    return pl.pallas_call(
        pack_kernel,
        in_specs=[ANY] * (len(heads) + 2),
        out_specs=(VMEM,) * 2,
        out_shape=(
            jax.ShapeDtypeStruct((rows, len(heads) * heads[0].shape[1]), bf16),
            jax.ShapeDtypeStruct((count, rows, 2 * DH), bf16),
        ),
        scratch_shapes=[pltpu.SemaphoreType.DMA((2 * count + len(heads),))],
        compiler_params=pltpu.CompilerParams(vmem_limit_bytes=BIG),
    )(*heads, key_rows, value_rows)


def cut_kernel(at, x, *refs):
    *cuts, sems = refs
    count, _, wide = cuts[0].shape
    xh, core = at[0], at[1]
    pairs = []
    for i, cut in enumerate(cuts):
        lead = (xh ^ (i & 1)) * (2 * count) + (core ^ (i >> 1))
        for j in range(count):
            columns = pl.ds(pl.multiple_of((lead + 2 * j) * wide, wide), wide)
            pairs.append((x.at[:, columns], cut.at[j]))
    for copy in fetch(pairs, sems):
        copy.wait()


def cut_input(at, x, count):
    cut = jax.ShapeDtypeStruct((count, x.shape[0], x.shape[1] // (4 * count)), bf16)
    return pl.pallas_call(
        cut_kernel,
        in_specs=[SMEM, ANY],
        out_specs=(VMEM,) * 4,
        out_shape=(cut,) * 4,
        scratch_shapes=[pltpu.SemaphoreType.DMA((4 * count,))],
        compiler_params=pltpu.CompilerParams(vmem_limit_bytes=BIG),
    )(at, x)


def key_sum_kernel(parts, grad):
    total = parts[0].astype(f32)
    for i in range(1, parts.shape[0]):
        total += parts[i].astype(f32)
    grad[...] = total.astype(bf16)


def key_sum(parts):
    return pl.pallas_call(
        key_sum_kernel,
        out_shape=jax.ShapeDtypeStruct(parts.shape[1:], bf16),
        in_specs=[VMEM],
        out_specs=VMEM,
        compiler_params=pltpu.CompilerParams(vmem_limit_bytes=SMALL),
    )(parts)


def input_terms_kernel(grad, key_weight, value_weight, out, k_held, v_held, terms, sems, out_sems):
    columns = out.shape[2]
    n = out.shape[0]
    spans = [pl.ds(j * columns, columns) for j in range(n)]
    k_in = fetch([(key_weight.at[p], k_held.at[p]) for p in spans], sems.at[0])
    v_in = fetch([(value_weight.at[p], v_held.at[p]) for p in spans], sems.at[1])
    outs = []
    for j in range(n):
        k_in[j].wait()
        v_in[j].wait()
        t = lax.dot_general(grad[:, :DH], k_held[spans[j], :], NT, preferred_element_type=f32)
        t += lax.dot_general(grad[:, DH:], v_held[spans[j], :], NT, preferred_element_type=f32)
        terms[j] = t.astype(bf16)
        copy = pltpu.make_async_copy(terms.at[j], out.at[j], out_sems.at[j])
        copy.start()
        outs.append(copy)
    for copy in outs:
        copy.wait()


def input_terms(grad, key_weight, value_weight, heads):
    rows = grad.shape[0]
    shape = (heads, rows, key_weight.shape[0] // heads)
    return pl.pallas_call(
        input_terms_kernel,
        out_shape=jax.ShapeDtypeStruct(shape, bf16),
        in_specs=[VMEM, ANY, ANY],
        out_specs=ANY,
        scratch_shapes=[
            pltpu.VMEM(key_weight.shape, bf16),
            pltpu.VMEM(key_weight.shape, bf16),
            pltpu.VMEM(shape, bf16),
            pltpu.SemaphoreType.DMA((2, heads)),
            pltpu.SemaphoreType.DMA((heads,)),
        ],
        compiler_params=pltpu.CompilerParams(vmem_limit_bytes=BIG),
        cost_estimate=pl.CostEstimate(
            flops=4 * rows * DH * key_weight.shape[0], bytes_accessed=6 * 2**20, transcendentals=0
        ),
    )(grad, key_weight, value_weight)


def weight_terms_kernel(at, g0, g1, g2, g3, x0, x1, x2, x3, *refs):
    *outs, held, turned, sems = refs
    z = at[0]
    copies = fetch([(x, held.at[i]) for i, x in enumerate((x0, x1, x2, x3))], sems)
    rows = g0.shape[0]
    for i, g in enumerate((g0, g1, g2, g3)):
        turned[:, i * rows:(i + 1) * rows] = g[...].T
    for copy in copies:
        copy.wait()
    n_z = len(outs)
    for k in reversed(range(n_z)):
        to = lax.rem(z + k, n_z)
        terms = jnp.dot(turned[:, :rows], held[0, to], preferred_element_type=f32)
        for i in range(1, 4):
            terms += jnp.dot(
                turned[:, i * rows:(i + 1) * rows], held[i, to], preferred_element_type=f32
            )
        outs[k][...] = terms.astype(outs[k].dtype)


def weight_terms(at, grads, cuts):
    rows, columns = grads[0].shape
    n_z = cuts[0].shape[0]
    shape = (columns, cuts[0].shape[2])
    return pl.pallas_call(
        weight_terms_kernel,
        out_shape=[jax.ShapeDtypeStruct(shape, bf16 if k else f32) for k in range(n_z)],
        in_specs=[SMEM] + [VMEM] * 4 + [ANY] * 4,
        out_specs=[VMEM] * n_z,
        scratch_shapes=[
            pltpu.VMEM((4,) + cuts[0].shape, bf16),
            pltpu.VMEM((columns, 4 * rows), bf16),
            pltpu.SemaphoreType.DMA((4,)),
        ],
        compiler_params=pltpu.CompilerParams(vmem_limit_bytes=MIDDLE),
        cost_estimate=pl.CostEstimate(
            flops=8 * rows * n_z * shape[0] * shape[1], bytes_accessed=4 * 2**20, transcendentals=0
        ),
    )(at, *grads, *cuts)


def weight_sum_kernel(*refs):
    *parts, key_out, value_out = refs
    total = parts[0][...]
    for part in parts[1:]:
        total += part[...].astype(f32)
    key_out[...] = total[:DH, :].T
    value_out[...] = total[DH:, :].T


def weight_sum(parts):
    shape = jax.ShapeDtypeStruct((parts[0].shape[1], DH), f32)
    return pl.pallas_call(
        weight_sum_kernel,
        out_shape=(shape, shape),
        in_specs=[VMEM] * len(parts),
        out_specs=(VMEM, VMEM),
        compiler_params=pltpu.CompilerParams(vmem_limit_bytes=SMALL),
    )(*parts)


def swap(x, axis):
    return lax.ppermute(x, axis, [(0, 1), (1, 0)])


def cross(x):
    return lax.ppermute(x, ("xh", "core"), [(0, 3), (1, 2), (2, 1), (3, 0)])


def on_device(
    queries_one, grads_one, queries_two, grads_two, key_rows, value_rows,
    shared_input, key_weight, value_weight, block_order,
):
    rows, width = shared_input.shape
    n_xh, n_z, n_core, n_xl, n_y = (lax.axis_size(a) for a in CTX + HEAD)
    heads = n_xl * n_y
    core, xh, z = lax.axis_index("core"), lax.axis_index("xh"), lax.axis_index("z")
    head = lax.axis_index(HEAD)

    def slot(h, at, c):
        return 2 * ((h * n_z + at) * n_core + c)

    where = jnp.stack(
        [slot(xh, z, core), slot(1 - xh, z, core), slot(xh, z, 1 - core), slot(1 - xh, z, 1 - core)]
        + [slot(xh, b, core) for b in range(n_z)]
    ).astype(jnp.int32)

    at = jnp.stack([xh, core]).astype(jnp.int32)

    with jax.named_scope("gather"):
        own, packed = pack(
            (queries_one, grads_one, queries_two, grads_two), key_rows, value_rows, n_z
        )
        shared_input, own = lax.optimization_barrier((shared_input, own))
        packed = lax.all_to_all(packed, "z", 0, 0)
        far = swap(own, "xh")
        side = swap(own, "core")
        both = swap(far, "core")
        where, packed = lax.optimization_barrier((where, packed))
    with jax.named_scope("spread_input"):
        cuts = cut_input(at, shared_input, n_z)
        far, *cuts = lax.optimization_barrier((far, *cuts))
        cuts = [cuts[0], swap(cuts[1], "xh"), swap(cuts[2], "core"), cross(cuts[3])]

    with jax.named_scope("attention_stats"):
        stats = attention_stats(block_order, where, own, far, side, both, packed)
    with jax.named_scope("share_stats"):
        stats, *cuts = lax.optimization_barrier((stats, *cuts))
        stats = (stats, swap(stats, "xh"), swap(stats, "core"), cross(stats))
    with jax.named_scope("attention_grads"):
        dq_own, dq_far, dq_pair, dkv = attention_grads(
            block_order, where, own, far, side, both, packed, stats
        )
    with jax.named_scope("scatter_grads"):
        dkv = lax.all_to_all(dkv, "z", 0, 0)
    with jax.named_scope("query_grads"):
        dq_pair = swap(dq_pair, "core").astype(f32)
        dq_own = dq_own + dq_pair[0]
        dq_far = swap((dq_far + dq_pair[1]).astype(bf16), "xh")
        dkv, dq_own, dq_far = lax.optimization_barrier((dkv, dq_own, dq_far))
        dq = (dq_own + dq_far.astype(f32)).astype(bf16)
        dq_one, dq_two = dq[:, :GROUP * DH], dq[:, GROUP * DH:]
    with jax.named_scope("scatter_grads"):
        grad = key_sum(dkv)

        grads = [grad, swap(grad, "xh"), swap(grad, "core"), cross(grad)]

        grads = [grad, swap(grad, "xh"), swap(grad, "core"), cross(grad)]

    with jax.named_scope("input_grad"):
        terms = input_terms(grad, key_weight, value_weight, heads)
        terms, *grads = lax.optimization_barrier((terms, *grads))
        terms = lax.all_to_all(terms, HEAD, 0, 0)
        input_grad = jnp.sum(terms.astype(f32), axis=0).astype(bf16)

    with jax.named_scope("weight_grad"):
        own, *rest = weight_terms(z.astype(jnp.int32).reshape(1), grads, cuts)
        parts = [own] + [
            lax.ppermute(part, "z", [(i, (i + k) % n_z) for i in range(n_z)])
            for k, part in enumerate(rest, 1)
        ]
        key_weight_grad, value_weight_grad = weight_sum(parts)
    return (dq_one, dq_two, input_grad, key_weight_grad, value_weight_grad)


def solution(mesh):
    fine = Mesh(mesh.devices.reshape(2, 8, 2, 2, 4), CTX + HEAD)
    both = P(CTX, HEAD)
    return jax.shard_map(
        on_device,
        mesh=fine,
        in_specs=(both,) * 6 + (P(CTX, None), P(None, HEAD), P(None, HEAD), P()),
        out_specs=(both,) * 5,
        check_vma=False,
    )
```

```python
import functools
import math

import jax
import jax.numpy as jnp
from jax import lax
from jax.experimental import pallas as pl
from jax.experimental.pallas import tpu as pltpu
from jax.sharding import Mesh
from jax.sharding import PartitionSpec as P

H = 32
KV = 8
DH = 128
GROUP = H // KV
CTX = ("xh", "z", "core")
HEAD = ("xl", "y")
NT = (((1,), (1,)), ((), ()))
TN = (((0,), (0,)), ((), ()))
f32 = jnp.float32
bf16 = jnp.bfloat16
SCALE = 1.0 / math.sqrt(DH)
TO_LOG2 = SCALE * math.log2(math.e)
LOWEST = -1e30
BIG = 56 * 2**20
SMALL = 8 * 2**20
VMEM = pl.BlockSpec(memory_space=pltpu.VMEM)
SMEM = pl.BlockSpec(memory_space=pltpu.SMEM)
ANY = pl.BlockSpec(memory_space=pl.ANY)


class Plan:
    def __init__(self, order, where, n_keys, half):
        self.half = half
        self.n_keys = n_keys
        self.order, self.where = order, where
        self.near = []
        for b in range(n_keys):
            slot = where[4 + b]
            self.near.append(jnp.minimum(order[slot], order[slot + 1]))
        self.rank = []
        for b in range(n_keys):
            r = jnp.int32(0)
            for o in range(n_keys):
                r += jnp.where(self.near[o] < self.near[b], 1, 0)
            self.rank.append(r)

    def key_rows(self, b, i):
        pos = self.order[self.where[4 + b] + i]
        r = self.rank[b]
        at = jnp.where(pos == self.near[b], r, 2 * self.n_keys - 1 - r)
        return pl.ds(pl.multiple_of(at * self.half, self.half), self.half)

    def limits(self, a, width):
        slot = self.where[a]
        first, second = self.order[slot], self.order[slot + 1]
        mine = jnp.minimum(first, second)
        below, upto = jnp.int32(0), jnp.int32(0)
        for near in self.near:
            below += jnp.where(near < mine, 1, 0)
            upto += jnp.where(near <= mine, 1, 0)
        early, late = upto, 2 * self.n_keys - below
        inside = lax.rem(lax.broadcasted_iota(jnp.int32, (1, width), 1), self.half)
        same = upto > below

        def last(blocks):
            return jnp.where(same, (blocks - 1) * self.half + inside, blocks * self.half - 1)

        return early, late, last(early), last(late)


def load_heads(a, ref, q_all, g_all, order, where, half):
    slot = where[a]
    late_at = jnp.where(order[slot] > order[slot + 1], 0, 1)
    for part, at in ((0, late_at), (1, 1 - late_at)):
        rows = pl.ds(pl.multiple_of(at * half, half), half)
        for layer in range(2):
            for h in range(GROUP):
                r = (layer * GROUP + h) * half
                c = (layer * 2 * GROUP + h) * DH
                q_all[part, r:r + half, :] = ref[rows, c:c + DH]
                c += GROUP * DH
                g_all[part, r:r + half, :] = ref[rows, c:c + DH]


def fetch(pairs, sems):
    copies = [pltpu.make_async_copy(src, dst, sems.at[i]) for i, (src, dst) in enumerate(pairs)]
    for copy in copies:
        copy.start()
    return copies


def sort_keys(plan, kv, k_sorted, v_sorted):
    for b in range(plan.n_keys):
        for i in range(2):
            to = plan.key_rows(b, i)
            rows = slice(i * plan.half, (i + 1) * plan.half)
            k_sorted[to, :] = kv[b, rows, :DH]
            v_sorted[to, :] = kv[b, rows, DH:2 * DH]


def fold(x, op):
    return op(x.reshape(x.shape[0] // 8, 8, x.shape[1]), axis=0)


def tiles(seen, n_keys, half, part):
    step = n_keys * half // 2
    if part == 0:
        return (
            (0, 2 * step, None, False),
            (2 * step, step, seen > n_keys, True),
            (3 * step, step, seen > n_keys + n_keys // 2, True),
        )
    return ((0, step, seen > 0, True), (step, step, seen > n_keys // 2, True))


def under(condition, body):
    if condition is None:
        body()
    else:
        pl.when(condition)(body)


def masked_scores(k, q, start, last, masked):
    s = lax.dot_general(k, q, NT, preferred_element_type=f32)
    if masked:
        key = start + lax.broadcasted_iota(jnp.int32, s.shape, 0)
        s = jnp.where(key <= last, s, -jnp.inf)
    return s


def stats_kernel(
    order, where, own, far, side, both, kv, stats, k_out, v_out, q_out, g_out, held, k_sorted, v_sorted, q_all, g_all,
    sems, out_sems, scores, peak, total, delta,
):
    half = own.shape[0] // 2
    n_keys = kv.shape[0]
    width = q_all.shape[2]
    copies = fetch([(ref, held.at[a]) for a, ref in enumerate((own, far, side, both))], sems)
    plan = Plan(order, where, n_keys, half)
    sort_keys(plan, kv, k_sorted, v_sorted)
    sent = fetch([(k_sorted, k_out), (v_sorted, v_out)], out_sems.at[0])
    for a in range(4):
        copies[a].wait()
        load_heads(a, held.at[a], q_all.at[a], g_all.at[a], order, where, half)
        sent += fetch([(q_all.at[a], q_out.at[a]), (g_all.at[a], g_out.at[a])], out_sems.at[1 + a])
        early, late, last_early, last_late = plan.limits(a, width)
        for part, seen, last in ((0, late, last_late), (1, early, last_early)):
            q, g = q_all[a, part], g_all[a, part]
            peak[...] = jnp.full(peak.shape, LOWEST, f32)
            for start, size, condition, masked in tiles(seen, n_keys, half, part):

                def score():
                    s = masked_scores(k_sorted[start:start + size, :], q, start, last, masked)
                    scores[start:start + size, :] = s
                    peak[...] = jnp.maximum(peak[...], fold(s, jnp.max))

                under(condition, score)
            top = jnp.max(peak[...], axis=0, keepdims=True) * TO_LOG2
            total[...] = jnp.zeros(total.shape, f32)
            delta[...] = jnp.zeros(delta.shape, f32)
            for start, size, condition, masked in tiles(seen, n_keys, half, part):

                def weigh():
                    e = jnp.exp2(scores[start:start + size, :] * TO_LOG2 - top)
                    d = lax.dot_general(
                        v_sorted[start:start + size, :], g, NT, preferred_element_type=f32
                    )
                    total[...] += fold(e, jnp.sum)
                    delta[...] += fold(e * d, jnp.sum)

                under(condition, weigh)
            row = 2 * a + part
            stats[0, row:row + 1, :] = top
            stats[1, row:row + 1, :] = jnp.sum(total[...], axis=0, keepdims=True)
            stats[2, row:row + 1, :] = jnp.sum(delta[...], axis=0, keepdims=True)
    for copy in sent:
        copy.wait()


def grads_kernel(
    order, where, keys, values, queries, grads, s_own, s_far, s_side, s_both, dq_own, dq_far, dq_pair, dkv,
    k_sorted, v_sorted, q_all, g_all, sems, s_held, out_mine, out_pair, out_kv, out_sems, dk, dv, dq,
):
    n_keys, half = dkv.shape[0], dkv.shape[1] // 2
    width = q_all.shape[2]
    copies = fetch([(keys, k_sorted), (values, v_sorted)], sems.at[0])
    parts = [
        fetch([(queries.at[a], q_all.at[a]), (grads.at[a], g_all.at[a])], sems.at[1 + a]) for a in range(4)
    ]
    copies += fetch([(ref, s_held.at[a]) for a, ref in enumerate((s_own, s_far, s_side, s_both))], sems.at[5])
    plan = Plan(order, where, n_keys, half)
    dk[...] = jnp.zeros(dk.shape, f32)
    dv[...] = jnp.zeros(dv.shape, f32)
    for copy in copies:
        copy.wait()
    sent = []
    for a, out in enumerate((dq_own, dq_far, dq_pair.at[0], dq_pair.at[1])):
        dq_out = out_pair.at[a - 2] if a > 1 else out_mine.at[a]
        for copy in parts[a]:
            copy.wait()
        early, late, last_early, last_late = plan.limits(a, width)
        slot = where[a]
        late_at = jnp.where(order[slot] > order[slot + 1], 0, 1)
        for part, seen, last, at in ((0, late, last_late, late_at), (1, early, last_early, 1 - late_at)):
            q, g = q_all[a, part], g_all[a, part]
            shares = []
            for flip in range(4):
                r = 2 * (a ^ flip) + part
                shares.append(tuple(s_held[flip, j, r:r + 1, :] for j in range(3)))
            top = functools.reduce(jnp.maximum, (t for t, _, _ in shares))
            total = sum(n * jnp.exp2(t - top) for t, n, _ in shares)
            delta = sum(d * jnp.exp2(t - top) for t, _, d in shares) / total
            base = top + jnp.log2(total)
            dq[...] = jnp.zeros(dq.shape, f32)
            for start, size, condition, masked in tiles(seen, n_keys, half, part):

                def step():
                    span = slice(start, start + size)
                    k = k_sorted[span, :]
                    s = masked_scores(k, q, start, last, masked)
                    p = jnp.exp2(s * TO_LOG2 - base)
                    d = lax.dot_general(v_sorted[span, :], g, NT, preferred_element_type=f32)
                    ds = (p * (d - delta)).astype(bf16)
                    dv[span, :] += jnp.dot(p.astype(bf16), g, preferred_element_type=f32)
                    dk[span, :] += jnp.dot(ds, q, preferred_element_type=f32)
                    dq[...] += lax.dot_general(k, ds, TN, preferred_element_type=f32)

                under(condition, step)
            turned = (dq[...] * SCALE).T.astype(dq_out.dtype)
            rows = pl.ds(pl.multiple_of(at * half, half), half)
            for j in range(2 * GROUP):
                dq_out[rows, j * DH:(j + 1) * DH] = turned[j * half:(j + 1) * half, :]
        copy = pltpu.make_async_copy(dq_out, out, out_sems.at[a])
        copy.start()
        sent.append(copy)
    for b in range(n_keys):
        for i in range(2):
            of = plan.key_rows(b, i)
            rows = slice(i * half, (i + 1) * half)
            out_kv[b, rows, :DH] = (dk[of, :] * SCALE).astype(bf16)
            out_kv[b, rows, DH:] = dv[of, :].astype(bf16)
    copy = pltpu.make_async_copy(out_kv, dkv, out_sems.at[4])
    copy.start()
    for copy in sent + [copy]:
        copy.wait()


def scratch(n_keys, rows):
    width = GROUP * rows
    return [
        pltpu.VMEM((n_keys * rows, DH), bf16),
        pltpu.VMEM((n_keys * rows, DH), bf16),
        pltpu.VMEM((4, 2, width, DH), bf16),
        pltpu.VMEM((4, 2, width, DH), bf16),
    ]


def cost(n_keys, rows, products):
    pairs = 4 * GROUP * rows * n_keys * rows
    return pl.CostEstimate(
        flops=2 * products * pairs * DH, bytes_accessed=8 * 2**20, transcendentals=pairs
    )


def attention_stats(order, where, own, far, side, both, kv):
    n_keys, rows, _ = kv.shape
    width = GROUP * rows
    keys = jax.ShapeDtypeStruct((n_keys * rows, DH), bf16)
    heads = jax.ShapeDtypeStruct((4, 2, width, DH), bf16)
    return pl.pallas_call(
        stats_kernel,
        out_shape=(jax.ShapeDtypeStruct((3, 8, width), f32), keys, keys, heads, heads),
        in_specs=[SMEM] * 2 + [ANY] * 4 + [VMEM],
        out_specs=(VMEM,) + (ANY,) * 4,
        scratch_shapes=[pltpu.VMEM((4,) + own.shape, bf16)]
        + scratch(n_keys, rows)
        + [pltpu.SemaphoreType.DMA((4,)), pltpu.SemaphoreType.DMA((5, 2))]
        + [pltpu.VMEM((n_keys * rows, width), f32)]
        + [pltpu.VMEM((8, width), f32)] * 3,
        compiler_params=pltpu.CompilerParams(vmem_limit_bytes=BIG),
        cost_estimate=cost(n_keys, rows, 2),
    )(order, where, own, far, side, both, kv)


def attention_grads(order, where, keys, values, queries, grads, stats, n_keys):
    rows = keys.shape[0] // n_keys
    width = GROUP * rows
    shape = (rows, 2 * GROUP * DH)
    return pl.pallas_call(
        grads_kernel,
        out_shape=(
            jax.ShapeDtypeStruct(shape, f32),
            jax.ShapeDtypeStruct(shape, f32),
            jax.ShapeDtypeStruct((2,) + shape, bf16),
            jax.ShapeDtypeStruct((n_keys, rows, 2 * DH), bf16),
        ),
        in_specs=[SMEM] * 2 + [ANY] * 8,
        out_specs=(ANY,) * 4,
        scratch_shapes=scratch(n_keys, rows)
        + [
            pltpu.SemaphoreType.DMA((6, 4)),
            pltpu.VMEM((4, 3, 8, width), f32),
            pltpu.VMEM((2,) + shape, f32),
            pltpu.VMEM((2,) + shape, bf16),
            pltpu.VMEM((n_keys, rows, 2 * DH), bf16),
            pltpu.SemaphoreType.DMA((5,)),
        ]
        + [pltpu.VMEM((n_keys * rows, DH), f32)] * 2
        + [pltpu.VMEM((DH, width), f32)],
        compiler_params=pltpu.CompilerParams(vmem_limit_bytes=BIG),
        cost_estimate=cost(n_keys, rows, 5),
    )(order, where, keys, values, queries, grads, *stats)


def pack_kernel(*refs):
    *heads, key_rows, value_rows, own, packed, sems = refs
    pairs = []
    for j in range(packed.shape[0]):
        for i, ref in enumerate((key_rows, value_rows)):
            pairs.append((ref, packed.at[j, :, i * DH:(i + 1) * DH]))
    wide = heads[0].shape[1]
    for i, ref in enumerate(heads):
        pairs.append((ref, own.at[:, i * wide:(i + 1) * wide]))
    for copy in fetch(pairs, sems):
        copy.wait()


def pack(heads, key_rows, value_rows, count):
    rows = key_rows.shape[0]
    return pl.pallas_call(
        pack_kernel,
        in_specs=[ANY] * (len(heads) + 2),
        out_specs=(VMEM,) * 2,
        out_shape=(
            jax.ShapeDtypeStruct((rows, len(heads) * heads[0].shape[1]), bf16),
            jax.ShapeDtypeStruct((count, rows, 2 * DH), bf16),
        ),
        scratch_shapes=[pltpu.SemaphoreType.DMA((2 * count + len(heads),))],
        compiler_params=pltpu.CompilerParams(vmem_limit_bytes=BIG),
    )(*heads, key_rows, value_rows)


def cut_kernel(at, x, *refs):
    *cuts, sems = refs
    count, _, wide = cuts[0].shape
    xh, core = at[0], at[1]
    pairs = []
    for i, cut in enumerate(cuts):
        lead = (xh ^ (i & 1)) * (2 * count) + (core ^ (i >> 1))
        for j in range(count):
            columns = pl.ds(pl.multiple_of((lead + 2 * j) * wide, wide), wide)
            pairs.append((x.at[:, columns], cut.at[j]))
    for copy in fetch(pairs, sems):
        copy.wait()


def cut_input(at, x, count):
    cut = jax.ShapeDtypeStruct((count, x.shape[0], x.shape[1] // (4 * count)), bf16)
    return pl.pallas_call(
        cut_kernel,
        in_specs=[SMEM, ANY],
        out_specs=(VMEM,) * 4,
        out_shape=(cut,) * 4,
        scratch_shapes=[pltpu.SemaphoreType.DMA((4 * count,))],
        compiler_params=pltpu.CompilerParams(vmem_limit_bytes=BIG),
    )(at, x)


def part_sum_kernel(parts, grad):
    total = parts[0].astype(f32)
    for i in range(1, parts.shape[0]):
        total += parts[i].astype(f32)
    grad[...] = total.astype(bf16)


def part_sum(parts):
    return pl.pallas_call(
        part_sum_kernel,
        out_shape=jax.ShapeDtypeStruct(parts.shape[1:], bf16),
        in_specs=[VMEM],
        out_specs=VMEM,
        compiler_params=pltpu.CompilerParams(vmem_limit_bytes=SMALL),
    )(parts)


def input_terms_kernel(grad, key_weight, value_weight, out, k_held, v_held, terms, sems, out_sems):
    columns = out.shape[2]
    n = out.shape[0]
    spans = [pl.ds(j * columns, columns) for j in range(n)]
    k_in = fetch([(key_weight.at[p], k_held.at[p]) for p in spans], sems.at[0])
    v_in = fetch([(value_weight.at[p], v_held.at[p]) for p in spans], sems.at[1])
    outs = []
    for j in range(n):
        k_in[j].wait()
        v_in[j].wait()
        t = lax.dot_general(grad[:, :DH], k_held[spans[j], :], NT, preferred_element_type=f32)
        t += lax.dot_general(grad[:, DH:], v_held[spans[j], :], NT, preferred_element_type=f32)
        terms[j] = t.astype(bf16)
        copy = pltpu.make_async_copy(terms.at[j], out.at[j], out_sems.at[j])
        copy.start()
        outs.append(copy)
    for copy in outs:
        copy.wait()


def input_terms(grad, key_weight, value_weight, heads):
    rows = grad.shape[0]
    shape = (heads, rows, key_weight.shape[0] // heads)
    return pl.pallas_call(
        input_terms_kernel,
        out_shape=jax.ShapeDtypeStruct(shape, bf16),
        in_specs=[VMEM, ANY, ANY],
        out_specs=ANY,
        scratch_shapes=[
            pltpu.VMEM(key_weight.shape, bf16),
            pltpu.VMEM(key_weight.shape, bf16),
            pltpu.VMEM(shape, bf16),
            pltpu.SemaphoreType.DMA((2, heads)),
            pltpu.SemaphoreType.DMA((heads,)),
        ],
        compiler_params=pltpu.CompilerParams(vmem_limit_bytes=BIG),
        cost_estimate=pl.CostEstimate(
            flops=4 * rows * DH * key_weight.shape[0], bytes_accessed=6 * 2**20, transcendentals=0
        ),
    )(grad, key_weight, value_weight)


def weight_terms_kernel(at, g0, g1, g2, g3, x0, x1, x2, x3, *refs):
    *outs, held, turned, sems = refs
    z = at[0]
    copies = fetch([(x, held.at[i]) for i, x in enumerate((x0, x1, x2, x3))], sems)
    rows = g0.shape[0]
    for i, g in enumerate((g0, g1, g2, g3)):
        turned[:, i * rows:(i + 1) * rows] = g[...].T
    for copy in copies:
        copy.wait()
    n_z = len(outs)
    for k in reversed(range(n_z)):
        to = lax.rem(z + k, n_z)
        terms = jnp.dot(turned[:, :rows], held[0, to], preferred_element_type=f32)
        for i in range(1, 4):
            terms += jnp.dot(
                turned[:, i * rows:(i + 1) * rows], held[i, to], preferred_element_type=f32
            )
        outs[k][...] = terms.astype(outs[k].dtype)


def weight_terms(at, grads, cuts):
    rows, columns = grads[0].shape
    n_z = cuts[0].shape[0]
    shape = (columns, cuts[0].shape[2])
    return pl.pallas_call(
        weight_terms_kernel,
        out_shape=[jax.ShapeDtypeStruct(shape, bf16 if k else f32) for k in range(n_z)],
        in_specs=[SMEM] + [VMEM] * 4 + [ANY] * 4,
        out_specs=[VMEM] * n_z,
        scratch_shapes=[
            pltpu.VMEM((4,) + cuts[0].shape, bf16),
            pltpu.VMEM((columns, 4 * rows), bf16),
            pltpu.SemaphoreType.DMA((4,)),
        ],
        compiler_params=pltpu.CompilerParams(vmem_limit_bytes=BIG),
        cost_estimate=pl.CostEstimate(
            flops=8 * rows * n_z * shape[0] * shape[1], bytes_accessed=4 * 2**20, transcendentals=0
        ),
    )(at, *grads, *cuts)


def weight_sum_kernel(*refs):
    *parts, key_out, value_out = refs
    total = parts[0][...]
    for part in parts[1:]:
        total += part[...].astype(f32)
    key_out[...] = total[:DH, :].T
    value_out[...] = total[DH:, :].T


def weight_sum(parts):
    shape = jax.ShapeDtypeStruct((parts[0].shape[1], DH), f32)
    return pl.pallas_call(
        weight_sum_kernel,
        out_shape=(shape, shape),
        in_specs=[VMEM] * len(parts),
        out_specs=(VMEM, VMEM),
        compiler_params=pltpu.CompilerParams(vmem_limit_bytes=SMALL),
    )(*parts)


def swap(x, axis):
    return lax.ppermute(x, axis, [(0, 1), (1, 0)])


def cross(x):
    return lax.ppermute(x, ("xh", "core"), [(0, 3), (1, 2), (2, 1), (3, 0)])


def on_device(
    queries_one, grads_one, queries_two, grads_two, key_rows, value_rows,
    shared_input, key_weight, value_weight, block_order,
):
    rows, width = shared_input.shape
    n_xh, n_z, n_core, n_xl, n_y = (lax.axis_size(a) for a in CTX + HEAD)
    heads = n_xl * n_y
    core, xh, z = lax.axis_index("core"), lax.axis_index("xh"), lax.axis_index("z")
    head = lax.axis_index(HEAD)

    def slot(h, at, c):
        return 2 * ((h * n_z + at) * n_core + c)

    where = jnp.stack(
        [slot(xh, z, core), slot(1 - xh, z, core), slot(xh, z, 1 - core), slot(1 - xh, z, 1 - core)]
        + [slot(xh, b, core) for b in range(n_z)]
    ).astype(jnp.int32)

    at = jnp.stack([xh, core]).astype(jnp.int32)

    with jax.named_scope("gather"):
        own, packed = pack(
            (queries_one, grads_one, queries_two, grads_two), key_rows, value_rows, n_z
        )
        shared_input, own = lax.optimization_barrier((shared_input, own))
        packed = lax.all_to_all(packed, "z", 0, 0)
        far = swap(own, "xh")
        side = swap(own, "core")
        where, packed = lax.optimization_barrier((where, packed))
    with jax.named_scope("spread_input"):
        cuts = cut_input(at, shared_input, n_z)
        far, *cuts = lax.optimization_barrier((far, *cuts))
        both = swap(far, "core")
        cuts = [cuts[0], swap(cuts[1], "xh"), swap(cuts[2], "core"), cross(cuts[3])]

    with jax.named_scope("attention_stats"):
        stats, *sorted_rows = attention_stats(block_order, where, own, far, side, both, packed)
    with jax.named_scope("share_stats"):
        stats, *cuts = lax.optimization_barrier((stats, *cuts))
        stats = (stats, swap(stats, "xh"), swap(stats, "core"), cross(stats))
    with jax.named_scope("attention_grads"):
        dq_own, dq_far, dq_pair, dkv = attention_grads(
            block_order, where, *sorted_rows, stats, n_z
        )
    with jax.named_scope("scatter_grads"):
        dkv = lax.all_to_all(dkv, "z", 0, 0)
    with jax.named_scope("query_grads"):
        dq_pair = swap(dq_pair, "core").astype(f32)
        dq_own = dq_own + dq_pair[0]
        dq_far = swap((dq_far + dq_pair[1]).astype(bf16), "xh")
        dkv, dq_own, dq_far = lax.optimization_barrier((dkv, dq_own, dq_far))
        dq = (dq_own + dq_far.astype(f32)).astype(bf16)
        dq_one, dq_two = dq[:, :GROUP * DH], dq[:, GROUP * DH:]
    with jax.named_scope("scatter_grads"):
        grad = part_sum(dkv)

        grads = [grad, swap(grad, "xh"), swap(grad, "core"), cross(grad)]

        grads = [grad, swap(grad, "xh"), swap(grad, "core"), cross(grad)]

    with jax.named_scope("input_grad"):
        terms = input_terms(grad, key_weight, value_weight, heads)
        terms, *grads = lax.optimization_barrier((terms, *grads))
        terms = lax.all_to_all(terms, HEAD, 0, 0)
        input_grad = part_sum(terms)

    with jax.named_scope("weight_grad"):
        own, *rest = weight_terms(z.astype(jnp.int32).reshape(1), grads, cuts)
        own, input_grad = lax.optimization_barrier((own, input_grad))
        parts = [own] + [
            lax.ppermute(part, "z", [(i, (i + k) % n_z) for i in range(n_z)])
            for k, part in enumerate(rest, 1)
        ]
        key_weight_grad, value_weight_grad = weight_sum(parts)
    return (dq_one, dq_two, input_grad, key_weight_grad, value_weight_grad)


def solution(mesh):
    fine = Mesh(mesh.devices.reshape(2, 8, 2, 2, 4), CTX + HEAD)
    both = P(CTX, HEAD)
    return jax.shard_map(
        on_device,
        mesh=fine,
        in_specs=(both,) * 6 + (P(CTX, None), P(None, HEAD), P(None, HEAD), P()),
        out_specs=(both,) * 5,
        check_vma=False,
    )
```

```python
import functools
import math

import jax
import jax.numpy as jnp
from jax import lax
from jax.experimental import pallas as pl
from jax.experimental.pallas import tpu as pltpu
from jax.sharding import Mesh
from jax.sharding import PartitionSpec as P

H = 32
KV = 8
DH = 128
GROUP = H // KV
CTX = ("xh", "z", "core")
HEAD = ("xl", "y")
NT = (((1,), (1,)), ((), ()))
TN = (((0,), (0,)), ((), ()))
f32 = jnp.float32
bf16 = jnp.bfloat16
SCALE = 1.0 / math.sqrt(DH)
TO_LOG2 = SCALE * math.log2(math.e)
LOWEST = -1e30
BIG = 56 * 2**20
SMALL = 8 * 2**20
VMEM = pl.BlockSpec(memory_space=pltpu.VMEM)
SMEM = pl.BlockSpec(memory_space=pltpu.SMEM)
ANY = pl.BlockSpec(memory_space=pl.ANY)


class Plan:
    def __init__(self, order, where, n_keys, half):
        self.half = half
        self.n_keys = n_keys
        self.order, self.where = order, where
        self.near = []
        for b in range(n_keys):
            slot = where[4 + b]
            self.near.append(jnp.minimum(order[slot], order[slot + 1]))
        self.rank = []
        for b in range(n_keys):
            r = jnp.int32(0)
            for o in range(n_keys):
                r += jnp.where(self.near[o] < self.near[b], 1, 0)
            self.rank.append(r)

    def key_rows(self, b, i):
        pos = self.order[self.where[4 + b] + i]
        r = self.rank[b]
        at = jnp.where(pos == self.near[b], r, 2 * self.n_keys - 1 - r)
        return pl.ds(pl.multiple_of(at * self.half, self.half), self.half)

    def limits(self, a, width):
        slot = self.where[a]
        first, second = self.order[slot], self.order[slot + 1]
        mine = jnp.minimum(first, second)
        below, upto = jnp.int32(0), jnp.int32(0)
        for near in self.near:
            below += jnp.where(near < mine, 1, 0)
            upto += jnp.where(near <= mine, 1, 0)
        early, late = upto, 2 * self.n_keys - below
        inside = lax.rem(lax.broadcasted_iota(jnp.int32, (1, width), 1), self.half)
        same = upto > below

        def last(blocks):
            return jnp.where(same, (blocks - 1) * self.half + inside, blocks * self.half - 1)

        return early, late, last(early), last(late)


def load_heads(a, ref, q_all, g_all, order, where, half):
    slot = where[a]
    late_at = jnp.where(order[slot] > order[slot + 1], 0, 1)
    for part, at in ((0, late_at), (1, 1 - late_at)):
        rows = pl.ds(pl.multiple_of(at * half, half), half)
        for layer in range(2):
            for h in range(GROUP):
                r = (layer * GROUP + h) * half
                c = (layer * 2 * GROUP + h) * DH
                q_all[part, r:r + half, :] = ref[rows, c:c + DH]
                c += GROUP * DH
                g_all[part, r:r + half, :] = ref[rows, c:c + DH]


def fetch(pairs, sems):
    copies = [pltpu.make_async_copy(src, dst, sems.at[i]) for i, (src, dst) in enumerate(pairs)]
    for copy in copies:
        copy.start()
    return copies


def sort_keys(plan, kv, k_sorted, v_sorted):
    for b in range(plan.n_keys):
        for i in range(2):
            to = plan.key_rows(b, i)
            rows = slice(i * plan.half, (i + 1) * plan.half)
            k_sorted[to, :] = kv[b, rows, :DH]
            v_sorted[to, :] = kv[b, rows, DH:2 * DH]


def fold(x, op):
    return op(x.reshape(x.shape[0] // 8, 8, x.shape[1]), axis=0)


def tiles(seen, n_keys, half, part):
    step = n_keys * half // 2
    if part == 0:
        return (
            (0, 2 * step, None, False),
            (2 * step, step // 2, (seen > n_keys) & (seen <= n_keys + n_keys // 4), True),
            (2 * step, step, seen > n_keys + n_keys // 4, True),
            (3 * step, step // 2, (seen > n_keys + n_keys // 2) & (seen <= n_keys + 3 * n_keys // 4), True),
            (3 * step, step, seen > n_keys + 3 * n_keys // 4, True),
        )
    return (
        (0, step // 2, (seen > 0) & (seen <= n_keys // 4), True),
        (0, step, seen > n_keys // 4, True),
        (step, step // 2, (seen > n_keys // 2) & (seen <= 3 * n_keys // 4), True),
        (step, step, seen > 3 * n_keys // 4, True),
    )


def under(condition, body):
    if condition is None:
        body()
    else:
        pl.when(condition)(body)


def masked_scores(k, q, start, last, masked):
    s = lax.dot_general(k, q, NT, preferred_element_type=f32)
    if masked:
        key = start + lax.broadcasted_iota(jnp.int32, s.shape, 0)
        s = jnp.where(key <= last, s, -jnp.inf)
    return s


def stats_kernel(
    order, where, own, far, side, both, kv, stats, k_out, v_out, q_out, g_out, held, k_sorted, v_sorted, q_all, g_all,
    sems, out_sems, scores, peak, total, delta,
):
    half = own.shape[0] // 2
    n_keys = kv.shape[0]
    width = q_all.shape[2]
    copies = fetch([(ref, held.at[a]) for a, ref in enumerate((own, far, side, both))], sems)
    plan = Plan(order, where, n_keys, half)
    sort_keys(plan, kv, k_sorted, v_sorted)
    sent = fetch([(k_sorted, k_out), (v_sorted, v_out)], out_sems.at[0])
    for a in range(4):
        copies[a].wait()
        load_heads(a, held.at[a], q_all.at[a], g_all.at[a], order, where, half)
        sent += fetch([(q_all.at[a], q_out.at[a]), (g_all.at[a], g_out.at[a])], out_sems.at[1 + a])
        early, late, last_early, last_late = plan.limits(a, width)
        for part, seen, last in ((0, late, last_late), (1, early, last_early)):
            q, g = q_all[a, part], g_all[a, part]
            peak[...] = jnp.full(peak.shape, LOWEST, f32)
            for start, size, condition, masked in tiles(seen, n_keys, half, part):

                def score():
                    s = masked_scores(k_sorted[start:start + size, :], q, start, last, masked)
                    scores[start:start + size, :] = s
                    peak[...] = jnp.maximum(peak[...], fold(s, jnp.max))

                under(condition, score)
            top = jnp.max(peak[...], axis=0, keepdims=True) * TO_LOG2
            total[...] = jnp.zeros(total.shape, f32)
            delta[...] = jnp.zeros(delta.shape, f32)
            for start, size, condition, masked in tiles(seen, n_keys, half, part):

                def weigh():
                    e = jnp.exp2(scores[start:start + size, :] * TO_LOG2 - top)
                    d = lax.dot_general(
                        v_sorted[start:start + size, :], g, NT, preferred_element_type=f32
                    )
                    total[...] += fold(e, jnp.sum)
                    delta[...] += fold(e * d, jnp.sum)

                under(condition, weigh)
            row = 2 * a + part
            stats[0, row:row + 1, :] = top
            stats[1, row:row + 1, :] = jnp.sum(total[...], axis=0, keepdims=True)
            stats[2, row:row + 1, :] = jnp.sum(delta[...], axis=0, keepdims=True)
    for copy in sent:
        copy.wait()


def grads_kernel(
    order, where, keys, values, queries, grads, s_own, s_far, s_side, s_both, dq_own, dq_far, dq_pair, dkv,
    k_sorted, v_sorted, q_all, g_all, sems, s_held, out_mine, out_pair, out_kv, out_sems, dk, dv, dq,
):
    n_keys, half = dkv.shape[0], dkv.shape[1] // 2
    width = q_all.shape[2]
    copies = fetch([(keys, k_sorted), (values, v_sorted)], sems.at[0])
    parts = [
        fetch([(queries.at[a], q_all.at[a]), (grads.at[a], g_all.at[a])], sems.at[1 + a]) for a in range(4)
    ]
    copies += fetch([(ref, s_held.at[a]) for a, ref in enumerate((s_own, s_far, s_side, s_both))], sems.at[5])
    plan = Plan(order, where, n_keys, half)
    dk[...] = jnp.zeros(dk.shape, f32)
    dv[...] = jnp.zeros(dv.shape, f32)
    for copy in copies:
        copy.wait()
    sent = []
    for a, out in enumerate((dq_own, dq_far, dq_pair.at[0], dq_pair.at[1])):
        dq_out = out_pair.at[a - 2] if a > 1 else out_mine.at[a]
        for copy in parts[a]:
            copy.wait()
        early, late, last_early, last_late = plan.limits(a, width)
        slot = where[a]
        late_at = jnp.where(order[slot] > order[slot + 1], 0, 1)
        for part, seen, last, at in ((0, late, last_late, late_at), (1, early, last_early, 1 - late_at)):
            q, g = q_all[a, part], g_all[a, part]
            shares = []
            for flip in range(4):
                r = 2 * (a ^ flip) + part
                shares.append(tuple(s_held[flip, j, r:r + 1, :] for j in range(3)))
            top = functools.reduce(jnp.maximum, (t for t, _, _ in shares))
            total = sum(n * jnp.exp2(t - top) for t, n, _ in shares)
            delta = sum(d * jnp.exp2(t - top) for t, _, d in shares) / total
            base = top + jnp.log2(total)
            dq[...] = jnp.zeros(dq.shape, f32)
            for start, size, condition, masked in tiles(seen, n_keys, half, part):

                def step():
                    span = slice(start, start + size)
                    k = k_sorted[span, :]
                    s = masked_scores(k, q, start, last, masked)
                    p = jnp.exp2(s * TO_LOG2 - base)
                    d = lax.dot_general(v_sorted[span, :], g, NT, preferred_element_type=f32)
                    ds = (p * (d - delta)).astype(bf16)
                    dv[span, :] += jnp.dot(p.astype(bf16), g, preferred_element_type=f32)
                    dk[span, :] += jnp.dot(ds, q, preferred_element_type=f32)
                    dq[...] += lax.dot_general(k, ds, TN, preferred_element_type=f32)

                under(condition, step)
            turned = (dq[...] * SCALE).T.astype(dq_out.dtype)
            rows = pl.ds(pl.multiple_of(at * half, half), half)
            for j in range(2 * GROUP):
                dq_out[rows, j * DH:(j + 1) * DH] = turned[j * half:(j + 1) * half, :]
        copy = pltpu.make_async_copy(dq_out, out, out_sems.at[a])
        copy.start()
        sent.append(copy)
    for b in range(n_keys):
        for i in range(2):
            of = plan.key_rows(b, i)
            rows = slice(i * half, (i + 1) * half)
            out_kv[b, rows, :DH] = (dk[of, :] * SCALE).astype(bf16)
            out_kv[b, rows, DH:] = dv[of, :].astype(bf16)
    copy = pltpu.make_async_copy(out_kv, dkv, out_sems.at[4])
    copy.start()
    for copy in sent + [copy]:
        copy.wait()


def scratch(n_keys, rows):
    width = GROUP * rows
    return [
        pltpu.VMEM((n_keys * rows, DH), bf16),
        pltpu.VMEM((n_keys * rows, DH), bf16),
        pltpu.VMEM((4, 2, width, DH), bf16),
        pltpu.VMEM((4, 2, width, DH), bf16),
    ]


def cost(n_keys, rows, products):
    pairs = 4 * GROUP * rows * n_keys * rows
    return pl.CostEstimate(
        flops=2 * products * pairs * DH, bytes_accessed=8 * 2**20, transcendentals=pairs
    )


def attention_stats(order, where, own, far, side, both, kv):
    n_keys, rows, _ = kv.shape
    width = GROUP * rows
    keys = jax.ShapeDtypeStruct((n_keys * rows, DH), bf16)
    heads = jax.ShapeDtypeStruct((4, 2, width, DH), bf16)
    return pl.pallas_call(
        stats_kernel,
        out_shape=(jax.ShapeDtypeStruct((3, 8, width), f32), keys, keys, heads, heads),
        in_specs=[SMEM] * 2 + [ANY] * 4 + [VMEM],
        out_specs=(VMEM,) + (ANY,) * 4,
        scratch_shapes=[pltpu.VMEM((4,) + own.shape, bf16)]
        + scratch(n_keys, rows)
        + [pltpu.SemaphoreType.DMA((4,)), pltpu.SemaphoreType.DMA((5, 2))]
        + [pltpu.VMEM((n_keys * rows, width), f32)]
        + [pltpu.VMEM((8, width), f32)] * 3,
        compiler_params=pltpu.CompilerParams(vmem_limit_bytes=BIG),
        cost_estimate=cost(n_keys, rows, 2),
    )(order, where, own, far, side, both, kv)


def attention_grads(order, where, keys, values, queries, grads, stats, n_keys):
    rows = keys.shape[0] // n_keys
    width = GROUP * rows
    shape = (rows, 2 * GROUP * DH)
    return pl.pallas_call(
        grads_kernel,
        out_shape=(
            jax.ShapeDtypeStruct(shape, f32),
            jax.ShapeDtypeStruct(shape, f32),
            jax.ShapeDtypeStruct((2,) + shape, bf16),
            jax.ShapeDtypeStruct((n_keys, rows, 2 * DH), bf16),
        ),
        in_specs=[SMEM] * 2 + [ANY] * 8,
        out_specs=(ANY,) * 4,
        scratch_shapes=scratch(n_keys, rows)
        + [
            pltpu.SemaphoreType.DMA((6, 4)),
            pltpu.VMEM((4, 3, 8, width), f32),
            pltpu.VMEM((2,) + shape, f32),
            pltpu.VMEM((2,) + shape, bf16),
            pltpu.VMEM((n_keys, rows, 2 * DH), bf16),
            pltpu.SemaphoreType.DMA((5,)),
        ]
        + [pltpu.VMEM((n_keys * rows, DH), f32)] * 2
        + [pltpu.VMEM((DH, width), f32)],
        compiler_params=pltpu.CompilerParams(vmem_limit_bytes=BIG),
        cost_estimate=cost(n_keys, rows, 5),
    )(order, where, keys, values, queries, grads, *stats)


def pack_kernel(*refs):
    *heads, key_rows, value_rows, own, packed, sems = refs
    pairs = []
    for j in range(packed.shape[0]):
        for i, ref in enumerate((key_rows, value_rows)):
            pairs.append((ref, packed.at[j, :, i * DH:(i + 1) * DH]))
    wide = heads[0].shape[1]
    for i, ref in enumerate(heads):
        pairs.append((ref, own.at[:, i * wide:(i + 1) * wide]))
    for copy in fetch(pairs, sems):
        copy.wait()


def pack(heads, key_rows, value_rows, count):
    rows = key_rows.shape[0]
    return pl.pallas_call(
        pack_kernel,
        in_specs=[ANY] * (len(heads) + 2),
        out_specs=(VMEM,) * 2,
        out_shape=(
            jax.ShapeDtypeStruct((rows, len(heads) * heads[0].shape[1]), bf16),
            jax.ShapeDtypeStruct((count, rows, 2 * DH), bf16),
        ),
        scratch_shapes=[pltpu.SemaphoreType.DMA((2 * count + len(heads),))],
        compiler_params=pltpu.CompilerParams(vmem_limit_bytes=BIG),
    )(*heads, key_rows, value_rows)


def cut_kernel(at, x, *refs):
    *cuts, sems = refs
    count, _, wide = cuts[0].shape
    xh, core = at[0], at[1]
    pairs = []
    for i, cut in enumerate(cuts):
        lead = (xh ^ (i & 1)) * (2 * count) + (core ^ (i >> 1))
        for j in range(count):
            columns = pl.ds(pl.multiple_of((lead + 2 * j) * wide, wide), wide)
            pairs.append((x.at[:, columns], cut.at[j]))
    for copy in fetch(pairs, sems):
        copy.wait()


def cut_input(at, x, count):
    cut = jax.ShapeDtypeStruct((count, x.shape[0], x.shape[1] // (4 * count)), bf16)
    return pl.pallas_call(
        cut_kernel,
        in_specs=[SMEM, ANY],
        out_specs=(VMEM,) * 4,
        out_shape=(cut,) * 4,
        scratch_shapes=[pltpu.SemaphoreType.DMA((4 * count,))],
        compiler_params=pltpu.CompilerParams(vmem_limit_bytes=BIG),
    )(at, x)


def part_sum_kernel(parts, grad):
    total = parts[0].astype(f32)
    for i in range(1, parts.shape[0]):
        total += parts[i].astype(f32)
    grad[...] = total.astype(bf16)


def part_sum(parts):
    return pl.pallas_call(
        part_sum_kernel,
        out_shape=jax.ShapeDtypeStruct(parts.shape[1:], bf16),
        in_specs=[VMEM],
        out_specs=VMEM,
        compiler_params=pltpu.CompilerParams(vmem_limit_bytes=SMALL),
    )(parts)


def input_terms_kernel(grad, key_weight, value_weight, out, k_held, v_held, terms, sems, out_sems):
    columns = out.shape[2]
    n = out.shape[0]
    spans = [pl.ds(j * columns, columns) for j in range(n)]
    k_in = fetch([(key_weight.at[p], k_held.at[p]) for p in spans], sems.at[0])
    v_in = fetch([(value_weight.at[p], v_held.at[p]) for p in spans], sems.at[1])
    outs = []
    for j in range(n):
        k_in[j].wait()
        v_in[j].wait()
        t = lax.dot_general(grad[:, :DH], k_held[spans[j], :], NT, preferred_element_type=f32)
        t += lax.dot_general(grad[:, DH:], v_held[spans[j], :], NT, preferred_element_type=f32)
        terms[j] = t.astype(bf16)
        copy = pltpu.make_async_copy(terms.at[j], out.at[j], out_sems.at[j])
        copy.start()
        outs.append(copy)
    for copy in outs:
        copy.wait()


def input_terms(grad, key_weight, value_weight, heads):
    rows = grad.shape[0]
    shape = (heads, rows, key_weight.shape[0] // heads)
    return pl.pallas_call(
        input_terms_kernel,
        out_shape=jax.ShapeDtypeStruct(shape, bf16),
        in_specs=[VMEM, ANY, ANY],
        out_specs=ANY,
        scratch_shapes=[
            pltpu.VMEM(key_weight.shape, bf16),
            pltpu.VMEM(key_weight.shape, bf16),
            pltpu.VMEM(shape, bf16),
            pltpu.SemaphoreType.DMA((2, heads)),
            pltpu.SemaphoreType.DMA((heads,)),
        ],
        compiler_params=pltpu.CompilerParams(vmem_limit_bytes=BIG),
        cost_estimate=pl.CostEstimate(
            flops=4 * rows * DH * key_weight.shape[0], bytes_accessed=6 * 2**20, transcendentals=0
        ),
    )(grad, key_weight, value_weight)


def weight_terms_kernel(at, *refs):
    grads, cuts, outs = refs[:4], refs[4:8], refs[8:-7]
    g_held, x_held, turned, first, rest, sems, out_sems = refs[-7:]
    n_z = len(outs)
    rows = g_held.shape[1]
    g_in = fetch([(g, g_held.at[i]) for i, g in enumerate(grads)], sems.at[n_z])
    steps = []
    for k in reversed(range(n_z)):
        to = lax.rem(at[0] + k, n_z)
        steps.append((k, fetch([(x.at[to], x_held.at[k, i]) for i, x in enumerate(cuts)], sems.at[k])))
    for i, copy in enumerate(g_in):
        copy.wait()
        turned[:, i * rows:(i + 1) * rows] = g_held[i].T
    sent = []
    for k, copies in steps:
        for copy in copies:
            copy.wait()
        x = x_held[k].reshape(4 * rows, x_held.shape[3])
        terms = jnp.dot(turned[...], x, preferred_element_type=f32)
        held = rest.at[k - 1] if k else first
        held[...] = terms.astype(held.dtype)
        sent += fetch([(held, outs[k])], out_sems.at[pl.ds(k, 1)])
    for copy in sent:
        copy.wait()


def weight_terms(at, grads, cuts):
    rows, columns = grads[0].shape
    n_z, _, wide = cuts[0].shape
    shape = (columns, wide)
    return pl.pallas_call(
        weight_terms_kernel,
        out_shape=[jax.ShapeDtypeStruct(shape, bf16 if k else f32) for k in range(n_z)],
        in_specs=[SMEM] + [ANY] * 8,
        out_specs=[ANY] * n_z,
        scratch_shapes=[
            pltpu.VMEM((4, rows, columns), bf16),
            pltpu.VMEM((n_z, 4, rows, wide), bf16),
            pltpu.VMEM((columns, 4 * rows), bf16),
            pltpu.VMEM(shape, f32),
            pltpu.VMEM((n_z - 1,) + shape, bf16),
            pltpu.SemaphoreType.DMA((n_z + 1, 4)),
            pltpu.SemaphoreType.DMA((n_z,)),
        ],
        compiler_params=pltpu.CompilerParams(vmem_limit_bytes=BIG),
        cost_estimate=pl.CostEstimate(
            flops=8 * rows * n_z * shape[0] * shape[1], bytes_accessed=4 * 2**20, transcendentals=0
        ),
    )(at, *grads, *cuts)


def weight_sum_kernel(*refs):
    *parts, key_out, value_out = refs
    total = parts[0][...]
    for part in parts[1:]:
        total += part[...].astype(f32)
    key_out[...] = total[:DH, :].T
    value_out[...] = total[DH:, :].T


def weight_sum(parts):
    shape = jax.ShapeDtypeStruct((parts[0].shape[1], DH), f32)
    return pl.pallas_call(
        weight_sum_kernel,
        out_shape=(shape, shape),
        in_specs=[VMEM] * len(parts),
        out_specs=(VMEM, VMEM),
        compiler_params=pltpu.CompilerParams(vmem_limit_bytes=SMALL),
    )(*parts)


def swap(x, axis):
    return lax.ppermute(x, axis, [(0, 1), (1, 0)])


def cross(x):
    return lax.ppermute(x, ("xh", "core"), [(0, 3), (1, 2), (2, 1), (3, 0)])


def on_device(
    queries_one, grads_one, queries_two, grads_two, key_rows, value_rows,
    shared_input, key_weight, value_weight, block_order,
):
    rows, width = shared_input.shape
    n_xh, n_z, n_core, n_xl, n_y = (lax.axis_size(a) for a in CTX + HEAD)
    heads = n_xl * n_y
    core, xh, z = lax.axis_index("core"), lax.axis_index("xh"), lax.axis_index("z")
    head = lax.axis_index(HEAD)

    def slot(h, at, c):
        return 2 * ((h * n_z + at) * n_core + c)

    where = jnp.stack(
        [slot(xh, z, core), slot(1 - xh, z, core), slot(xh, z, 1 - core), slot(1 - xh, z, 1 - core)]
        + [slot(xh, b, core) for b in range(n_z)]
    ).astype(jnp.int32)

    at = jnp.stack([xh, core]).astype(jnp.int32)

    with jax.named_scope("gather"):
        own, packed = pack(
            (queries_one, grads_one, queries_two, grads_two), key_rows, value_rows, n_z
        )
        shared_input, own = lax.optimization_barrier((shared_input, own))
        packed = lax.all_to_all(packed, "z", 0, 0)
        far = swap(own, "xh")
        side = swap(own, "core")
        where, packed = lax.optimization_barrier((where, packed))
    with jax.named_scope("spread_input"):
        cuts = cut_input(at, shared_input, n_z)
        far, *cuts = lax.optimization_barrier((far, *cuts))
        both = swap(far, "core")
        cuts = [cuts[0], swap(cuts[1], "xh"), swap(cuts[2], "core"), cross(cuts[3])]

    with jax.named_scope("attention_stats"):
        stats, *sorted_rows = attention_stats(block_order, where, own, far, side, both, packed)
    with jax.named_scope("share_stats"):
        stats, *cuts = lax.optimization_barrier((stats, *cuts))
        stats = (stats, swap(stats, "xh"), swap(stats, "core"), cross(stats))
    with jax.named_scope("attention_grads"):
        dq_own, dq_far, dq_pair, dkv = attention_grads(
            block_order, where, *sorted_rows, stats, n_z
        )
    with jax.named_scope("scatter_grads"):
        dkv = lax.all_to_all(dkv, "z", 0, 0)
    with jax.named_scope("query_grads"):
        dq_pair = swap(dq_pair, "core").astype(f32)
        dq_own = dq_own + dq_pair[0]
        dq_far = swap((dq_far + dq_pair[1]).astype(bf16), "xh")
        dkv, dq_own, dq_far = lax.optimization_barrier((dkv, dq_own, dq_far))
        dq = (dq_own + dq_far.astype(f32)).astype(bf16)
        dq_one, dq_two = dq[:, :GROUP * DH], dq[:, GROUP * DH:]
    with jax.named_scope("scatter_grads"):
        grad = part_sum(dkv)

        grads = [grad, swap(grad, "xh"), swap(grad, "core"), cross(grad)]

        grads = [grad, swap(grad, "xh"), swap(grad, "core"), cross(grad)]

    with jax.named_scope("input_grad"):
        terms = input_terms(grad, key_weight, value_weight, heads)
        terms, *grads = lax.optimization_barrier((terms, *grads))
        terms = lax.all_to_all(terms, HEAD, 0, 0)
        input_grad = part_sum(terms)

    with jax.named_scope("weight_grad"):
        own, *rest = weight_terms(z.astype(jnp.int32).reshape(1), grads, cuts)
        own, input_grad = lax.optimization_barrier((own, input_grad))
        parts = [own] + [
            lax.ppermute(part, "z", [(i, (i + k) % n_z) for i in range(n_z)])
            for k, part in enumerate(rest, 1)
        ]
        key_weight_grad, value_weight_grad = weight_sum(parts)
    return (dq_one, dq_two, input_grad, key_weight_grad, value_weight_grad)


def solution(mesh):
    fine = Mesh(mesh.devices.reshape(2, 8, 2, 2, 4), CTX + HEAD)
    both = P(CTX, HEAD)
    return jax.shard_map(
        on_device,
        mesh=fine,
        in_specs=(both,) * 6 + (P(CTX, None), P(None, HEAD), P(None, HEAD), P()),
        out_specs=(both,) * 5,
        check_vma=False,
    )
```

```python
import functools
import math

import jax
import jax.numpy as jnp
from jax import lax
from jax.experimental import pallas as pl
from jax.experimental.pallas import tpu as pltpu
from jax.sharding import Mesh
from jax.sharding import PartitionSpec as P

H = 32
KV = 8
DH = 128
GROUP = H // KV
CTX = ("xh", "z", "core")
HEAD = ("xl", "y")
NT = (((1,), (1,)), ((), ()))
TN = (((0,), (0,)), ((), ()))
f32 = jnp.float32
bf16 = jnp.bfloat16
SCALE = 1.0 / math.sqrt(DH)
TO_LOG2 = SCALE * math.log2(math.e)
LOWEST = -1e30
BIG = 56 * 2**20
SMALL = 8 * 2**20
VMEM = pl.BlockSpec(memory_space=pltpu.VMEM)
SMEM = pl.BlockSpec(memory_space=pltpu.SMEM)
ANY = pl.BlockSpec(memory_space=pl.ANY)


class Plan:
    def __init__(self, order, where, n_keys, half):
        self.half = half
        self.n_keys = n_keys
        self.order, self.where = order, where
        self.near = []
        for b in range(n_keys):
            slot = where[4 + b]
            self.near.append(jnp.minimum(order[slot], order[slot + 1]))
        self.rank = []
        for b in range(n_keys):
            r = jnp.int32(0)
            for o in range(n_keys):
                r += jnp.where(self.near[o] < self.near[b], 1, 0)
            self.rank.append(r)

    def key_rows(self, b, i):
        pos = self.order[self.where[4 + b] + i]
        r = self.rank[b]
        at = jnp.where(pos == self.near[b], r, 2 * self.n_keys - 1 - r)
        return pl.ds(pl.multiple_of(at * self.half, self.half), self.half)

    def limits(self, a, width):
        slot = self.where[a]
        first, second = self.order[slot], self.order[slot + 1]
        mine = jnp.minimum(first, second)
        below, upto = jnp.int32(0), jnp.int32(0)
        for near in self.near:
            below += jnp.where(near < mine, 1, 0)
            upto += jnp.where(near <= mine, 1, 0)
        early, late = upto, 2 * self.n_keys - below
        inside = lax.rem(lax.broadcasted_iota(jnp.int32, (1, width), 1), self.half)
        same = upto > below

        def last(blocks):
            return jnp.where(same, (blocks - 1) * self.half + inside, blocks * self.half - 1)

        return early, late, last(early), last(late)


def load_heads(a, ref, q_all, g_all, order, where, half):
    slot = where[a]
    late_at = jnp.where(order[slot] > order[slot + 1], 0, 1)
    for part, at in ((0, late_at), (1, 1 - late_at)):
        rows = pl.ds(pl.multiple_of(at * half, half), half)
        for layer in range(2):
            for h in range(GROUP):
                r = (layer * GROUP + h) * half
                c = (layer * 2 * GROUP + h) * DH
                q_all[part, r:r + half, :] = ref[rows, c:c + DH]
                c += GROUP * DH
                g_all[part, r:r + half, :] = ref[rows, c:c + DH]


def fetch(pairs, sems):
    copies = [pltpu.make_async_copy(src, dst, sems.at[i]) for i, (src, dst) in enumerate(pairs)]
    for copy in copies:
        copy.start()
    return copies


def sort_keys(plan, kv, k_sorted, v_sorted):
    for b in range(plan.n_keys):
        for i in range(2):
            to = plan.key_rows(b, i)
            rows = slice(i * plan.half, (i + 1) * plan.half)
            k_sorted[to, :] = kv[b, rows, :DH]
            v_sorted[to, :] = kv[b, rows, DH:2 * DH]


def fold(x, op):
    return op(x.reshape(x.shape[0] // 8, 8, x.shape[1]), axis=0)


def tiles(seen, n_keys, half, part):
    step = n_keys * half // 2
    if part == 0:
        return (
            (0, 2 * step, None, False),
            (2 * step, step, seen > n_keys, True),
            (3 * step, step, seen > n_keys + n_keys // 2, True),
        )
    return ((0, step, seen > 0, True), (step, step, seen > n_keys // 2, True))


def under(condition, body):
    if condition is None:
        body()
    else:
        pl.when(condition)(body)


def masked_scores(k, q, start, last, masked):
    s = lax.dot_general(k, q, NT, preferred_element_type=f32)
    if masked:
        key = start + lax.broadcasted_iota(jnp.int32, s.shape, 0)
        s = jnp.where(key <= last, s, -jnp.inf)
    return s


def stats_kernel(
    order, where, own, far, side, both, kv, stats, k_out, v_out, q_out, g_out, held, k_sorted, v_sorted, q_all, g_all,
    sems, out_sems, scores, peak, total, delta,
):
    half = own.shape[0] // 2
    n_keys = kv.shape[0]
    width = q_all.shape[2]
    copies = fetch([(ref, held.at[a]) for a, ref in enumerate((own, far, side, both))], sems)
    plan = Plan(order, where, n_keys, half)
    sort_keys(plan, kv, k_sorted, v_sorted)
    sent = fetch([(k_sorted, k_out), (v_sorted, v_out)], out_sems.at[0])
    for a in range(4):
        copies[a].wait()
        load_heads(a, held.at[a], q_all.at[a], g_all.at[a], order, where, half)
        sent += fetch([(q_all.at[a], q_out.at[a]), (g_all.at[a], g_out.at[a])], out_sems.at[1 + a])
        early, late, last_early, last_late = plan.limits(a, width)
        for part, seen, last in ((0, late, last_late), (1, early, last_early)):
            q, g = q_all[a, part], g_all[a, part]
            peak[...] = jnp.full(peak.shape, LOWEST, f32)
            for start, size, condition, masked in tiles(seen, n_keys, half, part):

                def score():
                    s = masked_scores(k_sorted[start:start + size, :], q, start, last, masked)
                    scores[start:start + size, :] = s
                    peak[...] = jnp.maximum(peak[...], fold(s, jnp.max))

                under(condition, score)
            top = jnp.max(peak[...], axis=0, keepdims=True) * TO_LOG2
            total[...] = jnp.zeros(total.shape, f32)
            delta[...] = jnp.zeros(delta.shape, f32)
            for start, size, condition, masked in tiles(seen, n_keys, half, part):

                def weigh():
                    e = jnp.exp2(scores[start:start + size, :] * TO_LOG2 - top)
                    d = lax.dot_general(
                        v_sorted[start:start + size, :], g, NT, preferred_element_type=f32
                    )
                    total[...] += fold(e, jnp.sum)
                    delta[...] += fold(e * d, jnp.sum)

                under(condition, weigh)
            row = 2 * a + part
            stats[0, row:row + 1, :] = top
            stats[1, row:row + 1, :] = jnp.sum(total[...], axis=0, keepdims=True)
            stats[2, row:row + 1, :] = jnp.sum(delta[...], axis=0, keepdims=True)
    for copy in sent:
        copy.wait()


def grads_kernel(
    order, where, keys, values, queries, grads, s_own, s_far, s_side, s_both, dq_own, dq_far, dq_pair, dkv,
    k_sorted, v_sorted, q_all, g_all, sems, s_held, out_mine, out_pair, out_kv, out_sems, dk, dv, dq,
):
    n_keys, half = dkv.shape[0], dkv.shape[1] // 2
    width = q_all.shape[2]
    copies = fetch([(keys, k_sorted), (values, v_sorted)], sems.at[0])
    parts = [
        fetch([(queries.at[a], q_all.at[a]), (grads.at[a], g_all.at[a])], sems.at[1 + a]) for a in range(4)
    ]
    copies += fetch([(ref, s_held.at[a]) for a, ref in enumerate((s_own, s_far, s_side, s_both))], sems.at[5])
    plan = Plan(order, where, n_keys, half)
    dk[...] = jnp.zeros(dk.shape, f32)
    dv[...] = jnp.zeros(dv.shape, f32)
    for copy in copies:
        copy.wait()
    sent = []
    for a, out in enumerate((dq_own, dq_far, dq_pair.at[0], dq_pair.at[1])):
        dq_out = out_pair.at[a - 2] if a > 1 else out_mine.at[a]
        for copy in parts[a]:
            copy.wait()
        early, late, last_early, last_late = plan.limits(a, width)
        slot = where[a]
        late_at = jnp.where(order[slot] > order[slot + 1], 0, 1)
        for part, seen, last, at in ((0, late, last_late, late_at), (1, early, last_early, 1 - late_at)):
            q, g = q_all[a, part], g_all[a, part]
            shares = []
            for flip in range(4):
                r = 2 * (a ^ flip) + part
                shares.append(tuple(s_held[flip, j, r:r + 1, :] for j in range(3)))
            top = functools.reduce(jnp.maximum, (t for t, _, _ in shares))
            total = sum(n * jnp.exp2(t - top) for t, n, _ in shares)
            delta = sum(d * jnp.exp2(t - top) for t, _, d in shares) / total
            base = top + jnp.log2(total)
            dq[...] = jnp.zeros(dq.shape, f32)
            for start, size, condition, masked in tiles(seen, n_keys, half, part):

                def step():
                    span = slice(start, start + size)
                    k = k_sorted[span, :]
                    s = masked_scores(k, q, start, last, masked)
                    p = jnp.exp2(s * TO_LOG2 - base)
                    d = lax.dot_general(v_sorted[span, :], g, NT, preferred_element_type=f32)
                    ds = (p * (d - delta)).astype(bf16)
                    dv[span, :] += jnp.dot(p.astype(bf16), g, preferred_element_type=f32)
                    dk[span, :] += jnp.dot(ds, q, preferred_element_type=f32)
                    dq[...] += lax.dot_general(k, ds, TN, preferred_element_type=f32)

                under(condition, step)
            turned = (dq[...] * SCALE).T.astype(dq_out.dtype)
            rows = pl.ds(pl.multiple_of(at * half, half), half)
            for j in range(2 * GROUP):
                dq_out[rows, j * DH:(j + 1) * DH] = turned[j * half:(j + 1) * half, :]
        copy = pltpu.make_async_copy(dq_out, out, out_sems.at[a])
        copy.start()
        sent.append(copy)
    for b in range(n_keys):
        for i in range(2):
            of = plan.key_rows(b, i)
            rows = slice(i * half, (i + 1) * half)
            out_kv[b, rows, :DH] = (dk[of, :] * SCALE).astype(bf16)
            out_kv[b, rows, DH:] = dv[of, :].astype(bf16)
    copy = pltpu.make_async_copy(out_kv, dkv, out_sems.at[4])
    copy.start()
    for copy in sent + [copy]:
        copy.wait()


def scratch(n_keys, rows):
    width = GROUP * rows
    return [
        pltpu.VMEM((n_keys * rows, DH), bf16),
        pltpu.VMEM((n_keys * rows, DH), bf16),
        pltpu.VMEM((4, 2, width, DH), bf16),
        pltpu.VMEM((4, 2, width, DH), bf16),
    ]


def cost(n_keys, rows, products):
    pairs = 4 * GROUP * rows * n_keys * rows
    return pl.CostEstimate(
        flops=2 * products * pairs * DH, bytes_accessed=8 * 2**20, transcendentals=pairs
    )


def attention_stats(order, where, own, far, side, both, kv):
    n_keys, rows, _ = kv.shape
    width = GROUP * rows
    keys = jax.ShapeDtypeStruct((n_keys * rows, DH), bf16)
    heads = jax.ShapeDtypeStruct((4, 2, width, DH), bf16)
    return pl.pallas_call(
        stats_kernel,
        out_shape=(jax.ShapeDtypeStruct((3, 8, width), f32), keys, keys, heads, heads),
        in_specs=[SMEM] * 2 + [ANY] * 4 + [VMEM],
        out_specs=(VMEM,) + (ANY,) * 4,
        scratch_shapes=[pltpu.VMEM((4,) + own.shape, bf16)]
        + scratch(n_keys, rows)
        + [pltpu.SemaphoreType.DMA((4,)), pltpu.SemaphoreType.DMA((5, 2))]
        + [pltpu.VMEM((n_keys * rows, width), f32)]
        + [pltpu.VMEM((8, width), f32)] * 3,
        compiler_params=pltpu.CompilerParams(vmem_limit_bytes=BIG),
        cost_estimate=cost(n_keys, rows, 2),
    )(order, where, own, far, side, both, kv)


def attention_grads(order, where, keys, values, queries, grads, stats, n_keys):
    rows = keys.shape[0] // n_keys
    width = GROUP * rows
    shape = (rows, 2 * GROUP * DH)
    return pl.pallas_call(
        grads_kernel,
        out_shape=(
            jax.ShapeDtypeStruct(shape, f32),
            jax.ShapeDtypeStruct(shape, f32),
            jax.ShapeDtypeStruct((2,) + shape, bf16),
            jax.ShapeDtypeStruct((n_keys, rows, 2 * DH), bf16),
        ),
        in_specs=[SMEM] * 2 + [ANY] * 8,
        out_specs=(ANY,) * 4,
        scratch_shapes=scratch(n_keys, rows)
        + [
            pltpu.SemaphoreType.DMA((6, 4)),
            pltpu.VMEM((4, 3, 8, width), f32),
            pltpu.VMEM((2,) + shape, f32),
            pltpu.VMEM((2,) + shape, bf16),
            pltpu.VMEM((n_keys, rows, 2 * DH), bf16),
            pltpu.SemaphoreType.DMA((5,)),
        ]
        + [pltpu.VMEM((n_keys * rows, DH), f32)] * 2
        + [pltpu.VMEM((DH, width), f32)],
        compiler_params=pltpu.CompilerParams(vmem_limit_bytes=BIG),
        cost_estimate=cost(n_keys, rows, 5),
    )(order, where, keys, values, queries, grads, *stats)


def pack_kernel(*refs):
    *heads, key_rows, value_rows, own, packed, sems = refs
    pairs = []
    for j in range(packed.shape[0]):
        for i, ref in enumerate((key_rows, value_rows)):
            pairs.append((ref, packed.at[j, :, i * DH:(i + 1) * DH]))
    wide = heads[0].shape[1]
    for i, ref in enumerate(heads):
        pairs.append((ref, own.at[:, i * wide:(i + 1) * wide]))
    for copy in fetch(pairs, sems):
        copy.wait()


def pack(heads, key_rows, value_rows, count):
    rows = key_rows.shape[0]
    return pl.pallas_call(
        pack_kernel,
        in_specs=[ANY] * (len(heads) + 2),
        out_specs=(VMEM,) * 2,
        out_shape=(
            jax.ShapeDtypeStruct((rows, len(heads) * heads[0].shape[1]), bf16),
            jax.ShapeDtypeStruct((count, rows, 2 * DH), bf16),
        ),
        scratch_shapes=[pltpu.SemaphoreType.DMA((2 * count + len(heads),))],
        compiler_params=pltpu.CompilerParams(vmem_limit_bytes=BIG),
    )(*heads, key_rows, value_rows)


def cut_kernel(at, x, *refs):
    *cuts, sems = refs
    count, _, wide = cuts[0].shape
    xh, core = at[0], at[1]
    pairs = []
    for i, cut in enumerate(cuts):
        lead = (xh ^ (i & 1)) * (2 * count) + (core ^ (i >> 1))
        for j in range(count):
            columns = pl.ds(pl.multiple_of((lead + 2 * j) * wide, wide), wide)
            pairs.append((x.at[:, columns], cut.at[j]))
    for copy in fetch(pairs, sems):
        copy.wait()


def cut_input(at, x, count):
    cut = jax.ShapeDtypeStruct((count, x.shape[0], x.shape[1] // (4 * count)), bf16)
    return pl.pallas_call(
        cut_kernel,
        in_specs=[SMEM, ANY],
        out_specs=(VMEM,) * 4,
        out_shape=(cut,) * 4,
        scratch_shapes=[pltpu.SemaphoreType.DMA((4 * count,))],
        compiler_params=pltpu.CompilerParams(vmem_limit_bytes=BIG),
    )(at, x)


def part_sum_kernel(parts, grad):
    total = parts[0].astype(f32)
    for i in range(1, parts.shape[0]):
        total += parts[i].astype(f32)
    grad[...] = total.astype(bf16)


def part_sum(parts):
    return pl.pallas_call(
        part_sum_kernel,
        out_shape=jax.ShapeDtypeStruct(parts.shape[1:], bf16),
        in_specs=[VMEM],
        out_specs=VMEM,
        compiler_params=pltpu.CompilerParams(vmem_limit_bytes=SMALL),
    )(parts)


def input_terms_kernel(grad, key_weight, value_weight, out, k_held, v_held, terms, sems, out_sems):
    columns = out.shape[2]
    n = out.shape[0]
    spans = [pl.ds(j * columns, columns) for j in range(n)]
    k_in = fetch([(key_weight.at[p], k_held.at[p]) for p in spans], sems.at[0])
    v_in = fetch([(value_weight.at[p], v_held.at[p]) for p in spans], sems.at[1])
    outs = []
    for j in range(n):
        k_in[j].wait()
        v_in[j].wait()
        t = lax.dot_general(grad[:, :DH], k_held[spans[j], :], NT, preferred_element_type=f32)
        t += lax.dot_general(grad[:, DH:], v_held[spans[j], :], NT, preferred_element_type=f32)
        terms[j] = t.astype(bf16)
        copy = pltpu.make_async_copy(terms.at[j], out.at[j], out_sems.at[j])
        copy.start()
        outs.append(copy)
    for copy in outs:
        copy.wait()


def input_terms(grad, key_weight, value_weight, heads):
    rows = grad.shape[0]
    shape = (heads, rows, key_weight.shape[0] // heads)
    return pl.pallas_call(
        input_terms_kernel,
        out_shape=jax.ShapeDtypeStruct(shape, bf16),
        in_specs=[VMEM, ANY, ANY],
        out_specs=ANY,
        scratch_shapes=[
            pltpu.VMEM(key_weight.shape, bf16),
            pltpu.VMEM(key_weight.shape, bf16),
            pltpu.VMEM(shape, bf16),
            pltpu.SemaphoreType.DMA((2, heads)),
            pltpu.SemaphoreType.DMA((heads,)),
        ],
        compiler_params=pltpu.CompilerParams(vmem_limit_bytes=BIG),
        cost_estimate=pl.CostEstimate(
            flops=4 * rows * DH * key_weight.shape[0], bytes_accessed=6 * 2**20, transcendentals=0
        ),
    )(grad, key_weight, value_weight)


def weight_terms_kernel(at, g0, g1, g2, g3, x0, x1, x2, x3, *refs):
    *outs, held, turned, sems = refs
    z = at[0]
    copies = fetch([(x, held.at[i]) for i, x in enumerate((x0, x1, x2, x3))], sems)
    rows = g0.shape[0]
    for i, g in enumerate((g0, g1, g2, g3)):
        turned[:, i * rows:(i + 1) * rows] = g[...].T
    for copy in copies:
        copy.wait()
    n_z = len(outs)
    for k in reversed(range(n_z)):
        to = lax.rem(z + k, n_z)
        terms = jnp.dot(turned[:, :rows], held[0, to], preferred_element_type=f32)
        for i in range(1, 4):
            terms += jnp.dot(
                turned[:, i * rows:(i + 1) * rows], held[i, to], preferred_element_type=f32
            )
        outs[k][...] = terms.astype(outs[k].dtype)


def weight_terms(at, grads, cuts):
    rows, columns = grads[0].shape
    n_z = cuts[0].shape[0]
    shape = (columns, cuts[0].shape[2])
    return pl.pallas_call(
        weight_terms_kernel,
        out_shape=[jax.ShapeDtypeStruct(shape, bf16 if k else f32) for k in range(n_z)],
        in_specs=[SMEM] + [VMEM] * 4 + [ANY] * 4,
        out_specs=[VMEM] * n_z,
        scratch_shapes=[
            pltpu.VMEM((4,) + cuts[0].shape, bf16),
            pltpu.VMEM((columns, 4 * rows), bf16),
            pltpu.SemaphoreType.DMA((4,)),
        ],
        compiler_params=pltpu.CompilerParams(vmem_limit_bytes=14 * 2**20),
        cost_estimate=pl.CostEstimate(
            flops=8 * rows * n_z * shape[0] * shape[1], bytes_accessed=4 * 2**20, transcendentals=0
        ),
    )(at, *grads, *cuts)


def weight_sum_kernel(*refs):
    *parts, key_out, value_out = refs
    total = parts[0][...]
    for part in parts[1:]:
        total += part[...].astype(f32)
    key_out[...] = total[:DH, :].T
    value_out[...] = total[DH:, :].T


def weight_sum(parts):
    shape = jax.ShapeDtypeStruct((parts[0].shape[1], DH), f32)
    return pl.pallas_call(
        weight_sum_kernel,
        out_shape=(shape, shape),
        in_specs=[VMEM] * len(parts),
        out_specs=(VMEM, VMEM),
        compiler_params=pltpu.CompilerParams(vmem_limit_bytes=SMALL),
    )(*parts)


def swap(x, axis):
    return lax.ppermute(x, axis, [(0, 1), (1, 0)])


def cross(x):
    return lax.ppermute(x, ("xh", "core"), [(0, 3), (1, 2), (2, 1), (3, 0)])


def on_device(
    queries_one, grads_one, queries_two, grads_two, key_rows, value_rows,
    shared_input, key_weight, value_weight, block_order,
):
    rows, width = shared_input.shape
    n_xh, n_z, n_core, n_xl, n_y = (lax.axis_size(a) for a in CTX + HEAD)
    heads = n_xl * n_y
    core, xh, z = lax.axis_index("core"), lax.axis_index("xh"), lax.axis_index("z")
    head = lax.axis_index(HEAD)

    def slot(h, at, c):
        return 2 * ((h * n_z + at) * n_core + c)

    where = jnp.stack(
        [slot(xh, z, core), slot(1 - xh, z, core), slot(xh, z, 1 - core), slot(1 - xh, z, 1 - core)]
        + [slot(xh, b, core) for b in range(n_z)]
    ).astype(jnp.int32)

    at = jnp.stack([xh, core]).astype(jnp.int32)

    with jax.named_scope("gather"):
        own, packed = pack(
            (queries_one, grads_one, queries_two, grads_two), key_rows, value_rows, n_z
        )
        shared_input, own = lax.optimization_barrier((shared_input, own))
        packed = lax.all_to_all(packed, "z", 0, 0)
        far = swap(own, "xh")
        side = swap(own, "core")
        where, packed = lax.optimization_barrier((where, packed))
    with jax.named_scope("spread_input"):
        cuts = cut_input(at, shared_input, n_z)
        far, *cuts = lax.optimization_barrier((far, *cuts))
        both = swap(far, "core")
        cuts = [cuts[0], swap(cuts[1], "xh"), swap(cuts[2], "core"), cross(cuts[3])]

    with jax.named_scope("attention_stats"):
        stats, *sorted_rows = attention_stats(block_order, where, own, far, side, both, packed)
    with jax.named_scope("share_stats"):
        others = [swap(stats, "xh"), swap(stats, "core"), cross(stats)]
        stats, *cuts = lax.optimization_barrier((stats, *cuts))
        stats = [stats] + others
    with jax.named_scope("attention_grads"):
        dq_own, dq_far, dq_pair, dkv = attention_grads(
            block_order, where, *sorted_rows, stats, n_z
        )
    with jax.named_scope("scatter_grads"):
        dkv = lax.all_to_all(dkv, "z", 0, 0)
    with jax.named_scope("query_grads"):
        dq_pair = swap(dq_pair, "core").astype(f32)
        dq_own = dq_own + dq_pair[0]
        dq_far = swap((dq_far + dq_pair[1]).astype(bf16), "xh")
        dkv, dq_own, dq_far = lax.optimization_barrier((dkv, dq_own, dq_far))
        dq = (dq_own + dq_far.astype(f32)).astype(bf16)
        dq_one, dq_two = dq[:, :GROUP * DH], dq[:, GROUP * DH:]
    with jax.named_scope("scatter_grads"):
        grad = part_sum(dkv)

        grads = [grad, swap(grad, "xh"), swap(grad, "core"), cross(grad)]

        grads = [grad, swap(grad, "xh"), swap(grad, "core"), cross(grad)]

    with jax.named_scope("input_grad"):
        terms = input_terms(grad, key_weight, value_weight, heads)
        terms, *grads = lax.optimization_barrier((terms, *grads))
        terms = lax.all_to_all(terms, HEAD, 0, 0)
        input_grad = part_sum(terms)

    with jax.named_scope("weight_grad"):
        own, *rest = weight_terms(z.astype(jnp.int32).reshape(1), grads, cuts)
        own, input_grad = lax.optimization_barrier((own, input_grad))
        parts = [own] + [
            lax.ppermute(part, "z", [(i, (i + k) % n_z) for i in range(n_z)])
            for k, part in enumerate(rest, 1)
        ]
        key_weight_grad, value_weight_grad = weight_sum(parts)
    return (dq_one, dq_two, input_grad, key_weight_grad, value_weight_grad)


def solution(mesh):
    fine = Mesh(mesh.devices.reshape(2, 8, 2, 2, 4), CTX + HEAD)
    both = P(CTX, HEAD)
    return jax.shard_map(
        on_device,
        mesh=fine,
        in_specs=(both,) * 6 + (P(CTX, None), P(None, HEAD), P(None, HEAD), P()),
        out_specs=(both,) * 5,
        check_vma=False,
    )
```
